32 devices in a mesh: section: 2 (over core), rows: 16 (over z, y, x).
Axes of the slice: x: 2, y: 2, z: 4, core: 2. Of those that a mesh axis runs over, the one named last changes fastest.
Arguments:
- boundary: bfloat16 [2, 2, 6144, 324], P('section', None, 'rows'), may hold values from -6 to 6
- utt_lengths: int32 [2, 16, 5], P(None, 'rows'), may hold values from 0 to 376, as said below
- attn_in: bfloat16 [324, 972], replicated, may hold values from -0.3125 to 0.3125
- pos_proj: bfloat16 [324, 324], replicated, may hold values from -0.3125 to 0.3125
- attn_out: bfloat16 [324, 324], replicated, may hold values from -2.5 to 2.5
- first_vectors: float32 [6, 324], replicated, may hold values from -1.8 to 1.8
- reduce_taps: float32 [3, 324], replicated, may hold values from -3.5 to 3.5
- reduce_proj: bfloat16 [324, 324], replicated, may hold values from -0.3125 to 0.3125
- glu_in: bfloat16 [324, 648], replicated, may hold values from -0.3125 to 0.3125
- conv_taps: float32 [31, 324], replicated, may hold values from -1 to 1
- second_vectors: float32 [4, 324], replicated, may hold values from -1.8 to 1.8
- bn_gain: float32 [324], replicated, may hold values from 0.5 to 1.5
- point_proj: bfloat16 [324, 324], replicated, may hold values from -0.3125 to 0.3125
- ffn_in: bfloat16 [2, 324, 1296], P('section'), may hold values from -0.3125 to 0.3125
- ffn_bias: float32 [2, 1296], P('section'), may hold values from -1.8 to 1.8
- ffn_out: bfloat16 [2, 1296, 324], P('section'), may hold values from -0.15625 to 0.15625
- norm_gain: float32 [2, 2, 324], P('section'), may hold values from 0.5 to 1.5
- block_vectors: float32 [2, 3, 324], P('section'), may hold values from -1.8 to 1.8
Outputs:
- boundary_out: float32 [2, 2, 6144, 324], P('section', None, 'rows')
- grad_attn_in: float32 [324, 972], replicated
- grad_pos_proj: float32 [324, 324], replicated
- grad_attn_out: float32 [324, 324], replicated
- grad_first_vectors: float32 [6, 324], replicated
- grad_reduce_taps: float32 [3, 324], replicated
- grad_reduce_proj: float32 [324, 324], replicated
- grad_glu_in: float32 [324, 648], replicated
- grad_conv_taps: float32 [31, 324], replicated
- grad_second_vectors: float32 [4, 324], replicated
- grad_bn_gain: float32 [324], replicated
- grad_point_proj: float32 [324, 324], replicated
- grad_ffn_in: float32 [2, 324, 1296], P('section')
- grad_ffn_bias: float32 [2, 1296], P('section')
- grad_ffn_out: float32 [2, 1296, 324], P('section')
- grad_norm_gain: float32 [2, 2, 324], P('section')
- grad_block_vectors: float32 [2, 3, 324], P('section')
The draws below stay inside these ranges and needn't reach their ends.
Inputs may be any that keep to these rules, and one draw needn't show every extreme that they name: `utt_lengths`: nonzero lengths come first in a buffer, are even, lie between 74 and 376, and add up to at most 384; every buffer holds at least one utterance; in every micro-batch some buffer's first utterance has exactly 376 frames; frames after the last utterance are padding.
All inputs are finite; a program needn't handle non-finite values.
Results may differ from the reference program's by a relative error of at most 0.03.
Values may be sent and summed in bfloat16 or wider, within the bound.
No kernel may reach another device: no remote copies, remote signals or barrier semaphores. Data moves between devices by JAX's collectives and lax.ppermute only.
A program may use at most 192 MiB of HBM per device.

```python
import math
import jax
import jax.numpy as jnp
from jax import lax

D = 324
HEADS = 4
FF = 1296
KCONV = 31
FR = 384
LMAX = 376
MB = 2
MINLEN = 74
SHORTMAX = 250
SLOTS = 5
FRAMES = 6144


def draw_utt_lengths(key, part):
    key = jax.random.fold_in(key, 11)
    row_count = FRAMES // FR
    key_short, key_rare, key_chosen = jax.random.split(key, 3)
    short_clips = 2 * jax.random.randint(key_short, (MB, row_count, SLOTS), MINLEN // 2, SHORTMAX // 2 + 1)
    rare_long = jax.random.randint(key_rare, (MB, row_count, SLOTS), 0, 16) == 0
    chosen_row = jax.random.randint(key_chosen, (MB, 1), 0, row_count)
    row_hit = (jnp.arange(row_count, dtype=jnp.int32)[None, :] == chosen_row)[:, :, None]
    slot_hit = (jnp.arange(SLOTS, dtype=jnp.int32) == 0)[None, None, :]
    drawn = jnp.where(rare_long | row_hit & slot_hit, LMAX, short_clips)
    running = jnp.cumsum(drawn, axis=2)
    return jnp.where(running <= FR, drawn, 0).astype(jnp.int32)


def levels(key, dims, shards, low, largest):
    level = 1.0
    for axis_at, shards_of in shards:
        heights = jax.random.uniform(jax.random.fold_in(jax.random.fold_in(key, 6), axis_at), (shards_of,), jnp.float32, low / len(shards), largest / len(shards))
        level = level * jnp.repeat(jnp.exp(heights), dims[axis_at] // shards_of).reshape((-1,) + (1,) * (len(dims) - 1 - axis_at))
    return level


def centred(rng, shape, scale, bound, pieces=(), kind=jnp.bfloat16):
    factor_of = levels(rng, shape, pieces, -0.22, 0.18) if pieces else 1.0
    values = jax.random.normal(rng, shape, jnp.float32) * scale * factor_of
    return jnp.minimum(jnp.maximum(values, -bound), bound).astype(kind)


def setup_inputs(seed: int = 0) -> dict:
    splits = jax.random.split(jax.random.key(seed), 19)
    boundary = centred(splits[0], (2, MB, FRAMES, D), 1.0, 6.0, ((0, 2), (2, 16)))
    utt_lengths = draw_utt_lengths(jax.random.fold_in(splits[18], 71), 0)
    attn_in = centred(splits[2], (D, 3 * D), D ** -0.5, 0.3125)
    pos_proj = centred(splits[3], (D, D), D ** -0.5, 0.3125)
    attn_out = centred(splits[4], (D, D), (max(4, D // 64)) ** -0.5, 2.5)
    first_vectors = centred(splits[5], (6, D), 0.3, 1.8, (), jnp.float32)
    reduce_taps = centred(splits[6], (3, D), 3 ** -0.5, 3.5, (), jnp.float32)
    reduce_proj = centred(splits[7], (D, D), D ** -0.5, 0.3125)
    glu_in = centred(splits[8], (D, 2 * D), D ** -0.5, 0.3125)
    conv_taps = centred(splits[9], (KCONV, D), KCONV ** -0.5, 1.0, (), jnp.float32)
    second_vectors = centred(splits[10], (4, D), 0.3, 1.8, (), jnp.float32)
    bn_gain = jnp.clip(1.0 + 0.1 * jax.random.normal(splits[11], (D,), jnp.float32), 0.5, 1.5)
    point_proj = centred(splits[12], (D, D), D ** -0.5, 0.3125)
    ffn_in = centred(splits[13], (2, D, FF), D ** -0.5, 0.3125, ((0, 2),))
    ffn_bias = centred(splits[14], (2, FF), 0.3, 1.8, ((0, 2),), jnp.float32)
    ffn_out = centred(splits[15], (2, FF, D), FF ** -0.5, 0.15625, ((0, 2),))
    norm_gain = jnp.clip(1.0 + 0.1 * jax.random.normal(splits[16], (2, 2, D), jnp.float32), 0.5, 1.5)
    block_vectors = centred(splits[17], (2, 3, D), 0.3, 1.8, ((0, 2),), jnp.float32)
    return dict(boundary=boundary, utt_lengths=utt_lengths, attn_in=attn_in, pos_proj=pos_proj, attn_out=attn_out, first_vectors=first_vectors, reduce_taps=reduce_taps, reduce_proj=reduce_proj, glu_in=glu_in, conv_taps=conv_taps, second_vectors=second_vectors, bn_gain=bn_gain, point_proj=point_proj, ffn_in=ffn_in, ffn_bias=ffn_bias, ffn_out=ffn_out, norm_gain=norm_gain, block_vectors=block_vectors)


@jax.custom_vjp
def low(v):
    return lax.optimization_barrier(v.astype(jnp.bfloat16)).astype(jnp.float32)

@jax.custom_vjp
def low_back(v):
    return v

def low_keep(v):
    return (low(v), None)

def low_pass(kept, grad):
    return (grad,)

def back_keep(v):
    return (v, None)

def back_low(kept, grad):
    return (low(grad),)
low.defvjp(low_keep, low_pass)
low_back.defvjp(back_keep, back_low)
highest = lax.Precision.HIGHEST
epsilon = 1e-05
masked_score = -1e+30

def product(left, right):
    return jnp.dot(left, right, precision=highest)

def layer_norm(values, gain_row, shift_row):
    centre = values - lax.optimization_barrier(jnp.mean(values, axis=-1, keepdims=True))
    spread = lax.optimization_barrier(jnp.mean(centre * centre, axis=-1, keepdims=True))
    return centre * lax.rsqrt(spread + epsilon) * gain_row + shift_row

def swish(values):
    return values * jax.nn.sigmoid(values)

def segment_ids(lengths, frames):
    bounds = jnp.cumsum(lengths)
    position = jnp.arange(frames, dtype=jnp.int32)
    segment = lax.optimization_barrier(jnp.sum((position[:, None] >= bounds[None, :]).astype(jnp.int32), axis=1))
    inside = (position < bounds[-1]).astype(jnp.float32)
    return (segment, inside)

def position_table(frames, features):
    distance = (frames - jnp.arange(2 * frames, dtype=jnp.int32)).astype(jnp.float32)
    frequency = jnp.exp(jnp.arange(0, features, 2, dtype=jnp.int32).astype(jnp.float32) * (-math.log(10000.0) / features))
    angles = distance[:, None] * frequency[None, :]
    return jnp.stack([jnp.sin(angles), jnp.cos(angles)], axis=-1).reshape(2 * frames, features)

def depthwise(values, segment, kernel):
    tap_count = kernel.shape[0]
    reach_back = tap_count // 2
    length = values.shape[0]
    padded = jnp.pad(values, ((reach_back, reach_back), (0, 0)))
    padded_segment = jnp.pad(segment, (reach_back, reach_back), constant_values=-1)
    running = jnp.zeros_like(values)
    for offset in range(tap_count):
        matched = (padded_segment[offset:offset + length] == segment).astype(values.dtype)
        running = running + kernel[offset] * padded[offset:offset + length] * matched[:, None]
    return running

def feed_forward(inputs, weight_in, bias_in, weight_out, bias_out):
    inner = low_back(product(low(inputs), weight_in) + bias_in)
    return low_back(product(low(swish(inner)), weight_out) + bias_out)

def attention_branch(block_input, segment, attn_in, pos_proj, attn_out, vectors, pos_table):
    frames, features = block_input.shape
    head_size = features // HEADS
    score_scale = head_size ** (-0.5)
    queries = low_back(product(block_input, attn_in[:, :features]) + vectors[0])
    key_heads = low(low_back(product(block_input, attn_in[:, features:2 * features]))).reshape(frames, HEADS, head_size)
    value_heads = low(low_back(product(block_input, attn_in[:, 2 * features:]) + vectors[1])).reshape(frames, HEADS, head_size)
    query_content = low(queries + vectors[3]).reshape(frames, HEADS, head_size)
    query_position = low(queries + vectors[4]).reshape(frames, HEADS, head_size)
    position = low(low_back(product(pos_table, pos_proj))).reshape(2 * frames, HEADS, head_size)
    content = jnp.einsum('ihd,jhd->hij', query_content, key_heads, precision=highest)
    relative = jnp.einsum('ihd,ehd->hie', query_position, position, precision=highest)
    places = jnp.arange(frames, dtype=jnp.int32)
    index = (frames - places[:, None] + places[None, :]).astype(jnp.int32)
    shifted = jnp.take_along_axis(relative, jnp.broadcast_to(index[None], (HEADS, frames, frames)), axis=2)
    scores = low_back((content + shifted) * score_scale)
    scores = jnp.where((segment[:, None] == segment[None, :])[None], scores, masked_score)
    peak = lax.optimization_barrier(jnp.max(scores, axis=-1, keepdims=True))
    raised = jnp.exp(scores - peak)
    weights = raised / lax.optimization_barrier(jnp.sum(raised, axis=-1, keepdims=True))
    mixture = jnp.einsum('hij,jhd->ihd', low(weights), value_heads, precision=highest).reshape(frames, features)
    mixture = low(low_back(mixture))
    return low_back(product(mixture, attn_out) + vectors[2])

def first_layer(block_input, lengths, weights, pos_table):
    attn_in, pos_proj, attn_out, vectors, reduce_taps, reduce_proj, weight_in, bias_in, weight_out, gain_rows, shift_rows = weights
    frames, features = block_input.shape
    segment, inside = segment_ids(lengths, frames)
    attended = attention_branch(block_input, segment, attn_in, pos_proj, attn_out, vectors, pos_table)
    first_norm = layer_norm(block_input + attended, gain_rows[0], shift_rows[0])
    feed_out = feed_forward(first_norm, weight_in, bias_in, weight_out, shift_rows[2])
    output = layer_norm(first_norm + feed_out, gain_rows[1], shift_rows[1]) * inside[:, None]
    frame_pairs = output.reshape(frames // 2, 2, features)
    segment_pairs = segment.reshape(frames // 2, 2)
    before = jnp.pad(frame_pairs[:-1, 1], ((1, 0), (0, 0)))
    segment_before = jnp.pad(segment_pairs[:-1, 1], (1, 0), constant_values=-1)
    joined = (segment_before == segment_pairs[:, 0]).astype(output.dtype)[:, None]
    mixture = reduce_taps[0] * before * joined + reduce_taps[1] * frame_pairs[:, 0] + reduce_taps[2] * frame_pairs[:, 1]
    reduced = low(low_back(product(low(mixture), reduce_proj) + vectors[5]))
    return (reduced, low_back(low(output)))

def conv_front(reduced, segment, glu_in, conv_taps, vectors):
    features = reduced.shape[1]
    linear = low_back(product(reduced, glu_in[:, :features]) + vectors[0])
    gating = low_back(product(reduced, glu_in[:, features:]) + vectors[1])
    return depthwise(linear * jax.nn.sigmoid(gating), segment, conv_taps)

def conv_rest(convolved, reduced, skip_rows, inside, centre, inverse, weights):
    bn_gain, vectors, point_proj, weight_in, bias_in, weight_out, gain_rows, shift_rows = weights
    normed = (convolved - centre) * inverse * bn_gain + vectors[3]
    branch = low_back(product(low(swish(normed)), point_proj) + vectors[2])
    first_norm = layer_norm(reduced + branch, gain_rows[0], shift_rows[0])
    feed_out = feed_forward(first_norm, weight_in, bias_in, weight_out, shift_rows[2])
    output = layer_norm(first_norm + feed_out, gain_rows[1], shift_rows[1])
    return (jnp.repeat(output, 2, axis=0) + skip_rows) * inside[:, None]

def reference(boundary, utt_lengths, attn_in, pos_proj, attn_out, first_vectors, reduce_taps, reduce_proj, glu_in, conv_taps, second_vectors, bn_gain, point_proj, ffn_in, ffn_bias, ffn_out, norm_gain, block_vectors):
    row_count = FRAMES // FR
    buffers = MB * row_count
    features = D
    half_frames = FR // 2
    inputs_all = boundary[0].astype(jnp.float32).reshape(buffers, FR, features)
    cotangent = boundary[1].astype(jnp.float32).reshape(MB, row_count, FR, features)
    lengths = utt_lengths.reshape(buffers, SLOTS)
    pos_table = low(position_table(FR, features))
    segment_all, inside_all = jax.vmap(lambda bundle: segment_ids(bundle, FR))(lengths)
    segment_half = segment_all.reshape(buffers, half_frames, 2)[:, :, 0]
    inside_half = inside_all.reshape(buffers, half_frames, 2)[:, :, 0]
    weights = tuple((entry.astype(jnp.float32) for entry in (attn_in, pos_proj, attn_out, first_vectors, reduce_taps, reduce_proj, glu_in, conv_taps, second_vectors, bn_gain, point_proj, ffn_in, ffn_bias, ffn_out, norm_gain, block_vectors)))

    def forward(block_input, attn_in, pos_proj, attn_out, first_vectors, reduce_taps, reduce_proj, glu_in, conv_taps, second_vectors, bn_gain, point_proj, ffn_in, ffn_bias, ffn_out, norm_gain, block_vectors):
        first_weights = (attn_in, pos_proj, attn_out, first_vectors, reduce_taps, reduce_proj, ffn_in[0], ffn_bias[0], ffn_out[0], norm_gain[0], block_vectors[0])

        def first_one(bundle):
            return first_layer(bundle[0], bundle[1], first_weights, pos_table)
        reduced, skip_rows = lax.map(jax.checkpoint(first_one), (block_input, lengths))

        def front_one(bundle):
            return conv_front(bundle[0], bundle[1], glu_in, conv_taps, second_vectors)
        convolved = lax.map(jax.checkpoint(front_one), (reduced, segment_half))
        grouped = convolved.reshape(MB, row_count * half_frames, features)
        valid_mask = inside_half.reshape(MB, row_count * half_frames, 1)
        frame_count = lax.optimization_barrier(jnp.sum(valid_mask, axis=1))
        centre = lax.optimization_barrier(jnp.sum(grouped * valid_mask, axis=1)) / frame_count
        inverse = lax.rsqrt(lax.optimization_barrier(jnp.sum(grouped * grouped * valid_mask, axis=1)) / frame_count - centre * centre + epsilon)
        second_weights = (bn_gain, second_vectors, point_proj, ffn_in[1], ffn_bias[1], ffn_out[1], norm_gain[1], block_vectors[1])

        def rest_one(bundle):
            return conv_rest(bundle[0], bundle[1], bundle[2], bundle[3], bundle[4], bundle[5], second_weights)
        result = lax.map(jax.checkpoint(rest_one), (convolved, reduced, skip_rows, inside_all, jnp.repeat(centre, row_count, axis=0), jnp.repeat(inverse, row_count, axis=0)))
        return result.reshape(MB, row_count, FR, features)
    output, pullback = jax.vjp(forward, inputs_all, *weights)
    grads = pullback(cotangent)
    stacked = jnp.stack([grads[0].reshape(MB, FRAMES, features), output.reshape(MB, FRAMES, features)])
    return (stacked, grads[1], grads[2], grads[3], grads[4], grads[5], grads[6], grads[7], grads[8], grads[9], grads[10], grads[11], grads[12], grads[13], grads[14], grads[15], grads[16])
```

```python
import functools
import math

import jax
import jax.numpy as jnp
import numpy as np
from jax import lax
from jax.experimental import pallas as pl
from jax.experimental.pallas import tpu as pltpu
from jax.sharding import PartitionSpec as P

HEADS = 4
LANE = 128
SUB = 16
EPSILON = 1e-05
MASKED = -1e30
F32 = jnp.float32
BF16 = jnp.bfloat16
VMEM_LIMIT = 56 << 20


def up(value, step):
    return -(-value // step) * step


def low(values):
    return values.astype(BF16)


def dot(left, right, dims=((1,), (0,)), precision=None):
    return lax.dot_general(
        left, right, (dims, ((), ())), preferred_element_type=F32, precision=precision
    )


def dot_rows(left, right):
    return dot(left, right, ((0,), (0,)))


def dot_cols(left, right):
    return dot(left, right, ((1,), (1,)))


def row_sum(values):
    return jnp.sum(values.astype(F32), axis=0, keepdims=True)


def normalise(values):
    centre = values - jnp.mean(values, axis=-1, keepdims=True)
    inverse = lax.rsqrt(jnp.mean(centre * centre, axis=-1, keepdims=True) + EPSILON)
    return centre * inverse, inverse


def normalise_back(grad, normed, inverse, gain):
    scaled = grad * gain
    first = jnp.mean(scaled, axis=-1, keepdims=True)
    second = jnp.mean(scaled * normed, axis=-1, keepdims=True)
    return inverse * (scaled - first - normed * second)


def bounds_of(lens_ref, batch):
    ends = []
    total = jnp.int32(0)
    for slot in range(lens_ref.shape[-1]):
        total = total + lens_ref[batch, 0, slot]
        ends.append(total)
    return ends


def segment_of(position, ends):
    segment = jnp.zeros(position.shape, jnp.int32)
    for end in ends:
        segment = segment + (position >= end).astype(jnp.int32)
    return segment


def iota(shape, axis):
    return lax.broadcasted_iota(jnp.int32, shape, axis)


def head_select(rows, base, head, dtype):
    row = iota((rows, HEADS * LANE), 0) + base
    col = iota((rows, HEADS * LANE), 1)
    within = col % LANE
    hit = (row == (col // LANE) * head + within) & (within < head)
    return jnp.where(hit, 1.0, 0.0).astype(dtype)


def head_unselect(cols, head):
    row = iota((HEADS * LANE, cols), 0)
    col = iota((HEADS * LANE, cols), 1)
    within = row % LANE
    hit = (col == (row // LANE) * head + within) & (within < head)
    return jnp.where(hit, 1.0, 0.0).astype(BF16)


def copy_chosen(is_first, first_ref, second_ref, target, sem, act):
    @pl.when(is_first)
    def _():
        act(pltpu.make_async_copy(first_ref, target, sem))

    @pl.when(jnp.logical_not(is_first))
    def _():
        act(pltpu.make_async_copy(second_ref, target, sem))


def start(copy):
    copy.start()


def finish(copy):
    copy.wait()


class Pack:
    def __init__(self, out_ref, stage_ref, vec_ref):
        self.out, self.stage, self.vec = out_ref, stage_ref, vec_ref
        self.row = 0
        self.stage[...] = jnp.zeros(self.stage.shape, F32)
        self.vec[...] = jnp.zeros(self.vec.shape, F32)

    def matrix(self, values):
        rows, cols = values.shape
        high = up(rows, SUB)
        self.stage[0:rows, 0:cols] = values
        for at in range(0, cols, LANE):
            self.out[self.row : self.row + high, :] = low(self.stage[0:high, at : at + LANE])
            self.row += high

    def vector(self, at, values):
        self.vec[at : at + values.shape[0], 0 : values.shape[1]] = values

    def finish(self):
        for at in range(0, self.vec.shape[1], LANE):
            self.out[self.row : self.row + SUB, :] = low(self.vec[:, at : at + LANE])
            self.row += SUB
        if self.row < self.out.shape[0]:
            rest = self.out.shape[0] - self.row
            self.out[self.row :, :] = jnp.zeros((rest, LANE), BF16)


def attention_forward(
    lens_ref,
    own_ref,
    recv_ref,
    attn_in_ref,
    pos_proj_ref,
    attn_out_ref,
    vec_ref,
    table_ref,
    x_out,
    qu_out,
    qw_out,
    k_out,
    v_out,
    p_out,
    a_out,
    o_out,
    n1_out,
    inv1_out,
    w_out,
    wo_out,
):
    core = lax.axis_index("section")
    frames, features = x_out.shape
    head = features // HEADS
    width = HEADS * LANE
    ends = bounds_of(lens_ref, core)
    x = jnp.where(core == 0, own_ref[0, 0], recv_ref[0, 1])
    x_out[...] = x
    for part in range(3):
        begin = part * features
        floor = begin // LANE * LANE
        stop = min(up(begin + features, LANE), 3 * features)
        piece = attn_in_ref[:, floor:stop]
        chosen = head_select(stop - floor, floor - begin, head, BF16)
        w_out[:, part * width : (part + 1) * width] = low(dot(piece, chosen))
    select = head_select(features, 0, head, BF16)
    wo_out[...] = low(dot(head_unselect(features, head), attn_out_ref[...]))
    vectors = dot(
        vec_ref[...], head_select(features, 0, head, F32), precision=lax.Precision.HIGHEST
    )
    q = dot(x, w_out[:, 0:width]) + vectors[0:1]
    qu_out[...] = low(q + vectors[3:4])
    qw_out[...] = low(q + vectors[4:5])
    k_out[...] = low(dot(x, w_out[:, width : 2 * width]))
    v_out[...] = low(dot(x, w_out[:, 2 * width :]) + vectors[1:2])
    pos = low(dot(pos_proj_ref[...], select))
    p_out[...] = low(dot(table_ref[...], pos))
    same = segment_of(iota((frames, 1), 0), ends) == segment_of(iota((1, frames), 1), ends)
    scale = head**-0.5
    for h in range(HEADS):
        cols = slice(h * LANE, (h + 1) * LANE)
        content = dot_cols(qu_out[:, cols], k_out[:, cols])
        relative = dot_cols(qw_out[:, cols], p_out[:, cols])
        shifted = pltpu.roll(relative, 0, 1, stride=1, stride_axis=0)[:, frames:]
        scores = jnp.where(same, (content + shifted) * scale, MASKED)
        raised = jnp.exp(scores - jnp.max(scores, axis=-1, keepdims=True))
        weights = low(raised / jnp.sum(raised, axis=-1, keepdims=True))
        a_out[h] = weights
        o_out[:, cols] = low(dot(weights, v_out[:, cols]))
    attended = dot(o_out[...], wo_out[...]) + vec_ref[2:3, :]
    normed, inverse = normalise(x.astype(F32) + attended)
    n1_out[...] = normed
    inv1_out[...] = inverse


def half_masks(half, ends):
    position = 2 * iota((half, 1), 0)
    segment = segment_of(position, ends)
    before = segment_of(position - 1, ends)
    joined = jnp.where((segment == before) & (position > 0), 1.0, 0.0)
    valid = jnp.where(position < ends[-1], 1.0, 0.0)
    return joined, valid


def tap_ranges(half, ends, reach):
    position = iota((half, LANE), 0)
    first = jnp.zeros((half, LANE), jnp.int32)
    last = jnp.full((half, LANE), half, jnp.int32)
    for end in ends:
        edge = end // 2
        first = jnp.where(position >= edge, edge, first)
    for end in reversed(ends):
        edge = end // 2
        last = jnp.where(position < edge, edge, last)
    return first - position + reach, last - position + reach


def put_tiles(ref, at, values):
    rows, cols = values.shape
    for t in range(ref.shape[0]):
        stop = min(cols, (t + 1) * LANE)
        ref[t, at : at + rows, 0 : stop - t * LANE] = values[:, t * LANE : stop]


def get_tiles(ref, cols):
    return jnp.concatenate([ref[t] for t in range(ref.shape[0])], axis=1)[:, 0:cols]


def layer_vectors(own_ref, recv_ref, use_own, features):
    rows = jnp.where(use_own, own_ref[...], recv_ref[...])
    bias = rows[0:1, :]
    return bias, rows[1:3, 0:features], rows[3:6, 0:features]


def feed_forward(inputs, bias, w_in, w_out, shift, hid_ref, slope_ref):
    z = dot(low(inputs), w_in) + bias
    logistic = jax.nn.sigmoid(z)
    hid_ref[...] = low(z * logistic)
    slope_ref[...] = low(logistic * (1.0 + z * (1.0 - logistic)))
    return dot(hid_ref[...], w_out) + shift


def convolution_forward(
    lens_ref,
    n1_ref,
    sm_own,
    sm_recv,
    win_own,
    win_recv,
    wout_own,
    wout_recv,
    vec_ref,
    taps_ref,
    proj_ref,
    glu_ref,
    conv_ref,
    vec2_ref,
    hid_out,
    slope_out,
    n2_out,
    inv2_out,
    ml_out,
    red_out,
    lin_out,
    sg_out,
    u_out,
    c_out,
    stat_out,
    win,
    wout,
    t_sc,
    u_sc,
    k_sc,
    sem,
):
    core = lax.axis_index("section")
    first = core == 0
    frames, features = n1_ref.shape
    half = frames // 2
    copy_chosen(first, win_own.at[0], win_recv.at[0], win, sem.at[0], start)
    copy_chosen(first, wout_own.at[0], wout_recv.at[0], wout, sem.at[1], start)
    ends = bounds_of(lens_ref, core)
    bias, gains, shifts = layer_vectors(sm_own, sm_recv, first, features)
    h1 = n1_ref[...] * gains[0:1] + shifts[0:1]
    copy_chosen(first, win_own.at[0], win_recv.at[0], win, sem.at[0], finish)
    copy_chosen(first, wout_own.at[0], wout_recv.at[0], wout, sem.at[1], finish)
    fed = feed_forward(h1, bias, win[...], wout[...], shifts[2:3], hid_out, slope_out)
    n2, inv2 = normalise(h1 + fed)
    n2_out[...] = n2
    inv2_out[...] = inv2
    inside = jnp.where(iota((frames, 1), 0) < ends[-1], 1.0, 0.0)
    put_tiles(t_sc, 0, (n2 * gains[1:2] + shifts[1:2]) * inside)
    joined, valid = half_masks(half, ends)
    even, odd = even_odd(t_sc, half, features)
    before = pltpu.roll(odd, 1, 0) * joined
    mixed = low(taps_ref[0:1] * before + taps_ref[1:2] * even + taps_ref[2:3] * odd)
    ml_out[...] = mixed
    reduced = low(dot(mixed, proj_ref[...]) + vec_ref[5:6])
    red_out[...] = reduced
    gates = dot(reduced, glu_ref[...])
    linear = gates[:, 0:features] + vec2_ref[0:1]
    logistic = jax.nn.sigmoid(gates[:, features:] + vec2_ref[1:2])
    gated = linear * logistic
    lin_out[...] = linear
    sg_out[...] = logistic
    u_out[...] = gated
    tap_count = conv_ref.shape[0]
    reach = tap_count // 2
    lowest, highest = tap_ranges(half, ends, reach)
    u_sc[...] = jnp.zeros(u_sc.shape, F32)
    k_sc[...] = jnp.zeros(k_sc.shape, F32)
    put_tiles(u_sc, SUB, gated)
    put_tiles(k_sc, 0, conv_ref[...])
    pieces = []
    for t in range(u_sc.shape[0]):
        total = jnp.zeros((half, LANE), F32)
        for o in range(tap_count):
            moved = u_sc[t, SUB - reach + o : SUB - reach + o + half, :]
            fits = (lowest <= o) & (o < highest)
            total = total + jnp.where(fits, moved, 0.0) * k_sc[t, o : o + 1, :]
        pieces.append(total)
    convolved = jnp.concatenate(pieces, axis=1)[:, 0:features]
    c_out[...] = convolved
    held = convolved * valid
    send_rows(
        stat_out, [row_sum(held), row_sum(held * convolved)], jnp.sum(valid, axis=0, keepdims=True)
    )


def even_odd(ref, half, features):
    even = [ref[t, pl.ds(0, half, stride=2), :] for t in range(ref.shape[0])]
    odd = [ref[t, pl.ds(1, half, stride=2), :] for t in range(ref.shape[0])]
    return (
        jnp.concatenate(even, axis=1)[:, 0:features],
        jnp.concatenate(odd, axis=1)[:, 0:features],
    )


def put_even_odd(ref, even, odd):
    half, features = even.shape
    for t in range(ref.shape[0]):
        stop = min(features, (t + 1) * LANE)
        span = slice(0, stop - t * LANE)
        ref[t, pl.ds(0, half, stride=2), span] = even[:, t * LANE : stop]
        ref[t, pl.ds(1, half, stride=2), span] = odd[:, t * LANE : stop]


def send_rows(out_ref, rows, count=None):
    out_ref[...] = jnp.zeros(out_ref.shape, F32)
    peers = out_ref.shape[0]
    at = 0
    for row in rows:
        for begin in range(0, row.shape[1], LANE):
            stop = min(begin + LANE, row.shape[1])
            piece = row[:, begin:stop]
            out_ref[:, at : at + 1, 0 : stop - begin] = jnp.broadcast_to(
                piece[None], (peers, 1, stop - begin)
            )
            at += 1
    if count is not None:
        out_ref[:, at : at + 1, :] = jnp.broadcast_to(count[None], (peers, 1, LANE))


def gather_rows(ref, features):
    total = jnp.sum(ref[...], axis=0)
    tiles = up(features, LANE) // LANE
    rows = []
    for at in range(2):
        pieces = [total[at * tiles + t : at * tiles + t + 1, :] for t in range(tiles)]
        rows.append(jnp.concatenate(pieces, axis=1)[:, 0:features])
    return rows[0], rows[1], total[2 * tiles : 2 * tiles + 1, 0:1]


def batch_moments(stat_ref, features):
    first, second, count = gather_rows(stat_ref, features)
    centre = first / count
    return count, centre, lax.rsqrt(second / count - centre * centre + EPSILON)


def feed_back(grad, inputs, hid_ref, slope_ref, w_in, w_out, pack, vec_at):
    grad_low = low(grad)
    inner = low(dot_cols(grad_low, w_out) * slope_ref[...].astype(F32))
    back = dot_cols(inner, w_in)
    pack.matrix(dot_rows(inputs, inner))
    pack.matrix(dot_rows(grad_low, hid_ref[...]))
    pack.vector(0, row_sum(inner))
    pack.vector(vec_at, row_sum(grad_low))
    return back


def second_layer(
    lens_ref,
    stat_ref,
    c_ref,
    red_ref,
    n2_ref,
    sm_own,
    sm_recv,
    win_own,
    win_recv,
    wout_own,
    wout_recv,
    point_ref,
    vec2_ref,
    gain_ref,
    own_ref,
    recv_ref,
    y_out,
    dch_out,
    ch_out,
    dr3_out,
    sums_out,
    pack_out,
    win,
    wout,
    t_sc,
    y_sc,
    hid_sc,
    slope_sc,
    stage,
    vec_sc,
    sem,
):
    core = lax.axis_index("section")
    first = core == 0
    frames, features = n2_ref.shape
    half = frames // 2
    copy_chosen(first, win_recv.at[0], win_own.at[0], win, sem.at[0], start)
    copy_chosen(first, wout_recv.at[0], wout_own.at[0], wout, sem.at[1], start)
    ends = bounds_of(lens_ref, core)
    inside = jnp.where(iota((frames, 1), 0) < ends[-1], 1.0, 0.0)
    bias, gains, shifts = layer_vectors(sm_own, sm_recv, jnp.logical_not(first), features)
    gains0, shifts0 = layer_vectors(sm_own, sm_recv, first, features)[1:]
    count, centre, rho = batch_moments(stat_ref, features)
    ch = (c_ref[...] - centre) * rho
    bnv = ch * gain_ref[...] + vec2_ref[3:4]
    logistic = jax.nn.sigmoid(bnv)
    active = low(bnv * logistic)
    active_slope = logistic * (1.0 + bnv * (1.0 - logistic))
    branch = dot(active, point_ref[...]) + vec2_ref[2:3]
    n3, inv3 = normalise(red_ref[...].astype(F32) + branch)
    h3 = n3 * gains[0:1] + shifts[0:1]
    copy_chosen(first, win_recv.at[0], win_own.at[0], win, sem.at[0], finish)
    copy_chosen(first, wout_recv.at[0], wout_own.at[0], wout, sem.at[1], finish)
    fed = feed_forward(h3, bias, win[...], wout[...], shifts[2:3], hid_sc, slope_sc)
    n4, inv4 = normalise(h3 + fed)
    t2 = n4 * gains[1:2] + shifts[1:2]
    skip = low((n2_ref[...] * gains0[1:2] + shifts0[1:2]) * inside).astype(F32)
    put_even_odd(y_sc, t2, t2)
    y_out[...] = (get_tiles(y_sc, features) + skip) * inside
    grad = jnp.where(first, recv_ref[0, 0], own_ref[0, 1]).astype(F32) * inside
    put_tiles(t_sc, 0, grad)
    even, odd = even_odd(t_sc, half, features)
    dt2 = even + odd
    pack = Pack(pack_out, stage, vec_sc)
    dv4 = normalise_back(dt2, n4, inv4, gains[1:2])
    pack.vector(2, row_sum(dt2 * n4))
    pack.vector(4, row_sum(dt2))
    dh3 = dv4 + feed_back(
        dv4, low(h3), hid_sc, slope_sc, win[...], wout[...], pack, 5
    )
    dr3 = normalise_back(dh3, n3, inv3, gains[0:1])
    pack.vector(1, row_sum(dh3 * n3))
    pack.vector(3, row_sum(dh3))
    dr3_out[...] = dr3
    dpw = low(dr3)
    dbn = dot_cols(dpw, point_ref[...]) * active_slope
    dch = dbn * gain_ref[...]
    dch_out[...] = dch
    ch_out[...] = ch
    send_rows(sums_out, [row_sum(dch), row_sum(dch * ch)])
    pack.matrix(dot_rows(active, dpw))
    pack.vector(6, row_sum(dpw))
    pack.vector(7, row_sum(dbn))
    pack.vector(8, row_sum(dbn * ch))
    pack.finish()


def first_layer_back(
    lens_ref,
    stat_ref,
    sums_ref,
    dch_ref,
    ch_ref,
    dr3_ref,
    u_ref,
    lin_ref,
    sg_ref,
    red_ref,
    ml_ref,
    n2_ref,
    inv2_ref,
    n1_ref,
    inv1_ref,
    hid_ref,
    slope_ref,
    sm_own,
    sm_recv,
    win_own,
    win_recv,
    wout_own,
    wout_recv,
    taps_ref,
    proj_ref,
    glu_ref,
    conv_ref,
    own_ref,
    recv_ref,
    dr1_out,
    pack_out,
    win,
    wout,
    t_sc,
    u_sc,
    d_sc,
    k_sc,
    kd_sc,
    stage,
    vec_sc,
    sem,
):
    core = lax.axis_index("section")
    first = core == 0
    frames, features = n2_ref.shape
    half = frames // 2
    copy_chosen(first, win_own.at[0], win_recv.at[0], win, sem.at[0], start)
    copy_chosen(first, wout_own.at[0], wout_recv.at[0], wout, sem.at[1], start)
    ends = bounds_of(lens_ref, core)
    inside = jnp.where(iota((frames, 1), 0) < ends[-1], 1.0, 0.0)
    joined, valid = half_masks(half, ends)
    bias, gains, shifts = layer_vectors(sm_own, sm_recv, first, features)
    pack = Pack(pack_out, stage, vec_sc)
    count, centre, rho = batch_moments(stat_ref, features)
    sum1, sum2, _ = gather_rows(sums_ref, features)
    dc = (rho * valid) * (dch_ref[...] - sum1 / count - ch_ref[...] * (sum2 / count))
    tap_count = conv_ref.shape[0]
    reach = tap_count // 2
    lowest, highest = tap_ranges(half, ends, reach)
    u_sc[...] = jnp.zeros(u_sc.shape, F32)
    d_sc[...] = jnp.zeros(d_sc.shape, F32)
    k_sc[...] = jnp.zeros(k_sc.shape, F32)
    kd_sc[...] = jnp.zeros(kd_sc.shape, F32)
    put_tiles(u_sc, SUB, u_ref[...])
    put_tiles(d_sc, SUB, dc)
    put_tiles(k_sc, 0, conv_ref[...])
    pieces = []
    for t in range(u_sc.shape[0]):
        total = jnp.zeros((half, LANE), F32)
        here = d_sc[t, SUB : SUB + half, :]
        for o in range(tap_count):
            span = slice(SUB - reach + o, SUB - reach + o + half)
            fits = (lowest <= o) & (o < highest)
            back = tap_count - 1 - o
            total = total + jnp.where(fits, d_sc[t, span, :], 0.0) * k_sc[t, back : back + 1, :]
            kd_sc[t, o : o + 1, :] = row_sum(jnp.where(fits, u_sc[t, span, :], 0.0) * here)
        pieces.append(total)
    du = jnp.concatenate(pieces, axis=1)[:, 0:features]
    logistic = sg_ref[...]
    dlin = low(du * logistic)
    dgat = low(du * lin_ref[...] * logistic * (1.0 - logistic))
    reduced = red_ref[...]
    dred = low(
        dot_cols(dlin, glu_ref[:, 0:features])
        + dot_cols(dgat, glu_ref[:, features:])
        + dr3_ref[...]
    )
    pack.matrix(dot_rows(reduced, dlin))
    pack.matrix(dot_rows(reduced, dgat))
    pack.matrix(dot_rows(ml_ref[...], dred))
    pack.vector(9, row_sum(dlin))
    pack.vector(10, row_sum(dgat))
    pack.vector(11, row_sum(dred))
    dm = dot_cols(dred, proj_ref[...])
    n2 = n2_ref[...]
    put_tiles(t_sc, 0, (n2 * gains[1:2] + shifts[1:2]) * inside)
    even, odd = even_odd(t_sc, half, features)
    pack.vector(6, row_sum(pltpu.roll(odd, 1, 0) * joined * dm))
    pack.vector(7, row_sum(even * dm))
    pack.vector(8, row_sum(odd * dm))
    carried = pltpu.roll(taps_ref[0:1] * joined * dm, half - 1, 0)
    put_even_odd(t_sc, taps_ref[1:2] * dm, taps_ref[2:3] * dm + carried)
    grad = jnp.where(first, recv_ref[0, 0], own_ref[0, 1]).astype(F32)
    dt = (grad + get_tiles(t_sc, features)) * inside
    dv2 = normalise_back(dt, n2, inv2_ref[...], gains[1:2])
    pack.vector(2, row_sum(dt * n2))
    pack.vector(4, row_sum(dt))
    n1 = n1_ref[...]
    h1 = low(n1 * gains[0:1] + shifts[0:1])
    copy_chosen(first, win_own.at[0], win_recv.at[0], win, sem.at[0], finish)
    copy_chosen(first, wout_own.at[0], wout_recv.at[0], wout, sem.at[1], finish)
    dh1 = dv2 + feed_back(dv2, h1, hid_ref, slope_ref, win[...], wout[...], pack, 5)
    pack.vector(1, row_sum(dh1 * n1))
    pack.vector(3, row_sum(dh1))
    dr1_out[...] = normalise_back(dh1, n1, inv1_ref[...], gains[0:1])
    for t in range(kd_sc.shape[0]):
        pack.out[pack.row : pack.row + kd_sc.shape[1], :] = low(kd_sc[t])
        pack.row += kd_sc.shape[1]
    pack.finish()


def attention_back(
    dr1_ref,
    x_ref,
    qu_ref,
    qw_ref,
    k_ref,
    v_ref,
    p_ref,
    a_ref,
    o_ref,
    w_ref,
    wo_ref,
    table_ref,
    y_ref,
    keep_out,
    send_out,
    pack_out,
    do_sc,
    qwr_sc,
    dqr_sc,
    dkv_sc,
    dp_sc,
    sum_sc,
    stage,
    vec_sc,
):
    core = lax.axis_index("section")
    frames, features = x_ref.shape
    head = features // HEADS
    width = HEADS * LANE
    scale = head**-0.5
    pack = Pack(pack_out, stage, vec_sc)
    dr1 = dr1_ref[...]
    dr1_low = low(dr1)
    unselect = head_unselect(features, head)
    pack.vector(2, row_sum(dr1_low))
    grad_out = low(dot_rows(o_ref[...], dr1_low))
    pack.matrix(dot_rows(unselect, grad_out))
    do_sc[...] = low(dot_cols(dr1_low, wo_ref[...]))
    flip = jnp.where(
        iota((frames, frames), 0) + iota((frames, frames), 1) == frames - 1, 1.0, 0.0
    ).astype(BF16)
    qwr_sc[...] = low(dot(flip, qw_ref[...]))
    for h in range(HEADS):
        cols = slice(h * LANE, (h + 1) * LANE)
        weights = a_ref[h]
        grad = do_sc[:, cols]
        weights_f = weights.astype(F32)
        product = weights_f * dot_cols(grad, v_ref[:, cols])
        ds = low(product - weights_f * jnp.sum(product, axis=-1, keepdims=True))
        dkv_sc[:, width + h * LANE : width + (h + 1) * LANE] = low(dot_rows(weights, grad))
        dkv_sc[:, cols] = low(scale * dot_rows(ds, qu_ref[:, cols]))
        dsr = low(dot(flip, ds))
        wide = jnp.concatenate([jnp.zeros((frames, frames), BF16), dsr], axis=1)
        band = pltpu.roll(wide.astype(F32), frames + 1, 1, stride=1, stride_axis=0).astype(BF16)
        dqu = scale * dot(dsr, k_ref[:, cols])
        dqw = scale * dot(band, p_ref[:, cols])
        dqr_sc[:, cols] = low(dqu + dqw)
        dp_sc[:, cols] = low(scale * dot_rows(band, qwr_sc[:, cols]))
        sum_sc[0:1, cols] = row_sum(dqu)
        sum_sc[1:2, cols] = row_sum(dqw)
    dq = low(dot(flip, dqr_sc[...]))
    dkv = dkv_sc[...]
    x = x_ref[...]
    chosen = unselect.astype(F32)
    sums = jnp.concatenate(
        [
            row_sum(dq),
            row_sum(dkv[:, width:]),
            sum_sc[0:2, :],
        ],
        axis=0,
    )
    sums = dot(sums, chosen, precision=lax.Precision.HIGHEST)
    pack.vector(0, sums[0:2])
    pack.vector(3, sums[2:4])
    pack.matrix(dot(low(dot_rows(x, dq)), unselect))
    pack.matrix(dot(low(dot_rows(x, dkv[:, 0:width])), unselect))
    pack.matrix(dot(low(dot_rows(x, dkv[:, width:])), unselect))
    pack.matrix(dot(low(dot_rows(table_ref[...], dp_sc[...])), unselect))
    dx = dr1 + dot_cols(dq, w_ref[:, 0:width]) + dot_cols(dkv, w_ref[:, width:])
    y = y_ref[...]
    keep_out[...] = jnp.where(core == 0, dx, y)
    send_out[...] = jnp.where(core == 0, y, dx)
    pack.finish()


def unpack(
    keep_ref,
    recv_ref,
    one_ref,
    two_ref,
    three_ref,
    boundary_out,
    attn_in_out,
    pos_out,
    attn_out_out,
    vec_out,
    taps_out,
    proj_out,
    glu_out,
    conv_out,
    vec2_out,
    gain_out,
    point_out,
    win_out,
    bias_out,
    wout_out,
    norm_out,
    block_out,
):
    core = lax.axis_index("section")
    features = pos_out.shape[0]
    inner = win_out.shape[2]
    high = up(features, SUB)
    tiles = up(features, LANE) // LANE
    inner_tiles = up(inner, LANE) // LANE
    boundary_out[0, pl.ds(core, 1)] = keep_ref[...][None]
    boundary_out[0, pl.ds(1 - core, 1)] = recv_ref[...][None]

    def square(ref, row):
        pieces = [ref[row + t * high : row + (t + 1) * high, :] for t in range(tiles)]
        return jnp.concatenate(pieces, axis=1).astype(F32)[0:features, 0:features]

    def vectors(ref, row, count):
        pieces = [ref[row + t * SUB : row + (t + 1) * SUB, :] for t in range(count)]
        return jnp.concatenate(pieces, axis=1).astype(F32)

    three = three_ref
    at = 0
    attn_out_out[...] = square(three, at)
    at += tiles * high
    for part in range(3):
        attn_in_out[:, part * features : (part + 1) * features] = square(three, at)
        at += tiles * high
    pos_out[...] = square(three, at)
    at += tiles * high
    rows3 = vectors(three, at, tiles)[:, 0:features]
    vec_out[0:5, :] = rows3[0:5]

    one_at, two_at = 0, 3 * tiles * high
    glu_out[:, 0:features] = square(two_ref, 0)
    glu_out[:, features:] = square(two_ref, tiles * high)
    proj_out[...] = square(two_ref, 2 * tiles * high)

    def feed(ref, begin):
        for t in range(inner_tiles):
            stop = min(inner, (t + 1) * LANE)
            piece = ref[begin + t * high : begin + (t + 1) * high, :].astype(F32)
            win_out[0, :, t * LANE : stop] = piece[0:features, 0 : stop - t * LANE]
        begin += inner_tiles * high
        for t in range(inner_tiles):
            stop = min(inner, (t + 1) * LANE)
            piece = ref[begin + t * high : begin + (t + 1) * high, :].astype(F32)
            wout_out[0, t * LANE : stop, :] = piece.T[0 : stop - t * LANE, 0:features]

    @pl.when(core == 0)
    def _():
        feed(two_ref, two_at)

    @pl.when(core != 0)
    def _():
        feed(one_ref, one_at)

    one_at += 2 * inner_tiles * high
    two_at += 2 * inner_tiles * high
    point_out[...] = square(one_ref, one_at)
    one_at += tiles * high
    taps = conv_out.shape[0]
    tap_rows = up(taps, SUB)
    pieces = [two_ref[two_at + t * tap_rows : two_at + (t + 1) * tap_rows, :] for t in range(tiles)]
    conv_out[...] = jnp.concatenate(pieces, axis=1).astype(F32)[0:taps, 0:features]
    two_at += tiles * tap_rows
    rows1 = vectors(one_ref, one_at, inner_tiles)
    rows2 = vectors(two_ref, two_at, inner_tiles)
    vec_out[5:6, :] = rows2[11:12, 0:features]
    taps_out[...] = rows2[6:9, 0:features]
    vec2_out[0:2, :] = rows2[9:11, 0:features]
    vec2_out[2:4, :] = rows1[6:8, 0:features]
    gain_out[...] = rows1[8:9, 0:features]
    rows = jnp.where(core == 0, rows2, rows1)
    bias_out[...] = rows[0:1, 0:inner]
    norm_out[0] = rows[1:3, 0:features]
    block_out[0] = rows[3:6, 0:features]


def shape(dims, dtype=F32):
    return jax.ShapeDtypeStruct(dims, dtype)


SMEM = pl.BlockSpec(memory_space=pltpu.SMEM)
VMEM = pl.BlockSpec(memory_space=pltpu.VMEM)
ANY = pl.BlockSpec(memory_space=pl.ANY)


def call(kernel, name, in_specs, out_shape, scratch=(), flops=0, bytes_accessed=0):
    return pl.pallas_call(
        kernel,
        name=name,
        in_specs=in_specs,
        out_specs=[VMEM] * len(out_shape),
        out_shape=out_shape,
        scratch_shapes=list(scratch),
        compiler_params=pltpu.CompilerParams(vmem_limit_bytes=VMEM_LIMIT),
        cost_estimate=pl.CostEstimate(
            flops=flops, bytes_accessed=bytes_accessed, transcendentals=0
        ),
    )


def position_table(frames, features):
    distance = (frames - np.arange(2 * frames)).astype(np.float32)
    frequency = np.exp(
        np.arange(0, features, 2).astype(np.float32) * np.float32(-math.log(10000.0) / features)
    ).astype(np.float32)
    angles = (distance[:, None] * frequency[None, :]).astype(np.float64)
    table = np.stack([np.sin(angles), np.cos(angles)], axis=-1).reshape(2 * frames, features)
    return jnp.asarray(table.astype(np.float32), BF16)


def swap(values):
    return lax.ppermute(values, "section", [(0, 1), (1, 0)])


def total(pack):
    return lax.psum(pack, ("section", "rows"))


def everyone(values):
    return lax.all_to_all(values, "rows", 0, 0, tiled=True)


def shards(
    boundary,
    utt_lengths,
    attn_in,
    pos_proj,
    attn_out,
    first_vectors,
    reduce_taps,
    reduce_proj,
    glu_in,
    conv_taps,
    second_vectors,
    bn_gain,
    point_proj,
    ffn_in,
    ffn_bias,
    ffn_out,
    norm_gain,
    block_vectors,
):
    peers = lax.axis_size("rows")
    _, batches, frames, features = boundary.shape
    half = frames // 2
    inner = ffn_in.shape[2]
    width = HEADS * LANE
    high = up(features, SUB)
    tiles = up(features, LANE) // LANE
    inner_tiles = up(inner, LANE) // LANE
    tap_rows = up(conv_taps.shape[0], SUB)
    grain = 2 * peers * SUB
    pack_rows = [
        up(high * (2 * inner_tiles + tiles) + SUB * inner_tiles, grain),
        up(high * (2 * inner_tiles + 3 * tiles) + (SUB * inner_tiles + tap_rows * tiles), grain),
        up(high * 5 * tiles + SUB * tiles, grain),
    ]
    table = position_table(frames, features)
    gain_row = bn_gain[None]

    recv = swap(boundary)
    small = jnp.concatenate(
        [
            ffn_bias,
            jnp.pad(norm_gain[0], ((0, 0), (0, inner - features))),
            jnp.pad(block_vectors[0], ((0, 0), (0, inner - features))),
        ],
        axis=0,
    )
    win_recv, wout_recv, small_recv = swap(ffn_in), swap(ffn_out), swap(small)

    x, qu, qw, k, v, p, a, o, n1, inv1, w_pad, wo_pad = call(
        attention_forward,
        "attention_forward",
        [SMEM] + [VMEM] * 7,
        [
            shape((frames, features), BF16),
            shape((frames, width), BF16),
            shape((frames, width), BF16),
            shape((frames, width), BF16),
            shape((frames, width), BF16),
            shape((2 * frames, width), BF16),
            shape((HEADS, frames, frames), BF16),
            shape((frames, width), BF16),
            shape((frames, features)),
            shape((frames, 1)),
            shape((features, 3 * width), BF16),
            shape((width, features), BF16),
        ],
        flops=2 * 10**9,
        bytes_accessed=10**7,
    )(utt_lengths, boundary, recv, attn_in, pos_proj, attn_out, first_vectors, table)

    weights_scratch = [pltpu.VMEM((features, inner), BF16), pltpu.VMEM((inner, features), BF16)]
    rows_scratch = pltpu.VMEM((tiles, frames, LANE), F32)
    edge_scratch = pltpu.VMEM((tiles, half + 2 * SUB, LANE), F32)
    taps_scratch = pltpu.VMEM((tiles, tap_rows, LANE), F32)
    stage_scratch = pltpu.VMEM((high, inner_tiles * LANE), F32)
    vec_scratch = pltpu.VMEM((SUB, inner_tiles * LANE), F32)
    two_sems = pltpu.SemaphoreType.DMA((2,))

    hid, slope, n2, inv2, ml, red, lin, sg, u, c, stat = call(
        convolution_forward,
        "convolution_forward",
        [SMEM] + [VMEM] * 3 + [ANY] * 4 + [VMEM] * 6,
        [
            shape((frames, inner), BF16),
            shape((frames, inner), BF16),
            shape((frames, features)),
            shape((frames, 1)),
            shape((half, features), BF16),
            shape((half, features), BF16),
            shape((half, features)),
            shape((half, features)),
            shape((half, features)),
            shape((half, features)),
            shape((peers, 8, LANE)),
        ],
        weights_scratch
        + [rows_scratch, edge_scratch, taps_scratch, two_sems],
        flops=10**9,
        bytes_accessed=10**7,
    )(
        utt_lengths,
        n1,
        small,
        small_recv,
        ffn_in,
        win_recv,
        ffn_out,
        wout_recv,
        first_vectors,
        reduce_taps,
        reduce_proj,
        glu_in,
        conv_taps,
        second_vectors,
    )
    stat = everyone(stat)
    y, dch, ch, dr3, sums, pack1 = call(
        second_layer,
        "second_layer",
        [SMEM] + [VMEM] * 6 + [ANY] * 4 + [VMEM] * 5,
        [
            shape((frames, features)),
            shape((half, features)),
            shape((half, features)),
            shape((half, features)),
            shape((peers, 8, LANE)),
            shape((pack_rows[0], LANE), BF16),
        ],
        weights_scratch
        + [
            rows_scratch,
            rows_scratch,
            pltpu.VMEM((half, inner), BF16),
            pltpu.VMEM((half, inner), BF16),
            stage_scratch,
            vec_scratch,
            two_sems,
        ],
        flops=2 * 10**9,
        bytes_accessed=10**7,
    )(
        utt_lengths,
        stat,
        c,
        red,
        n2,
        small,
        small_recv,
        ffn_in,
        win_recv,
        ffn_out,
        wout_recv,
        point_proj,
        second_vectors,
        gain_row,
        boundary,
        recv,
    )
    sums = everyone(sums)
    one = total(pack1)
    dr1, pack2 = call(
        first_layer_back,
        "first_layer_back",
        [SMEM] + [VMEM] * 18 + [ANY] * 4 + [VMEM] * 6,
        [shape((frames, features)), shape((pack_rows[1], LANE), BF16)],
        weights_scratch
        + [
            rows_scratch,
            edge_scratch,
            edge_scratch,
            taps_scratch,
            taps_scratch,
            stage_scratch,
            vec_scratch,
            two_sems,
        ],
        flops=2 * 10**9,
        bytes_accessed=10**7,
    )(
        utt_lengths,
        stat,
        sums,
        dch,
        ch,
        dr3,
        u,
        lin,
        sg,
        red,
        ml,
        n2,
        inv2,
        n1,
        inv1,
        hid,
        slope,
        small,
        small_recv,
        ffn_in,
        win_recv,
        ffn_out,
        wout_recv,
        reduce_taps,
        reduce_proj,
        glu_in,
        conv_taps,
        boundary,
        recv,
    )
    two = total(pack2)
    keep, send, pack3 = call(
        attention_back,
        "attention_back",
        [VMEM] * 13,
        [
            shape((frames, features)),
            shape((frames, features)),
            shape((pack_rows[2], LANE), BF16),
        ],
        [
            pltpu.VMEM((frames, width), BF16),
            pltpu.VMEM((frames, width), BF16),
            pltpu.VMEM((frames, width), BF16),
            pltpu.VMEM((frames, 2 * width), BF16),
            pltpu.VMEM((2 * frames, width), BF16),
            pltpu.VMEM((8, width), F32),
            pltpu.VMEM((high, tiles * LANE), F32),
            pltpu.VMEM((SUB, tiles * LANE), F32),
        ],
        flops=3 * 10**9,
        bytes_accessed=10**7,
    )(dr1, x, qu, qw, k, v, p, a, o, w_pad, wo_pad, table, y)
    arrived = swap(send)
    three = total(pack3)
    outs = call(
        unpack,
        "unpack",
        [VMEM] * 5,
        [
            shape((1, batches, frames, features)),
            shape(attn_in.shape),
            shape(pos_proj.shape),
            shape(attn_out.shape),
            shape(first_vectors.shape),
            shape(reduce_taps.shape),
            shape(reduce_proj.shape),
            shape(glu_in.shape),
            shape(conv_taps.shape),
            shape(second_vectors.shape),
            shape((1, features)),
            shape(point_proj.shape),
            shape(ffn_in.shape),
            shape(ffn_bias.shape),
            shape(ffn_out.shape),
            shape(norm_gain.shape),
            shape(block_vectors.shape),
        ],
        bytes_accessed=10**7,
    )(keep, arrived, one, two, three)
    outs = list(outs)
    outs[10] = outs[10][0]
    return tuple(outs)


def solution(mesh):
    split = (
        P("section", None, None),
        P("section", None),
        P("section", None, None),
        P("section", None, None),
        P("section", None, None),
    )
    return jax.shard_map(
        shards,
        mesh=mesh,
        in_specs=(P("section", None, "rows", None), P(None, "rows", None)) + (P(),) * 11 + split,
        out_specs=(P("section", None, "rows", None),) + (P(),) * 11 + split,
        check_vma=False,
    )
```

```python
import functools
import math

import jax
import jax.numpy as jnp
import numpy as np
from jax import lax
from jax.experimental import pallas as pl
from jax.experimental.pallas import tpu as pltpu
from jax.sharding import PartitionSpec as P

HEADS = 4
LANE = 128
SUB = 16
EPSILON = 1e-05
MASKED = -1e30
F32 = jnp.float32
BF16 = jnp.bfloat16
VMEM_LIMIT = 28 << 20
STEP_LIMIT = 8 << 20


def up(value, step):
    return -(-value // step) * step


def low(values):
    return values.astype(BF16)


def dot(left, right, dims=((1,), (0,)), precision=None):
    return lax.dot_general(
        left, right, (dims, ((), ())), preferred_element_type=F32, precision=precision
    )


def dot_rows(left, right):
    return dot(left, right, ((0,), (0,)))


def dot_cols(left, right):
    return dot(left, right, ((1,), (1,)))


def row_sum(values):
    return jnp.sum(values.astype(F32), axis=0, keepdims=True)


def normalise(values):
    centre = values - jnp.mean(values, axis=-1, keepdims=True)
    inverse = lax.rsqrt(jnp.mean(centre * centre, axis=-1, keepdims=True) + EPSILON)
    return centre * inverse, inverse


def normalise_back(grad, normed, inverse, gain):
    scaled = grad * gain
    first = jnp.mean(scaled, axis=-1, keepdims=True)
    second = jnp.mean(scaled * normed, axis=-1, keepdims=True)
    return inverse * (scaled - first - normed * second)


def bounds_of(lens_ref, batch):
    ends = []
    total = jnp.int32(0)
    for slot in range(lens_ref.shape[-1]):
        total = total + lens_ref[batch, 0, slot]
        ends.append(total)
    return ends


def segment_of(position, ends):
    segment = jnp.zeros(position.shape, jnp.int32)
    for end in ends:
        segment = segment + (position >= end).astype(jnp.int32)
    return segment


def iota(shape, axis):
    return lax.broadcasted_iota(jnp.int32, shape, axis)


def head_select(rows, base, head, dtype):
    row = iota((rows, HEADS * LANE), 0) + base
    col = iota((rows, HEADS * LANE), 1)
    within = col % LANE
    hit = (row == (col // LANE) * head + within) & (within < head)
    return jnp.where(hit, 1.0, 0.0).astype(dtype)


def head_unselect(cols, head):
    row = iota((HEADS * LANE, cols), 0)
    col = iota((HEADS * LANE, cols), 1)
    within = row % LANE
    hit = (col == (row // LANE) * head + within) & (within < head)
    return jnp.where(hit, 1.0, 0.0).astype(BF16)


def choose(use_own, own_ref, other_ref, target):
    @pl.when(use_own)
    def _():
        target[...] = own_ref[0]

    @pl.when(jnp.logical_not(use_own))
    def _():
        target[...] = other_ref[0]


class Pack:
    def __init__(self, out_ref, stage_ref, vec_ref):
        self.out, self.stage, self.vec = out_ref, stage_ref, vec_ref
        self.row = 0
        self.col = 0
        self.used = 0
        self.vec[...] = jnp.zeros(self.vec.shape, F32)

    def matrix(self, values):
        rows, cols = values.shape
        self.stage[0:rows, self.col : self.col + cols] = values
        self.col += cols
        self.used = max(self.used, self.col)
        self.rows = rows

    def vector(self, at, values):
        self.vec[at : at + values.shape[0], 0 : values.shape[1]] = values

    def put(self, values):
        self.out[self.row : self.row + values.shape[0], :] = low(values)
        self.row += values.shape[0]

    def finish(self, core, keep_out, send_out, others=()):
        high, wide = self.stage.shape
        self.stage[self.rows : high, :] = jnp.zeros((high - self.rows, wide), F32)
        if self.used < wide:
            self.stage[:, self.used : wide] = jnp.zeros((high, wide - self.used), F32)
        for at in range(0, wide, LANE):
            self.put(self.stage[:, at : at + LANE])
        for values in others:
            self.put(values)
        for at in range(0, self.vec.shape[1], LANE):
            self.put(self.vec[:, at : at + LANE])
        if self.row < self.out.shape[0]:
            self.put(jnp.zeros((self.out.shape[0] - self.row, LANE), F32))
        half = self.out.shape[0] // 2
        keep_out[...] = self.out[pl.ds(pl.multiple_of(core * half, SUB), half), :]
        send_out[...] = self.out[pl.ds(pl.multiple_of((1 - core) * half, SUB), half), :]


def prepare(
    attn_in_hbm,
    pos_proj_hbm,
    attn_out_hbm,
    vec_hbm,
    table_hbm,
    p_out,
    w_out,
    wo_out,
    vectors_out,
    attn_in_ref,
    pos_proj_ref,
    attn_out_ref,
    vec_ref,
    table_ref,
    sem,
):
    sources = (pos_proj_hbm, table_hbm, attn_in_hbm, attn_out_hbm, vec_hbm)
    targets = (pos_proj_ref, table_ref, attn_in_ref, attn_out_ref, vec_ref)
    copies = [
        pltpu.make_async_copy(source, target, sem.at[at])
        for at, (source, target) in enumerate(zip(sources, targets))
    ]
    for copy in copies:
        copy.start()
    features = attn_out_ref.shape[0]
    head = features // HEADS
    width = HEADS * LANE
    select = head_select(features, 0, head, BF16)
    copies[0].wait()
    pos = low(dot(pos_proj_ref[...], select))
    copies[1].wait()
    p_out[...] = low(dot(table_ref[...], pos))
    copies[2].wait()
    for part in range(3):
        begin = part * features
        floor = begin // LANE * LANE
        stop = min(up(begin + features, LANE), 3 * features)
        piece = attn_in_ref[:, floor:stop]
        chosen = head_select(stop - floor, floor - begin, head, BF16)
        w_out[:, part * width : (part + 1) * width] = low(dot(piece, chosen))
    copies[3].wait()
    wo_out[...] = low(dot(head_unselect(features, head), attn_out_ref[...]))
    copies[4].wait()
    vectors_out[...] = dot(
        vec_ref[...], head_select(features, 0, head, F32), precision=lax.Precision.HIGHEST
    )


def attention_forward(
    lens_ref,
    own_ref,
    recv_ref,
    p_ref,
    w_ref,
    wo_ref,
    vectors_ref,
    vec_ref,
    xt_out,
    qu_out,
    qw_out,
    k_out,
    v_out,
    a_out,
    o_out,
    n1_out,
    inv1_out,
):
    core = lax.axis_index("section")
    features, frames = xt_out.shape
    head = features // HEADS
    width = HEADS * LANE
    ends = bounds_of(lens_ref, core)
    x_turned = jnp.where(core == 0, own_ref[0, :, 0, :], recv_ref[0, :, 1, :])
    xt_out[...] = x_turned
    x_rows = x_turned.astype(F32).T
    x = low(x_rows)
    vectors = vectors_ref[...]
    q = dot(x, w_ref[:, 0:width]) + vectors[0:1]
    qu_out[...] = low(q + vectors[3:4])
    qw_out[...] = low(q + vectors[4:5])
    k_out[...] = low(dot(x, w_ref[:, width : 2 * width]))
    v_out[...] = low(dot(x, w_ref[:, 2 * width :]) + vectors[1:2])
    same = segment_of(iota((frames, 1), 0), ends) == segment_of(iota((1, frames), 1), ends)
    scale = head**-0.5
    for h in range(HEADS):
        cols = slice(h * LANE, (h + 1) * LANE)
        content = dot_cols(qu_out[:, cols], k_out[:, cols])
        relative = dot_cols(qw_out[:, cols], p_ref[:, cols])
        shifted = pltpu.roll(relative, 0, 1, stride=1, stride_axis=0)[:, frames:]
        scores = jnp.where(same, (content + shifted) * scale, MASKED)
        raised = jnp.exp(scores - jnp.max(scores, axis=-1, keepdims=True))
        weights = low(raised / jnp.sum(raised, axis=-1, keepdims=True))
        a_out[h] = weights
        o_out[:, cols] = low(dot(weights, v_out[:, cols]))
    attended = dot(o_out[...], wo_ref[...]) + vec_ref[2:3, :]
    normed, inverse = normalise(x_rows + attended)
    n1_out[...] = normed
    inv1_out[...] = inverse


def half_masks(half, ends):
    position = 2 * iota((half, 1), 0)
    segment = segment_of(position, ends)
    before = segment_of(position - 1, ends)
    joined = jnp.where((segment == before) & (position > 0), 1.0, 0.0)
    valid = jnp.where(position < ends[-1], 1.0, 0.0)
    return joined, valid


def tap_ranges(half, ends, reach):
    position = iota((half, LANE), 0)
    first = jnp.zeros((half, LANE), jnp.int32)
    last = jnp.full((half, LANE), half, jnp.int32)
    for end in ends:
        edge = end // 2
        first = jnp.where(position >= edge, edge, first)
    for end in reversed(ends):
        edge = end // 2
        last = jnp.where(position < edge, edge, last)
    return first - position + reach, last - position + reach


def put_tiles(ref, at, values):
    rows, cols = values.shape
    for t in range(ref.shape[0]):
        stop = min(cols, (t + 1) * LANE)
        ref[t, at : at + rows, 0 : stop - t * LANE] = values[:, t * LANE : stop]


def get_tiles(ref, cols):
    return jnp.concatenate([ref[t] for t in range(ref.shape[0])], axis=1)[:, 0:cols]


def layer_vectors(refs, use_own):
    bias, gains, shifts = [
        jnp.where(use_own, own[...], other[...]) for own, other in zip(refs[0:3], refs[3:6])
    ]
    return bias, gains[0], jnp.concatenate([shifts[at] for at in range(3)], axis=0)


def feed_forward(inputs, bias, w_in, w_out, shift, hid_ref, slope_ref):
    z = dot(low(inputs), w_in) + bias
    logistic = jax.nn.sigmoid(z)
    hid_ref[...] = low(z * logistic)
    slope_ref[...] = low(logistic * (1.0 + z * (1.0 - logistic)))
    return dot_cols(hid_ref[...], w_out) + shift


def convolution_forward(
    lens_ref,
    n1_ref,
    bias_own,
    gain_own,
    shift_own,
    bias_recv,
    gain_recv,
    shift_recv,
    win_own,
    win_recv,
    wout_own,
    wout_recv,
    vec_ref,
    taps_ref,
    proj_ref,
    glu_ref,
    conv_ref,
    vec2_ref,
    hid_out,
    slope_out,
    n2_out,
    inv2_out,
    ml_out,
    red_out,
    lin_out,
    sg_out,
    u_out,
    c_out,
    stat_out,
    win,
    wout,
    t_sc,
    u_sc,
    k_sc,
):
    core = lax.axis_index("section")
    first = core == 0
    frames, features = n1_ref.shape
    half = frames // 2
    choose(first, win_own, win_recv, win)
    choose(first, wout_own, wout_recv, wout)
    ends = bounds_of(lens_ref, core)
    small = (bias_own, gain_own, shift_own, bias_recv, gain_recv, shift_recv)
    bias, gains, shifts = layer_vectors(small, first)
    h1 = n1_ref[...] * gains[0:1] + shifts[0:1]
    fed = feed_forward(h1, bias, win[...], wout[...], shifts[2:3], hid_out, slope_out)
    n2, inv2 = normalise(h1 + fed)
    n2_out[...] = n2
    inv2_out[...] = inv2
    inside = jnp.where(iota((frames, 1), 0) < ends[-1], 1.0, 0.0)
    put_tiles(t_sc, 0, (n2 * gains[1:2] + shifts[1:2]) * inside)
    joined, valid = half_masks(half, ends)
    even, odd = even_odd(t_sc, half, features)
    before = pltpu.roll(odd, 1, 0) * joined
    mixed = low(taps_ref[0:1] * before + taps_ref[1:2] * even + taps_ref[2:3] * odd)
    ml_out[...] = mixed
    reduced = low(dot(mixed, proj_ref[...]) + vec_ref[5:6])
    red_out[...] = reduced
    gates = dot_cols(reduced, glu_ref[...])
    linear = gates[:, 0:features] + vec2_ref[0:1]
    logistic = jax.nn.sigmoid(gates[:, features:] + vec2_ref[1:2])
    gated = linear * logistic
    lin_out[...] = linear
    sg_out[...] = logistic
    u_out[...] = gated
    tap_count = conv_ref.shape[0]
    reach = tap_count // 2
    lowest, highest = tap_ranges(half, ends, reach)
    u_sc[...] = jnp.zeros(u_sc.shape, F32)
    k_sc[...] = jnp.zeros(k_sc.shape, F32)
    put_tiles(u_sc, SUB, gated)
    put_tiles(k_sc, 0, conv_ref[...])
    pieces = []
    for t in range(u_sc.shape[0]):
        total = jnp.zeros((half, LANE), F32)
        for o in range(tap_count):
            moved = u_sc[t, SUB - reach + o : SUB - reach + o + half, :]
            fits = (lowest <= o) & (o < highest)
            total = total + jnp.where(fits, moved, 0.0) * k_sc[t, o : o + 1, :]
        pieces.append(total)
    convolved = jnp.concatenate(pieces, axis=1)[:, 0:features]
    c_out[...] = convolved
    held = convolved * valid
    send_rows(
        stat_out, [row_sum(held), row_sum(held * convolved)], jnp.sum(valid, axis=0, keepdims=True)
    )


def even_odd(ref, half, features):
    even = [ref[t, pl.ds(0, half, stride=2), :] for t in range(ref.shape[0])]
    odd = [ref[t, pl.ds(1, half, stride=2), :] for t in range(ref.shape[0])]
    return (
        jnp.concatenate(even, axis=1)[:, 0:features],
        jnp.concatenate(odd, axis=1)[:, 0:features],
    )


def put_even_odd(ref, even, odd):
    half, features = even.shape
    for t in range(ref.shape[0]):
        stop = min(features, (t + 1) * LANE)
        span = slice(0, stop - t * LANE)
        ref[t, pl.ds(0, half, stride=2), span] = even[:, t * LANE : stop]
        ref[t, pl.ds(1, half, stride=2), span] = odd[:, t * LANE : stop]


def send_rows(out_ref, rows, count=None):
    out_ref[...] = jnp.zeros(out_ref.shape, F32)
    at = 0
    for row in rows:
        for begin in range(0, row.shape[1], LANE):
            stop = min(begin + LANE, row.shape[1])
            out_ref[at : at + 1, 0 : stop - begin] = row[:, begin:stop]
            at += 1
    if count is not None:
        out_ref[at : at + 1, :] = jnp.broadcast_to(count, (1, LANE))


def gather_rows(refs, features):
    total = functools.reduce(jnp.add, [ref[...] for ref in refs])
    tiles = up(features, LANE) // LANE
    rows = []
    for at in range(2):
        pieces = [total[at * tiles + t : at * tiles + t + 1, :] for t in range(tiles)]
        rows.append(jnp.concatenate(pieces, axis=1)[:, 0:features])
    return rows[0], rows[1], total[2 * tiles : 2 * tiles + 1, 0:1]


def batch_moments(stat_refs, features):
    first, second, count = gather_rows(stat_refs, features)
    centre = first / count
    return count, centre, lax.rsqrt(second / count - centre * centre + EPSILON)


def feed_back(grad, hid_slope, w_in, w_out):
    grad_low = low(grad)
    inner = low(dot(grad_low, w_out) * hid_slope.astype(F32))
    return grad_low, inner, dot_cols(inner, w_in)


def second_layer(
    parts,
    lens_ref,
    *refs,
):
    second_layer_body(lens_ref, refs[0:parts], *refs[parts:])


def second_layer_body(
    lens_ref,
    stat_refs,
    c_ref,
    red_ref,
    bias_own,
    gain_own,
    shift_own,
    bias_recv,
    gain_recv,
    shift_recv,
    win_own,
    win_recv,
    wout_own,
    wout_recv,
    point_ref,
    vec2_ref,
    gain_ref,
    own_ref,
    recv_ref,
    g_out,
    dch_out,
    ch_out,
    dr3_out,
    sums_out,
    t2_out,
    h3_out,
    grad_out,
    inner_out,
    hid_out,
    active_out,
    vec_out,
    win,
    wout,
    t_sc,
    slope_sc,
):
    core = lax.axis_index("section")
    first = core == 0
    frames, features = g_out.shape
    half = frames // 2
    choose(first, win_recv, win_own, win)
    choose(first, wout_recv, wout_own, wout)
    ends = bounds_of(lens_ref, core)
    inside = jnp.where(iota((frames, 1), 0) < ends[-1], 1.0, 0.0)
    small = (bias_own, gain_own, shift_own, bias_recv, gain_recv, shift_recv)
    bias, gains, shifts = layer_vectors(small, jnp.logical_not(first))
    count, centre, rho = batch_moments(stat_refs, features)
    ch = (c_ref[...] - centre) * rho
    bnv = ch * gain_ref[...] + vec2_ref[3:4]
    logistic = jax.nn.sigmoid(bnv)
    active = low(bnv * logistic)
    active_slope = logistic * (1.0 + bnv * (1.0 - logistic))
    branch = dot(active, point_ref[...]) + vec2_ref[2:3]
    n3, inv3 = normalise(red_ref[...].astype(F32) + branch)
    h3 = n3 * gains[0:1] + shifts[0:1]
    fed = feed_forward(h3, bias, win[...], wout[...], shifts[2:3], hid_out, slope_sc)
    n4, inv4 = normalise(h3 + fed)
    t2 = n4 * gains[1:2] + shifts[1:2]
    t2_out[...] = n4 * gains[1:2] + shifts[1:2]
    grad = jnp.where(first, recv_ref[0, :, 0, :], own_ref[0, :, 1, :]).astype(F32).T * inside
    g_out[...] = low(grad)
    put_tiles(t_sc, 0, grad)
    even, odd = even_odd(t_sc, half, features)
    dt2 = even + odd
    dv4 = normalise_back(dt2, n4, inv4, gains[1:2])
    grad_low, inner, back = feed_back(dv4, slope_sc[...], win[...], wout[...])
    dh3 = dv4 + back
    dr3 = normalise_back(dh3, n3, inv3, gains[0:1])
    dr3_out[...] = dr3
    dpw = low(dr3)
    dbn = dot_cols(dpw, point_ref[...]) * active_slope
    dch = dbn * gain_ref[...]
    dch_out[...] = dch
    ch_out[...] = ch
    send_rows(sums_out, [row_sum(dch), row_sum(dch * ch)])
    h3_out[...] = low(h3)
    grad_out[...] = grad_low
    inner_out[...] = inner
    active_out[...] = active
    sums = (dh3 * n3, dt2 * n4, dh3, dt2, grad_low, dpw, dbn, dbn * ch)
    vec_out[...] = jnp.zeros(vec_out.shape, F32)
    for at, values in enumerate(sums):
        vec_out[at : at + 1, :] = row_sum(values)


def second_weights(
    lens_ref,
    h3_ref,
    grad_ref,
    inner_ref,
    hid_ref,
    active_ref,
    dr3_ref,
    vec_ref,
    t2_ref,
    n2_ref,
    bias_own,
    gain_own,
    shift_own,
    bias_recv,
    gain_recv,
    shift_recv,
    y_out,
    keep_out,
    send_out,
    pack_sc,
    y_sc,
    stage,
    vec_sc,
):
    core = lax.axis_index("section")
    frames, features = n2_ref.shape
    inner = inner_ref[...]
    pack = Pack(pack_sc, stage, vec_sc)
    pack.matrix(dot_rows(h3_ref[...], inner))
    pack.matrix(dot_rows(grad_ref[...], hid_ref[...]))
    pack.matrix(dot_rows(active_ref[...], low(dr3_ref[...])))
    pack.vector(0, row_sum(inner))
    pack.vector(1, vec_ref[...])
    pack.finish(core, keep_out, send_out)
    ends = bounds_of(lens_ref, core)
    inside = jnp.where(iota((frames, 1), 0) < ends[-1], 1.0, 0.0)
    small = (bias_own, gain_own, shift_own, bias_recv, gain_recv, shift_recv)
    bias, gains, shifts = layer_vectors(small, core == 0)
    skip = low((n2_ref[...] * gains[1:2] + shifts[1:2]) * inside).astype(F32)
    put_even_odd(y_sc, t2_ref[...], t2_ref[...])
    y_out[...] = (get_tiles(y_sc, features) + skip) * inside


def convolution_back(
    parts,
    after,
    lens_ref,
    *refs,
):
    convolution_back_body(
        lens_ref, refs[0:parts], refs[parts : 2 * parts], *refs[2 * parts + after :]
    )


def convolution_back_body(
    lens_ref,
    stat_refs,
    sums_refs,
    dch_ref,
    ch_ref,
    dr3_ref,
    u_ref,
    lin_ref,
    sg_ref,
    red_ref,
    ml_ref,
    n2_ref,
    bias_own,
    gain_own,
    shift_own,
    bias_recv,
    gain_recv,
    shift_recv,
    taps_ref,
    proj_ref,
    glu_ref,
    conv_ref,
    g_ref,
    dt_out,
    mats_out,
    vec_out,
    kd_out,
    t_sc,
    u_sc,
    d_sc,
    k_sc,
    gate_sc,
):
    first = lax.axis_index("section") == 0
    frames, features = n2_ref.shape
    half = frames // 2
    ends = bounds_of(lens_ref, lax.axis_index("section"))
    inside = jnp.where(iota((frames, 1), 0) < ends[-1], 1.0, 0.0)
    joined, valid = half_masks(half, ends)
    small = (bias_own, gain_own, shift_own, bias_recv, gain_recv, shift_recv)
    bias, gains, shifts = layer_vectors(small, first)
    count, centre, rho = batch_moments(stat_refs, features)
    sum1, sum2, _ = gather_rows(sums_refs, features)
    dc = (rho * valid) * (dch_ref[...] - sum1 / count - ch_ref[...] * (sum2 / count))
    tap_count = conv_ref.shape[0]
    reach = tap_count // 2
    lowest, highest = tap_ranges(half, ends, reach)
    u_sc[...] = jnp.zeros(u_sc.shape, F32)
    d_sc[...] = jnp.zeros(d_sc.shape, F32)
    k_sc[...] = jnp.zeros(k_sc.shape, F32)
    kd_out[...] = jnp.zeros(kd_out.shape, F32)
    vec_out[...] = jnp.zeros(vec_out.shape, F32)
    put_tiles(u_sc, SUB, u_ref[...])
    put_tiles(d_sc, SUB, dc)
    put_tiles(k_sc, 0, conv_ref[...])
    pieces = []
    for t in range(u_sc.shape[0]):
        total = jnp.zeros((half, LANE), F32)
        here = d_sc[t, SUB : SUB + half, :]
        for o in range(tap_count):
            span = slice(SUB - reach + o, SUB - reach + o + half)
            fits = (lowest <= o) & (o < highest)
            back = tap_count - 1 - o
            total = total + jnp.where(fits, d_sc[t, span, :], 0.0) * k_sc[t, back : back + 1, :]
            kd_out[t, o : o + 1, :] = row_sum(jnp.where(fits, u_sc[t, span, :], 0.0) * here)
        pieces.append(total)
    du = jnp.concatenate(pieces, axis=1)[:, 0:features]
    logistic = sg_ref[...]
    dlin = low(du * logistic)
    dgat = low(du * lin_ref[...] * logistic * (1.0 - logistic))
    reduced = red_ref[...]
    gate_sc[:, 0:features] = dlin.astype(F32)
    gate_sc[:, features:] = dgat.astype(F32)
    dred = low(dot(low(gate_sc[...]), glu_ref[...]) + dr3_ref[...])
    at = 2 * vec_out.shape[1] % LANE
    for grads in (dot_rows(dlin, reduced), dot_rows(dgat, reduced), dot_rows(ml_ref[...], dred)):
        mats_out[0:features, at : at + features] = grads
        at += features
    for row, values in ((9, dlin), (10, dgat), (11, dred)):
        vec_out[row : row + 1, 0:features] = row_sum(values)
    dm = dot_cols(dred, proj_ref[...])
    n2 = n2_ref[...]
    put_tiles(t_sc, 0, (n2 * gains[1:2] + shifts[1:2]) * inside)
    even, odd = even_odd(t_sc, half, features)
    vec_out[6:7, 0:features] = row_sum(pltpu.roll(odd, 1, 0) * joined * dm)
    vec_out[7:8, 0:features] = row_sum(even * dm)
    vec_out[8:9, 0:features] = row_sum(odd * dm)
    carried = pltpu.roll(taps_ref[0:1] * joined * dm, half - 1, 0)
    put_even_odd(t_sc, taps_ref[1:2] * dm, taps_ref[2:3] * dm + carried)
    dt_out[...] = (g_ref[...].astype(F32) + get_tiles(t_sc, features)) * inside

def first_layer_back(
    dt_ref,
    mats_ref,
    vec_ref,
    kd_ref,
    n2_ref,
    inv2_ref,
    n1_ref,
    inv1_ref,
    hid_ref,
    slope_ref,
    bias_own,
    gain_own,
    shift_own,
    bias_recv,
    gain_recv,
    shift_recv,
    win_own,
    win_recv,
    wout_own,
    wout_recv,
    after_ref,
    dr1_out,
    keep_out,
    send_out,
    pack_sc,
    win,
    wout,
    stage,
    vec_sc,
):
    core = lax.axis_index("section")
    first = core == 0
    choose(first, win_own, win_recv, win)
    choose(first, wout_own, wout_recv, wout)
    small = (bias_own, gain_own, shift_own, bias_recv, gain_recv, shift_recv)
    bias, gains, shifts = layer_vectors(small, first)
    pack = Pack(pack_sc, stage, vec_sc)
    vec_sc[:, 0 : vec_ref.shape[1]] = vec_ref[...]
    features, begin = win.shape[0], 2 * win.shape[1] // LANE * LANE
    stage[0:features, begin:] = mats_ref[0:features, :]
    dt = dt_ref[...]
    n2 = n2_ref[...]
    dv2 = normalise_back(dt, n2, inv2_ref[...], gains[1:2])
    pack.vector(2, row_sum(dt * n2))
    pack.vector(4, row_sum(dt))
    n1 = n1_ref[...]
    h1 = low(n1 * gains[0:1] + shifts[0:1])
    grad_low, inner, back = feed_back(dv2, slope_ref[...], win[...], wout[...])
    dh1 = dv2 + back
    pack.matrix(dot_rows(h1, inner))
    pack.matrix(dot_rows(grad_low, hid_ref[...]))
    pack.vector(0, row_sum(inner))
    pack.vector(5, row_sum(grad_low))
    pack.vector(1, row_sum(dh1 * n1))
    pack.vector(3, row_sum(dh1))
    dr1_out[...] = normalise_back(dh1, n1, inv1_ref[...], gains[0:1])
    pack.used = 2 * win.shape[1] + 3 * features
    pack.finish(core, keep_out, send_out, [kd_ref[t] for t in range(kd_ref.shape[0])])


def attention_back(
    dr1_ref,
    qu_ref,
    qw_ref,
    k_ref,
    v_ref,
    p_ref,
    a_ref,
    wo_ref,
    *refs,
):
    dq_out, dkv_out, dp_out, sums_out, do_sc, qwr_sc, dqr_sc = refs[-7:]
    frames, features = dr1_ref.shape
    head = features // HEADS
    width = HEADS * LANE
    scale = head**-0.5
    do_sc[...] = low(dot_cols(low(dr1_ref[...]), wo_ref[...]))
    flip = jnp.where(
        iota((frames, frames), 0) + iota((frames, frames), 1) == frames - 1, 1.0, 0.0
    ).astype(BF16)
    qwr_sc[...] = low(dot(flip, qw_ref[...]))
    for h in range(HEADS):
        cols = slice(h * LANE, (h + 1) * LANE)
        weights = a_ref[h]
        grad = do_sc[:, cols]
        weights_f = weights.astype(F32)
        product = weights_f * dot_cols(grad, v_ref[:, cols])
        ds = low(product - weights_f * jnp.sum(product, axis=-1, keepdims=True))
        dkv_out[:, width + h * LANE : width + (h + 1) * LANE] = low(dot_rows(weights, grad))
        dkv_out[:, cols] = low(scale * dot_rows(ds, qu_ref[:, cols]))
        dsr = low(dot(flip, ds))
        wide = jnp.concatenate([jnp.zeros((frames, frames), BF16), dsr], axis=1)
        band = pltpu.roll(wide.astype(F32), frames + 1, 1, stride=1, stride_axis=0).astype(BF16)
        dqu = scale * dot(dsr, k_ref[:, cols])
        dqw = scale * dot(band, p_ref[:, cols])
        dqr_sc[:, cols] = low(dqu + dqw)
        dp_out[:, cols] = low(scale * dot_rows(band, qwr_sc[:, cols]))
        sums_out[2:3, cols] = row_sum(dqu)
        sums_out[3:4, cols] = row_sum(dqw)
    dq = low(dot(flip, dqr_sc[...]))
    dq_out[...] = dq
    sums_out[0:1, :] = row_sum(dq)
    sums_out[1:2, :] = row_sum(dkv_out[:, width:])


def attention_weights_back(
    dr1_ref,
    xt_ref,
    o_ref,
    table_ref,
    dq_ref,
    dkv_ref,
    dp_ref,
    sums_ref,
    *refs,
):
    keep_out, send_out, pack_sc, stage, vec_sc = refs[-5:]
    core = lax.axis_index("section")
    frames, features = dr1_ref.shape
    width = HEADS * LANE
    pack = Pack(pack_sc, stage, vec_sc)
    dr1_low = low(dr1_ref[...])
    unselect = head_unselect(features, features // HEADS)
    pack.vector(2, row_sum(dr1_low))
    pack.matrix(dot_rows(unselect, low(dot_rows(o_ref[...], dr1_low))))
    sums = dot(sums_ref[0:4, :], unselect.astype(F32), precision=lax.Precision.HIGHEST)
    pack.vector(0, sums[0:2])
    pack.vector(3, sums[2:4])
    x_turned = xt_ref[...]
    pack.matrix(dot(low(dot(x_turned, dq_ref[...])), unselect))
    pack.matrix(dot(low(dot(x_turned, dkv_ref[:, 0:width])), unselect))
    pack.matrix(dot(low(dot(x_turned, dkv_ref[:, width:])), unselect))
    pack.matrix(dot(low(dot_rows(table_ref[...], dp_ref[...])), unselect))
    pack.finish(core, keep_out, send_out)


def input_back(dr1_ref, dq_ref, dkv_ref, w_ref, y_ref, after_ref, rows_out, cross_out):
    core = lax.axis_index("section")
    width = dq_ref.shape[1]
    dx = dr1_ref[...] + dot_cols(dq_ref[...], w_ref[:, 0:width])
    dx = (dx + dot_cols(dkv_ref[...], w_ref[:, width:])).T
    y = y_ref[...].T
    rows_out[...] = jnp.where(core == 0, dx, y)
    cross_out[...] = jnp.where(core == 0, y, dx)


def digit(bit, core):
    place = jnp.where(core == 0, bit, 1 - bit) if bit < 2 else bit
    return (lax.axis_index("rows") >> place) & 1


def partner(values, bit):
    peers = lax.axis_size("rows")
    pairs = []
    for core in range(2):
        place = 1 - bit if bit < 2 and core == 1 else bit
        pairs += [(core * peers + r, core * peers + (r ^ (1 << place))) for r in range(peers)]
    return lax.ppermute(values, ("section", "rows"), pairs)


def step_kernel(bit, join, count, *refs):
    parts = refs[:count]
    if bit is not None:
        keep_out, send_out = refs[-2:]
        rows = keep_out.shape[0]
        mine = digit(bit, lax.axis_index("section"))
        for which, out in ((mine, keep_out), (1 - mine, send_out)):
            span = pl.ds(pl.multiple_of(which * rows, SUB), rows)
            out[...] = low(sum(part[span, :].astype(F32) for part in parts))
    elif join:
        rows = parts[0].shape[0]
        for at, part in enumerate(parts):
            refs[-1][at * rows : (at + 1) * rows, :] = part[...]
    else:
        refs[-1][...] = low(sum(part[...].astype(F32) for part in parts))


def step(parts, after, name, bit=None, join=False):
    rows = parts[0].shape[0]
    if bit is not None:
        outs = [shape((rows // 2, LANE), BF16)] * 2
    else:
        outs = [shape((rows * (len(parts) if join else 1), LANE), BF16)]
    return call(
        functools.partial(step_kernel, bit, join, len(parts)),
        name,
        [VMEM] * len(parts) + [ANY] * len(after),
        outs,
        limit=STEP_LIMIT,
    )(*parts, *after)


class Chain:
    def __init__(self, name, keep, send):
        self.name = name
        self.parts = [keep, swap(send)]
        last = lax.axis_size("rows").bit_length() - 2
        self.plan = [("halve", bit) for bit in range(last)]
        self.plan += [("whole", last)]
        self.plan += [("whole" if bit == last - 1 else "join", bit) for bit in reversed(range(last))]
        self.plan.append(("last", None))

    def advance(self, after=()):
        kind, bit = self.plan.pop(0)
        name = f"{self.name}_{kind}_{bit}"
        if kind == "last":
            (send,) = step(self.parts[1:], after, name)
            self.pieces = [self.parts[0], send, self.early, swap(send)]
            return send
        if kind == "halve":
            keep, send = step(self.parts, after, name, bit=bit)
        else:
            (keep,) = step(self.parts, after, name, join=kind == "join")
            send = keep
        self.parts = [keep, partner(send, bit)]
        if len(self.plan) == 1:
            self.early = swap(keep)
        return send


def reorder(pieces, target):
    core = lax.axis_index("section")
    bits = lax.axis_size("rows").bit_length() - 2
    half = target.shape[0] // 2
    block = half >> bits
    each = 1 << (bits - 1)
    for side in range(2):
        owner = core if side == 0 else 1 - core
        mine = jnp.int32(0)
        for bit in range(bits):
            mine = (mine << 1) | digit(bit, owner)
        for at in range(1 << bits):
            first = at % each * block
            begin = pl.multiple_of(owner * half + (mine ^ at) * block, SUB)
            target[pl.ds(begin, block), :] = pieces[2 * side + at // each][first : first + block, :]


def spread_tiles(pack, stage):
    high = stage.shape[0]
    for t in range(stage.shape[1] // LANE):
        stage[:, t * LANE : (t + 1) * LANE] = pack[t * high : (t + 1) * high, :].astype(F32)
    return stage.shape[1] // LANE * high


def vectors_at(ref, row, count, rows):
    pieces = [ref[row + t * rows : row + (t + 1) * rows, :] for t in range(count)]
    return jnp.concatenate(pieces, axis=1).astype(F32)


def unpack_one(
    piece0,
    piece1,
    piece2,
    piece3,
    after_ref,
    point_out,
    win_out,
    wout_out,
    vec_out,
    pack,
    stage,
):
    reorder((piece0, piece1, piece2, piece3), pack)
    at = spread_tiles(pack, stage)
    features = point_out.shape[0]
    inner = win_out.shape[2]
    win_out[:, 0, :] = stage[0:features, 0:inner]
    wout_out[:, 0, :] = stage[0:features, inner : 2 * inner]
    point_out[...] = stage[0:features, 2 * inner : 2 * inner + features]
    vec_out[...] = vectors_at(pack, at, vec_out.shape[1] // LANE, SUB)


def unpack_two(
    win_ref,
    wout_ref,
    vec_ref,
    last_ref,
    piece0,
    piece1,
    piece2,
    piece3,
    vec_out,
    taps_out,
    proj_out,
    glu_out,
    conv_out,
    vec2_out,
    gain_out,
    win_out,
    bias_out,
    wout_out,
    norm_out,
    block_out,
    pack,
    stage,
):
    core = lax.axis_index("section")
    reorder((piece0, piece1, piece2, piece3), pack)
    at = spread_tiles(pack, stage)
    features = proj_out.shape[0]
    inner = win_out.shape[2]

    @pl.when(core == 0)
    def _():
        win_out[:, 0, :] = stage[0:features, 0:inner]
        wout_out[:, 0, :] = stage[0:features, inner : 2 * inner]

    @pl.when(core != 0)
    def _():
        win_out[...] = win_ref[...]
        wout_out[...] = wout_ref[...]

    begin = 2 * inner
    glu_out[0:features, :] = stage[0:features, begin : begin + features]
    glu_out[features:, :] = stage[0:features, begin + features : begin + 2 * features]
    proj_out[...] = stage[0:features, begin + 2 * features : begin + 3 * features]
    taps = conv_out.shape[0]
    tap_rows = up(taps, SUB)
    tiles = up(features, LANE) // LANE
    conv_out[...] = vectors_at(pack, at, tiles, tap_rows)[0:taps, 0:features]
    at += tiles * tap_rows
    rows1 = vec_ref[...]
    rows2 = vectors_at(pack, at, rows1.shape[1] // LANE, SUB)
    vec_out[0:5, :] = last_ref[...]
    vec_out[5:6, :] = rows2[11:12, 0:features]
    taps_out[...] = rows2[6:9, 0:features]
    vec2_out[0:2, :] = rows2[9:11, 0:features]
    vec2_out[2:4, :] = rows1[6:8, 0:features]
    gain_out[...] = rows1[8:9, 0:features]
    mine = jnp.where(core == 0, rows2, rows1)
    bias_out[...] = mine[0:1, 0:inner]
    norm_out[0] = mine[1:3, 0:features]
    for row in range(3):
        block_out[row] = mine[3 + row : 4 + row, 0:features]


def unpack_three(
    piece0,
    piece1,
    piece2,
    piece3,
    attn_in_out,
    pos_out,
    attn_out_out,
    vec_out,
    pack,
    stage,
):
    reorder((piece0, piece1, piece2, piece3), pack)
    at = spread_tiles(pack, stage)
    features = pos_out.shape[0]
    attn_out_out[...] = stage[0:features, 0:features]
    attn_in_out[...] = stage[0:features, features : 4 * features]
    pos_out[...] = stage[0:features, 4 * features : 5 * features]
    tiles = up(features, LANE) // LANE
    vec_out[...] = vectors_at(pack, at, tiles, SUB)[0:5, 0:features]


def join_rows(rows_ref, cross_ref, after_ref, boundary_out, mark_out):
    mark_out[...] = jnp.zeros(mark_out.shape, F32)
    core = lax.axis_index("section")
    rows, cross = rows_ref[...], cross_ref[...]
    boundary_out[0, :, 0, :] = jnp.where(core == 0, rows, cross)
    boundary_out[0, :, 1, :] = jnp.where(core == 0, cross, rows)


def shape(dims, dtype=F32):
    return jax.ShapeDtypeStruct(dims, dtype)


SMEM = pl.BlockSpec(memory_space=pltpu.SMEM)
VMEM = pl.BlockSpec(memory_space=pltpu.VMEM)
ANY = pl.BlockSpec(memory_space=pl.ANY)
HBM = pl.BlockSpec(memory_space=pltpu.HBM)


def call(kernel, name, in_specs, out_shape, scratch=(), limit=None, cost=0):
    return pl.pallas_call(
        kernel,
        name=name,
        in_specs=in_specs,
        out_specs=[VMEM] * len(out_shape),
        out_shape=out_shape,
        scratch_shapes=list(scratch),
        compiler_params=pltpu.CompilerParams(vmem_limit_bytes=limit or VMEM_LIMIT),
        cost_estimate=pl.CostEstimate(flops=0, bytes_accessed=cost, transcendentals=0),
    )


def position_table(frames, features):
    distance = (frames - np.arange(2 * frames)).astype(np.float32)
    frequency = np.exp(
        np.arange(0, features, 2).astype(np.float32) * np.float32(-math.log(10000.0) / features)
    ).astype(np.float32)
    angles = (distance[:, None] * frequency[None, :]).astype(np.float64)
    table = np.stack([np.sin(angles), np.cos(angles)], axis=-1).reshape(2 * frames, features)
    return jnp.asarray(table.astype(np.float32), BF16)


def in_hbm(values):
    return pltpu.with_memory_space_constraint(values, pltpu.HBM)


def swap(values):
    return lax.ppermute(values, "section", [(0, 1), (1, 0)])


def share(values):
    bits = lax.axis_size("rows").bit_length() - 1
    parts = [values]
    for begin in range(0, bits, 2):
        values = functools.reduce(jnp.add, parts)
        parts = [values]
        for step in range(1, 1 << min(2, bits - begin)):
            pairs = [(r, r ^ (step << begin)) for r in range(1 << bits)]
            parts.append(lax.ppermute(values, "rows", pairs))
    return parts, values


def shards(
    boundary,
    utt_lengths,
    attn_in,
    pos_proj,
    attn_out,
    first_vectors,
    reduce_taps,
    reduce_proj,
    glu_in,
    conv_taps,
    second_vectors,
    bn_gain,
    point_proj,
    ffn_in,
    ffn_bias,
    ffn_out,
    norm_gain,
    block_vectors,
):
    peers = lax.axis_size("rows")
    _, batches, frames, features = boundary.shape
    half = frames // 2
    inner = ffn_in.shape[2]
    width = HEADS * LANE
    high = up(features, SUB)
    tiles = up(features, LANE) // LANE
    inner_tiles = up(inner, LANE) // LANE
    tap_rows = up(conv_taps.shape[0], SUB)
    wide = [up(cols, LANE) for cols in (2 * inner + features, 2 * inner + 3 * features, 5 * features)]
    extra = [SUB * inner_tiles, SUB * inner_tiles + tap_rows * tiles, SUB * tiles]
    pack_rows = [up(high * (w // LANE) + e, peers * SUB) for w, e in zip(wide, extra)]
    table = position_table(frames, features)
    turned = jnp.transpose(boundary, (0, 3, 1, 2))
    wout_own = jnp.transpose(ffn_out, (0, 2, 1))
    shift_own = jnp.transpose(block_vectors, (1, 0, 2))
    glu_turned = glu_in.T

    recv = swap(turned)
    small = (ffn_bias, norm_gain, shift_own) + tuple(
        swap(values) for values in (ffn_bias, norm_gain, shift_own)
    )
    weights = (ffn_in, swap(ffn_in), wout_own, swap(wout_own))

    def scratch(*dims, dtype=F32):
        return pltpu.VMEM(dims, dtype)

    p, w_pad, wo_pad, vectors = call(
        prepare,
        "prepare",
        [HBM] * 5,
        [
            shape((2 * frames, width), BF16),
            shape((features, 3 * width), BF16),
            shape((width, features), BF16),
            shape((first_vectors.shape[0], width)),
        ],
        [
            scratch(*attn_in.shape, dtype=BF16),
            scratch(*pos_proj.shape, dtype=BF16),
            scratch(*attn_out.shape, dtype=BF16),
            scratch(*first_vectors.shape),
            scratch(*table.shape, dtype=BF16),
            pltpu.SemaphoreType.DMA((5,)),
        ],
        cost=10**7,
    )(*map(in_hbm, (attn_in, pos_proj, attn_out, first_vectors, table)))
    xt, qu, qw, k, v, a, o, n1, inv1 = call(
        attention_forward,
        "attention_forward",
        [SMEM] + [VMEM] * 7,
        [
            shape((features, frames), BF16),
            shape((frames, width), BF16),
            shape((frames, width), BF16),
            shape((frames, width), BF16),
            shape((frames, width), BF16),
            shape((HEADS, frames, frames), BF16),
            shape((frames, width), BF16),
            shape((frames, features)),
            shape((frames, 1)),
        ],
    )(
        in_hbm(utt_lengths),
        in_hbm(turned),
        recv,
        p,
        w_pad,
        wo_pad,
        vectors,
        in_hbm(first_vectors),
    )

    weights_scratch = [scratch(features, inner, dtype=BF16)] * 2
    rows_scratch = scratch(tiles, frames, LANE)
    edge_scratch = scratch(tiles, half + 2 * SUB, LANE)
    taps_scratch = scratch(tiles, tap_rows, LANE)
    vec_scratch = scratch(SUB, inner_tiles * LANE)

    def pack_scratch(index):
        return scratch(pack_rows[index], LANE, dtype=BF16)

    def stage_scratch(index):
        return scratch(high, wide[index])

    def pack_halves(index):
        return [shape((pack_rows[index] // 2, LANE), BF16)] * 2

    hid, slope, n2, inv2, ml, red, lin, sg, u, c, stat = call(
        convolution_forward,
        "convolution_forward",
        [SMEM] + [VMEM] * 17,
        [
            shape((frames, inner), BF16),
            shape((frames, inner), BF16),
            shape((frames, features)),
            shape((frames, 1)),
            shape((half, features), BF16),
            shape((half, features), BF16),
            shape((half, features)),
            shape((half, features)),
            shape((half, features)),
            shape((half, features)),
            shape((8, LANE)),
        ],
        weights_scratch + [rows_scratch, edge_scratch, taps_scratch],
    )(
        utt_lengths,
        n1,
        *small,
        *weights,
        first_vectors,
        reduce_taps,
        reduce_proj,
        glu_turned,
        conv_taps,
        second_vectors,
    )
    stat, _ = share(stat)
    g, dch, ch, dr3, sums, t2, h3, grad4, inner4, hid4, active, vec1 = call(
        functools.partial(second_layer, len(stat)),
        "second_layer",
        [SMEM] + [VMEM] * (17 + len(stat)),
        [
            shape((frames, features), BF16),
            shape((half, features)),
            shape((half, features)),
            shape((half, features)),
            shape((8, LANE)),
            shape((half, features)),
            shape((half, features), BF16),
            shape((half, features), BF16),
            shape((half, inner), BF16),
            shape((half, inner), BF16),
            shape((half, features), BF16),
            shape((8, features)),
        ],
        weights_scratch + [rows_scratch, scratch(half, inner, dtype=BF16)],
    )(
        utt_lengths,
        *stat,
        c,
        red,
        *small,
        *weights,
        point_proj,
        second_vectors,
        bn_gain[None],
        turned,
        recv,
    )
    sums, sent = share(sums)
    y, keep1, send1 = call(
        second_weights,
        "second_weights",
        [SMEM] + [VMEM] * 15,
        [shape((frames, features))] + pack_halves(0),
        [pack_scratch(0), rows_scratch, stage_scratch(0), vec_scratch],
    )(utt_lengths, h3, grad4, inner4, hid4, active, dr3, vec1, t2, n2, *small)
    one = Chain("one", keep1, send1)
    mark = one.advance([sent])
    dt, mats, vec2, kd = call(
        functools.partial(convolution_back, len(stat), 1),
        "convolution_back",
        [SMEM] + [VMEM] * (2 * len(stat)) + [ANY] + [VMEM] * 20,
        [
            shape((frames, features)),
            shape((high, wide[1] - 2 * inner // LANE * LANE)),
            shape((SUB, inner)),
            shape((tiles, tap_rows, LANE)),
        ],
        [
            rows_scratch,
            edge_scratch,
            edge_scratch,
            taps_scratch,
            scratch(half, 2 * features),
        ],
    )(
        utt_lengths,
        *stat,
        *sums,
        mark,
        dch,
        ch,
        dr3,
        u,
        lin,
        sg,
        red,
        ml,
        n2,
        *small,
        reduce_taps,
        reduce_proj,
        glu_turned,
        conv_taps,
        g,
    )
    mark = one.advance([dt])
    dr1, keep2, send2 = call(
        first_layer_back,
        "first_layer_back",
        [VMEM] * 20 + [ANY],
        [shape((frames, features))] + pack_halves(1),
        [pack_scratch(1)] + weights_scratch + [stage_scratch(1), vec_scratch],
    )(dt, mats, vec2, kd, n2, inv2, n1, inv1, hid, slope, *small, *weights, mark)
    two = Chain("two", keep2, send2)
    mark = two.advance([dr1])
    dq, dkv, dp, head_sums = call(
        attention_back,
        "attention_back",
        [VMEM] * 8 + [ANY],
        [
            shape((frames, width), BF16),
            shape((frames, 2 * width), BF16),
            shape((2 * frames, width), BF16),
            shape((8, width)),
        ],
        [scratch(frames, width, dtype=BF16)] * 3,
    )(dr1, qu, qw, k, v, p, a, wo_pad, mark)
    mark = one.advance([dq])
    keep3, send3 = call(
        attention_weights_back,
        "attention_weights_back",
        [VMEM] * 8 + [ANY],
        pack_halves(2),
        [pack_scratch(2), stage_scratch(2), scratch(SUB, tiles * LANE)],
    )(dr1, xt, o, table, dq, dkv, dp, head_sums, mark)
    three = Chain("three", keep3, send3)
    mark = two.advance([keep3])
    rows, cross = call(
        input_back,
        "input_back",
        [VMEM] * 5 + [ANY],
        [shape((features, frames))] * 2,
    )(dr1, dq, dkv, w_pad, y, mark)
    mark = rows
    crossed = swap(cross)
    opened = joined = False
    while two.plan or three.plan or one.plan:
        for chain in (three, one, two):
            if chain.plan:
                mark = chain.advance([mark])
            elif chain is one and not opened:
                opened = True
                point_out, win_one, wout_one, vec_one = call(
                    unpack_one,
                    "unpack_one",
                    [VMEM] * 4 + [ANY],
                    [
                        shape(point_proj.shape),
                        shape((features, 1, inner)),
                        shape((features, 1, inner)),
                        shape((SUB, inner_tiles * LANE)),
                    ],
                    [pack_scratch(0), stage_scratch(0)],
                )(*one.pieces, mark)
                mark = vec_one
            elif chain is one and not joined:
                joined = True
                boundary_out, mark = call(
                    join_rows,
                    "join_rows",
                    [VMEM] * 2 + [ANY],
                    [shape((1, features, batches, frames)), shape((8, LANE))],
                )(rows, crossed, mark)
    attn_in_out, pos_out, attn_out_out, vec_three = call(
        unpack_three,
        "unpack_three",
        [VMEM] * 4,
        [
            shape(attn_in.shape),
            shape(pos_proj.shape),
            shape(attn_out.shape),
            shape((first_vectors.shape[0] - 1, features)),
        ],
        [pack_scratch(2), stage_scratch(2)],
    )(*three.pieces)
    (
        vec_out,
        taps_out,
        proj_out,
        glu_out,
        conv_out,
        vec2_out,
        gain_out,
        win_out,
        bias_out,
        wout_out,
        norm_out,
        block_out,
    ) = call(
        unpack_two,
        "unpack_two",
        [VMEM] * 8,
        [
            shape(first_vectors.shape),
            shape(reduce_taps.shape),
            shape(reduce_proj.shape),
            shape(glu_turned.shape),
            shape(conv_taps.shape),
            shape(second_vectors.shape),
            shape((1, features)),
            shape((features, 1, inner)),
            shape(ffn_bias.shape),
            shape((features, 1, inner)),
            shape(norm_gain.shape),
            shape(shift_own.shape),
        ],
        [pack_scratch(1), stage_scratch(1)],
    )(win_one, wout_one, vec_one, vec_three, *two.pieces)
    return (
        jnp.transpose(boundary_out, (0, 2, 3, 1)),
        attn_in_out,
        pos_out,
        attn_out_out,
        vec_out,
        taps_out,
        proj_out,
        glu_out.T,
        conv_out,
        vec2_out,
        gain_out[0],
        point_out,
        jnp.transpose(win_out, (1, 0, 2)),
        bias_out,
        jnp.transpose(wout_out, (1, 2, 0)),
        norm_out,
        jnp.transpose(block_out, (1, 0, 2)),
    )


def solution(mesh):
    split = (
        P("section", None, None),
        P("section", None),
        P("section", None, None),
        P("section", None, None),
        P("section", None, None),
    )
    return jax.shard_map(
        shards,
        mesh=mesh,
        in_specs=(P("section", None, "rows", None), P(None, "rows", None)) + (P(),) * 11 + split,
        out_specs=(P("section", None, "rows", None),) + (P(),) * 11 + split,
        check_vma=False,
    )
```

```python
import functools
import math

import jax
import jax.numpy as jnp
import numpy as np
from jax import lax
from jax.experimental import pallas as pl
from jax.experimental.pallas import tpu as pltpu
from jax.sharding import PartitionSpec as P

HEADS = 4
LANE = 128
SUB = 16
BLOCK = 64
EPSILON = 1e-05
MASKED = -1e30
F32 = jnp.float32
BF16 = jnp.bfloat16
VMEM_LIMIT = 28 << 20
STEP_LIMIT = 8 << 20
STEP_COST = 12 * 10**6
KERNEL_COST = 12 * 10**6
ORDER = "KE1F2AB1C2D1321321J321321321323UV3W"


def up(value, step):
    return -(-value // step) * step


def low(values):
    return values.astype(BF16)


def dot(left, right, dims=((1,), (0,)), precision=None):
    return lax.dot_general(
        left, right, (dims, ((), ())), preferred_element_type=F32, precision=precision
    )


def dot_rows(left, right):
    return dot(left, right, ((0,), (0,)))


def dot_cols(left, right):
    return dot(left, right, ((1,), (1,)))


def row_sum(values):
    return jnp.sum(values.astype(F32), axis=0, keepdims=True)


def normalise(values):
    centre = values - jnp.mean(values, axis=-1, keepdims=True)
    inverse = lax.rsqrt(jnp.mean(centre * centre, axis=-1, keepdims=True) + EPSILON)
    return centre * inverse, inverse


def normalise_back(grad, normed, inverse, gain):
    scaled = grad * gain
    first = jnp.mean(scaled, axis=-1, keepdims=True)
    second = jnp.mean(scaled * normed, axis=-1, keepdims=True)
    return inverse * (scaled - first - normed * second)


def bounds_of(lens_ref, batch):
    ends = []
    total = jnp.int32(0)
    for slot in range(lens_ref.shape[-1]):
        total = total + lens_ref[batch, 0, slot]
        ends.append(total)
    return ends


def segment_of(position, ends):
    segment = jnp.zeros(position.shape, jnp.int32)
    for end in ends:
        segment = segment + (position >= end).astype(jnp.int32)
    return segment


def iota(shape, axis):
    return lax.broadcasted_iota(jnp.int32, shape, axis)


def head_select(rows, base, head, dtype):
    row = iota((rows, HEADS * LANE), 0) + base
    col = iota((rows, HEADS * LANE), 1)
    within = col % LANE
    hit = (row == (col // LANE) * head + within) & (within < head)
    return jnp.where(hit, 1.0, 0.0).astype(dtype)


def head_unselect(cols, head):
    row = iota((HEADS * LANE, cols), 0)
    col = iota((HEADS * LANE, cols), 1)
    within = row % LANE
    hit = (col == (row // LANE) * head + within) & (within < head)
    return jnp.where(hit, 1.0, 0.0).astype(BF16)


def choose(use_own, own_ref, other_ref, target):
    @pl.when(use_own)
    def _():
        target[...] = own_ref[0]

    @pl.when(jnp.logical_not(use_own))
    def _():
        target[...] = other_ref[0]


def pack_heights(features, cols, bias_cols, others):
    tall = features // SUB * SUB
    tiles = up(cols, LANE) // LANE
    rest = up((features - tall) * tiles, SUB)
    vectors = up(features, LANE) // LANE * SUB + (SUB if bias_cols else 0)
    return tall, rest, tall * tiles + rest + others + vectors


class Pack:
    def __init__(self, stage_ref, rest_ref, vec_ref):
        self.stage, self.rest, self.vec = stage_ref, rest_ref, vec_ref
        self.col = 0
        self.used = 0
        self.bias = None

    def matrix(self, values):
        rows, cols = values.shape
        self.stage[0:rows, self.col : self.col + cols] = values
        self.col += cols
        self.used = max(self.used, self.col)

    def vector(self, at, values):
        self.vec[at : at + values.shape[0], 0 : values.shape[1]] = values

    def finish(self, core, keep_out, send_out, others=()):
        rows, wide = self.stage.shape
        if self.used < wide:
            self.stage[:, self.used : wide] = jnp.zeros((rows, wide - self.used), F32)
        tall = rows // SUB * SUB
        tail = rows - tall
        self.rest[...] = jnp.zeros(self.rest.shape, F32)
        for t in range(wide // LANE):
            part = self.stage[tall:rows, t * LANE : (t + 1) * LANE]
            self.rest[t * tail : (t + 1) * tail, :] = part
        blocks = [lambda t=t: self.stage[0:tall, t * LANE : (t + 1) * LANE] for t in range(wide // LANE)]
        blocks += [lambda: self.rest[...]] + [lambda values=values: values for values in others]
        for t in range(self.vec.shape[1] // LANE):
            blocks.append(lambda t=t: self.vec[:, t * LANE : (t + 1) * LANE])
        if self.bias is not None:
            cols = self.bias.shape[1]
            lines = [self.bias[:, at : at + LANE] for at in range(0, cols, LANE)]
            lines[-1] = jnp.pad(lines[-1], ((0, 0), (0, LANE - lines[-1].shape[1])))
            lines.append(jnp.zeros((SUB - len(lines), LANE), F32))
            blocks.append(lambda: jnp.concatenate(lines, axis=0))

        @pl.when(core == 0)
        def _():
            self.place(keep_out, send_out, blocks)

        @pl.when(core != 0)
        def _():
            self.place(send_out, keep_out, blocks)

    def place(self, low_out, high_out, blocks):
        half = low_out.shape[0]
        row = 0

        def put(values):
            nonlocal row
            rows = values.shape[0]
            cut = min(max(half - row, 0), rows)
            if cut:
                low_out[row : row + cut, :] = low(values[0:cut])
            if cut < rows:
                high_out[row + cut - half : row + rows - half, :] = low(values[cut:])
            row += rows

        for block in blocks:
            put(block())
        if row < 2 * half:
            put(jnp.zeros((2 * half - row, LANE), F32))


def prepare(
    attn_in_hbm,
    pos_proj_hbm,
    attn_out_hbm,
    vec_hbm,
    table_hbm,
    bias_hbm,
    gain_hbm,
    shift_hbm,
    p_out,
    w_out,
    wo_out,
    vectors_out,
    small_out,
    attn_in_ref,
    pos_proj_ref,
    attn_out_ref,
    vec_ref,
    table_ref,
    bias_ref,
    gain_ref,
    shift_ref,
    sem,
):
    sources = (pos_proj_hbm, table_hbm, attn_in_hbm, attn_out_hbm, vec_hbm)
    sources += (bias_hbm, gain_hbm, shift_hbm)
    targets = (pos_proj_ref, table_ref, attn_in_ref, attn_out_ref, vec_ref)
    targets += (bias_ref, gain_ref, shift_ref)
    copies = [
        pltpu.make_async_copy(source, target, sem.at[at])
        for at, (source, target) in enumerate(zip(sources, targets))
    ]
    for copy in copies:
        copy.start()
    features = attn_out_ref.shape[0]
    head = features // HEADS
    width = HEADS * LANE
    select = head_select(features, 0, head, BF16)
    copies[0].wait()
    pos = low(dot(pos_proj_ref[...], select))
    copies[1].wait()
    p_out[...] = low(dot(table_ref[...], pos))
    copies[2].wait()
    for part in range(3):
        begin = part * features
        floor = begin // LANE * LANE
        stop = min(up(begin + features, LANE), 3 * features)
        piece = attn_in_ref[:, floor:stop]
        chosen = head_select(stop - floor, floor - begin, head, BF16)
        w_out[:, part * width : (part + 1) * width] = low(dot(piece, chosen))
    copies[3].wait()
    wo_out[...] = low(dot(head_unselect(features, head), attn_out_ref[...]))
    copies[4].wait()
    vectors_out[...] = dot(
        vec_ref[...], head_select(features, 0, head, F32), precision=lax.Precision.HIGHEST
    )
    for copy in copies[5:]:
        copy.wait()
    small_out[...] = jnp.zeros(small_out.shape, F32)
    small_out[0:1, :] = bias_ref[...]
    small_out[1:3, 0:features] = gain_ref[0]
    for at in range(3):
        small_out[3 + at : 4 + at, 0:features] = shift_ref[at]


def attention_forward(
    lens_ref,
    own_ref,
    recv_ref,
    p_ref,
    w_ref,
    wo_ref,
    vectors_ref,
    vec_ref,
    xt_out,
    qu_out,
    qw_out,
    k_out,
    v_out,
    a_out,
    o_out,
    n1_out,
    inv1_out,
):
    core = lax.axis_index("section")
    features, frames = xt_out.shape
    head = features // HEADS
    width = HEADS * LANE
    ends = bounds_of(lens_ref, core)
    x_turned = jnp.where(core == 0, own_ref[0, :, 0, :], recv_ref[0, :, 1, :])
    xt_out[...] = x_turned
    x_rows = x_turned.astype(F32).T
    x = low(x_rows)
    vectors = vectors_ref[...]
    q = dot(x, w_ref[:, 0:width]) + vectors[0:1]
    qu_out[...] = low(q + vectors[3:4])
    qw_out[...] = low(q + vectors[4:5])
    k_out[...] = low(dot(x, w_ref[:, width : 2 * width]))
    v_out[...] = low(dot(x, w_ref[:, 2 * width :]) + vectors[1:2])
    same = segment_of(iota((frames, 1), 0), ends) == segment_of(iota((1, frames), 1), ends)
    scale = head**-0.5
    for h in range(HEADS):
        cols = slice(h * LANE, (h + 1) * LANE)
        content = dot_cols(qu_out[:, cols], k_out[:, cols])
        relative = dot_cols(qw_out[:, cols], p_ref[:, cols])
        shifted = pltpu.roll(relative, 0, 1, stride=1, stride_axis=0)[:, frames:]
        scores = jnp.where(same, (content + shifted) * scale, MASKED)
        raised = jnp.exp(scores - jnp.max(scores, axis=-1, keepdims=True))
        weights = low(raised / jnp.sum(raised, axis=-1, keepdims=True))
        a_out[h] = weights
        o_out[:, cols] = low(dot(weights, v_out[:, cols]))
    attended = dot(o_out[...], wo_ref[...]) + vec_ref[2:3, :]
    normed, inverse = normalise(x_rows + attended)
    n1_out[...] = normed
    inv1_out[...] = inverse


def half_masks(half, ends):
    position = 2 * iota((half, 1), 0)
    segment = segment_of(position, ends)
    before = segment_of(position - 1, ends)
    joined = jnp.where((segment == before) & (position > 0), 1.0, 0.0)
    valid = jnp.where(position < ends[-1], 1.0, 0.0)
    return joined, valid


def tap_ranges(half, ends, reach):
    position = iota((half, LANE), 0)
    first = jnp.zeros((half, LANE), jnp.int32)
    last = jnp.full((half, LANE), half, jnp.int32)
    for end in ends:
        edge = end // 2
        first = jnp.where(position >= edge, edge, first)
    for end in reversed(ends):
        edge = end // 2
        last = jnp.where(position < edge, edge, last)
    return first - position + reach, last - position + reach


def put_tiles(ref, at, values):
    rows, cols = values.shape
    for t in range(ref.shape[0]):
        stop = min(cols, (t + 1) * LANE)
        ref[t, at : at + rows, 0 : stop - t * LANE] = values[:, t * LANE : stop]


def get_tiles(ref, cols):
    return jnp.concatenate([ref[t] for t in range(ref.shape[0])], axis=1)[:, 0:cols]


def layer_vectors(own_ref, recv_ref, use_own, features):
    rows = jnp.where(use_own, own_ref[...], recv_ref[...])
    return rows[0:1], rows[1:3, 0:features], rows[3:6, 0:features]


def feed_forward(inputs, bias, w_in, w_out, shift, hid_ref, slope_ref):
    z = dot(low(inputs), w_in) + bias
    logistic = jax.nn.sigmoid(z)
    hid_ref[...] = low(z * logistic)
    slope_ref[...] = low(logistic * (1.0 + z * (1.0 - logistic)))
    return dot_cols(hid_ref[...], w_out) + shift


def convolution_forward(
    lens_ref,
    n1_ref,
    small_own,
    small_recv,
    win_own,
    win_recv,
    wout_own,
    wout_recv,
    vec_ref,
    taps_ref,
    proj_ref,
    glu_ref,
    conv_ref,
    vec2_ref,
    hid_out,
    slope_out,
    n2_out,
    inv2_out,
    ml_out,
    red_out,
    lin_out,
    sg_out,
    u_out,
    c_out,
    stat_out,
    win,
    wout,
    t_sc,
    u_sc,
    k_sc,
    c_sc,
):
    core = lax.axis_index("section")
    first = core == 0
    frames, features = n1_ref.shape
    half = frames // 2
    choose(first, win_own, win_recv, win)
    choose(first, wout_own, wout_recv, wout)
    ends = bounds_of(lens_ref, core)
    bias, gains, shifts = layer_vectors(small_own, small_recv, first, features)
    h1 = n1_ref[...] * gains[0:1] + shifts[0:1]
    fed = feed_forward(h1, bias, win[...], wout[...], shifts[2:3], hid_out, slope_out)
    n2, inv2 = normalise(h1 + fed)
    n2_out[...] = n2
    inv2_out[...] = inv2
    inside = jnp.where(iota((frames, 1), 0) < ends[-1], 1.0, 0.0)
    put_tiles(t_sc, 0, (n2 * gains[1:2] + shifts[1:2]) * inside)
    joined, valid = half_masks(half, ends)
    even, odd = even_odd(t_sc, half, features)
    before = pltpu.roll(odd, 1, 0) * joined
    mixed = low(taps_ref[0:1] * before + taps_ref[1:2] * even + taps_ref[2:3] * odd)
    ml_out[...] = mixed
    reduced = low(dot(mixed, proj_ref[...]) + vec_ref[5:6])
    red_out[...] = reduced
    gates = dot_cols(reduced, glu_ref[...])
    linear = gates[:, 0:features] + vec2_ref[0:1]
    logistic = jax.nn.sigmoid(gates[:, features:] + vec2_ref[1:2])
    gated = linear * logistic
    lin_out[...] = linear
    sg_out[...] = logistic
    u_out[...] = gated
    tap_count = conv_ref.shape[0]
    reach = tap_count // 2
    lowest, highest = tap_ranges(half, ends, reach)
    u_sc[...] = jnp.zeros(u_sc.shape, F32)
    k_sc[...] = jnp.zeros(k_sc.shape, F32)
    put_tiles(u_sc, SUB, gated)
    put_tiles(k_sc, 0, conv_ref[...])
    for begin in range(0, half, BLOCK):
        first, last = lowest[begin : begin + BLOCK], highest[begin : begin + BLOCK]
        totals = [jnp.zeros((BLOCK, LANE), F32)] * u_sc.shape[0]
        for o in range(tap_count):
            fits = (first <= o) & (o < last)
            at = SUB - reach + o + begin
            for t in range(u_sc.shape[0]):
                moved = jnp.where(fits, u_sc[t, at : at + BLOCK, :], 0.0)
                totals[t] = totals[t] + moved * k_sc[t, o : o + 1, :]
        for t, total in enumerate(totals):
            c_sc[t, begin : begin + BLOCK, :] = total
    convolved = get_tiles(c_sc, features)
    c_out[...] = convolved
    held = convolved * valid
    send_rows(
        stat_out, [row_sum(held), row_sum(held * convolved)], jnp.sum(valid, axis=0, keepdims=True)
    )


def even_odd(ref, half, features):
    even = [ref[t, pl.ds(0, half, stride=2), :] for t in range(ref.shape[0])]
    odd = [ref[t, pl.ds(1, half, stride=2), :] for t in range(ref.shape[0])]
    return (
        jnp.concatenate(even, axis=1)[:, 0:features],
        jnp.concatenate(odd, axis=1)[:, 0:features],
    )


def put_even_odd(ref, even, odd):
    half, features = even.shape
    for t in range(ref.shape[0]):
        stop = min(features, (t + 1) * LANE)
        span = slice(0, stop - t * LANE)
        ref[t, pl.ds(0, half, stride=2), span] = even[:, t * LANE : stop]
        ref[t, pl.ds(1, half, stride=2), span] = odd[:, t * LANE : stop]


def send_rows(out_ref, rows, count=None):
    out_ref[...] = jnp.zeros(out_ref.shape, F32)
    at = 0
    for row in rows:
        for begin in range(0, row.shape[1], LANE):
            stop = min(begin + LANE, row.shape[1])
            out_ref[at : at + 1, 0 : stop - begin] = row[:, begin:stop]
            at += 1
    if count is not None:
        out_ref[at : at + 1, :] = jnp.broadcast_to(count, (1, LANE))


def gather_rows(refs, features):
    total = functools.reduce(jnp.add, [ref[...] for ref in refs])
    tiles = up(features, LANE) // LANE
    rows = []
    for at in range(2):
        pieces = [total[at * tiles + t : at * tiles + t + 1, :] for t in range(tiles)]
        rows.append(jnp.concatenate(pieces, axis=1)[:, 0:features])
    return rows[0], rows[1], total[2 * tiles : 2 * tiles + 1, 0:1]


def batch_moments(stat_refs, features):
    first, second, count = gather_rows(stat_refs, features)
    centre = first / count
    return count, centre, lax.rsqrt(second / count - centre * centre + EPSILON)


def feed_back(grad, hid_slope, w_in, w_out):
    grad_low = low(grad)
    inner = low(dot(grad_low, w_out) * hid_slope.astype(F32))
    return grad_low, inner, dot_cols(inner, w_in)


def second_layer(
    parts,
    lens_ref,
    *refs,
):
    second_layer_body(lens_ref, refs[0:parts], *refs[parts:])


def second_layer_body(
    lens_ref,
    stat_refs,
    c_ref,
    red_ref,
    small_own,
    small_recv,
    win_own,
    win_recv,
    wout_own,
    wout_recv,
    point_ref,
    vec2_ref,
    gain_ref,
    own_ref,
    recv_ref,
    g_out,
    dch_out,
    ch_out,
    dr3_out,
    sums_out,
    t2_out,
    h3_out,
    grad_out,
    inner_out,
    hid_out,
    active_out,
    vec_out,
    win,
    wout,
    t_sc,
    slope_sc,
):
    core = lax.axis_index("section")
    first = core == 0
    frames, features = g_out.shape
    half = frames // 2
    choose(first, win_recv, win_own, win)
    choose(first, wout_recv, wout_own, wout)
    ends = bounds_of(lens_ref, core)
    inside = jnp.where(iota((frames, 1), 0) < ends[-1], 1.0, 0.0)
    bias, gains, shifts = layer_vectors(small_own, small_recv, jnp.logical_not(first), features)
    count, centre, rho = batch_moments(stat_refs, features)
    ch = (c_ref[...] - centre) * rho
    bnv = ch * gain_ref[...] + vec2_ref[3:4]
    logistic = jax.nn.sigmoid(bnv)
    active = low(bnv * logistic)
    active_slope = logistic * (1.0 + bnv * (1.0 - logistic))
    branch = dot(active, point_ref[...]) + vec2_ref[2:3]
    n3, inv3 = normalise(red_ref[...].astype(F32) + branch)
    h3 = n3 * gains[0:1] + shifts[0:1]
    fed = feed_forward(h3, bias, win[...], wout[...], shifts[2:3], hid_out, slope_sc)
    n4, inv4 = normalise(h3 + fed)
    t2 = n4 * gains[1:2] + shifts[1:2]
    t2_out[...] = n4 * gains[1:2] + shifts[1:2]
    grad = jnp.where(first, recv_ref[0, :, 0, :], own_ref[0, :, 1, :]).astype(F32).T * inside
    g_out[...] = low(grad)
    put_tiles(t_sc, 0, grad)
    even, odd = even_odd(t_sc, half, features)
    dt2 = even + odd
    dv4 = normalise_back(dt2, n4, inv4, gains[1:2])
    grad_low, inner, back = feed_back(dv4, slope_sc[...], win[...], wout[...])
    dh3 = dv4 + back
    dr3 = normalise_back(dh3, n3, inv3, gains[0:1])
    dr3_out[...] = dr3
    dpw = low(dr3)
    dbn = dot_cols(dpw, point_ref[...]) * active_slope
    dch = dbn * gain_ref[...]
    dch_out[...] = dch
    ch_out[...] = ch
    send_rows(sums_out, [row_sum(dch), row_sum(dch * ch)])
    h3_out[...] = low(h3)
    grad_out[...] = grad_low
    inner_out[...] = inner
    active_out[...] = active
    sums = (dh3 * n3, dt2 * n4, dh3, dt2, grad_low, dpw, dbn, dbn * ch)
    vec_out[...] = jnp.zeros(vec_out.shape, F32)
    for at, values in enumerate(sums):
        vec_out[at : at + 1, :] = row_sum(values)


def second_weights(
    lens_ref,
    h3_ref,
    grad_ref,
    inner_ref,
    hid_ref,
    active_ref,
    dr3_ref,
    vec_ref,
    t2_ref,
    n2_ref,
    small_own,
    small_recv,
    after_ref,
    y_out,
    keep_out,
    send_out,
    y_sc,
    stage,
    rest,
    vec_sc,
):
    core = lax.axis_index("section")
    frames, features = n2_ref.shape
    inner = inner_ref[...]
    pack = Pack(stage, rest, vec_sc)
    vec_sc[...] = jnp.zeros(vec_sc.shape, F32)
    pack.matrix(dot_rows(h3_ref[...], inner))
    pack.matrix(dot_rows(grad_ref[...], hid_ref[...]))
    pack.matrix(dot_rows(active_ref[...], low(dr3_ref[...])))
    pack.bias = row_sum(inner)
    pack.vector(1, vec_ref[...])
    pack.finish(core, keep_out, send_out)
    ends = bounds_of(lens_ref, core)
    inside = jnp.where(iota((frames, 1), 0) < ends[-1], 1.0, 0.0)
    bias, gains, shifts = layer_vectors(small_own, small_recv, core == 0, features)
    skip = low((n2_ref[...] * gains[1:2] + shifts[1:2]) * inside).astype(F32)
    put_even_odd(y_sc, t2_ref[...], t2_ref[...])
    y_out[...] = (get_tiles(y_sc, features) + skip) * inside


def convolution_back(
    parts,
    after,
    lens_ref,
    *refs,
):
    convolution_back_body(
        lens_ref, refs[0:parts], refs[parts : 2 * parts], *refs[2 * parts + after :]
    )


def convolution_back_body(
    lens_ref,
    stat_refs,
    sums_refs,
    dch_ref,
    ch_ref,
    dr3_ref,
    u_ref,
    lin_ref,
    sg_ref,
    red_ref,
    ml_ref,
    n2_ref,
    small_own,
    small_recv,
    taps_ref,
    proj_ref,
    glu_ref,
    conv_ref,
    g_ref,
    dt_out,
    mats_out,
    vec_out,
    kd_out,
    t_sc,
    u_sc,
    d_sc,
    k_sc,
    c_sc,
    gate_sc,
):
    first = lax.axis_index("section") == 0
    frames, features = n2_ref.shape
    half = frames // 2
    ends = bounds_of(lens_ref, lax.axis_index("section"))
    inside = jnp.where(iota((frames, 1), 0) < ends[-1], 1.0, 0.0)
    joined, valid = half_masks(half, ends)
    bias, gains, shifts = layer_vectors(small_own, small_recv, first, features)
    count, centre, rho = batch_moments(stat_refs, features)
    sum1, sum2, _ = gather_rows(sums_refs, features)
    dc = (rho * valid) * (dch_ref[...] - sum1 / count - ch_ref[...] * (sum2 / count))
    tap_count = conv_ref.shape[0]
    reach = tap_count // 2
    lowest, highest = tap_ranges(half, ends, reach)
    u_sc[...] = jnp.zeros(u_sc.shape, F32)
    d_sc[...] = jnp.zeros(d_sc.shape, F32)
    k_sc[...] = jnp.zeros(k_sc.shape, F32)
    kd_out[...] = jnp.zeros(kd_out.shape, F32)
    vec_out[...] = jnp.zeros(vec_out.shape, F32)
    put_tiles(u_sc, 0, u_ref[...])
    put_tiles(d_sc, SUB, dc)
    put_tiles(k_sc, 0, conv_ref[...])
    for begin in range(0, half, BLOCK):
        lead, stop = lowest[begin : begin + BLOCK], highest[begin : begin + BLOCK]
        totals = [jnp.zeros((BLOCK, LANE), F32)] * u_sc.shape[0]
        for o in range(tap_count):
            fits = (lead <= o) & (o < stop)
            at = SUB - reach + o + begin
            tap = slice(tap_count - 1 - o, tap_count - o)
            for t in range(u_sc.shape[0]):
                moved = jnp.where(fits, d_sc[t, at : at + BLOCK, :], 0.0)
                totals[t] = totals[t] + moved * k_sc[t, tap, :]
                met = row_sum(moved * u_sc[t, begin : begin + BLOCK, :])
                kd_out[t, tap, :] = kd_out[t, tap, :] + met
        for t, total in enumerate(totals):
            c_sc[t, begin : begin + BLOCK, :] = total
    du = get_tiles(c_sc, features)
    logistic = sg_ref[...]
    dlin = low(du * logistic)
    dgat = low(du * lin_ref[...] * logistic * (1.0 - logistic))
    reduced = red_ref[...]
    gate_sc[:, 0:features] = dlin.astype(F32)
    gate_sc[:, features:] = dgat.astype(F32)
    dred = low(dot(low(gate_sc[...]), glu_ref[...]) + dr3_ref[...])
    at = 5 * features % LANE
    for grads in (dot_rows(dlin, reduced), dot_rows(dgat, reduced), dot_rows(ml_ref[...], dred)):
        mats_out[:, at : at + features] = grads
        at += features
    for row, values in ((9, dlin), (10, dgat), (5, dred)):
        vec_out[row : row + 1, 0:features] = row_sum(values)
    dm = dot_cols(dred, proj_ref[...])
    n2 = n2_ref[...]
    put_tiles(t_sc, 0, (n2 * gains[1:2] + shifts[1:2]) * inside)
    even, odd = even_odd(t_sc, half, features)
    vec_out[6:7, 0:features] = row_sum(pltpu.roll(odd, 1, 0) * joined * dm)
    vec_out[7:8, 0:features] = row_sum(even * dm)
    vec_out[8:9, 0:features] = row_sum(odd * dm)
    carried = pltpu.roll(taps_ref[0:1] * joined * dm, half - 1, 0)
    put_even_odd(t_sc, taps_ref[1:2] * dm, taps_ref[2:3] * dm + carried)
    dt_out[...] = (g_ref[...].astype(F32) + get_tiles(t_sc, features)) * inside

def first_layer_back(
    dt_ref,
    n2_ref,
    inv2_ref,
    n1_ref,
    inv1_ref,
    hid_ref,
    slope_ref,
    small_own,
    small_recv,
    win_own,
    win_recv,
    wout_own,
    wout_recv,
    after_ref,
    dr1_out,
    keep_out,
    send_out,
    win,
    wout,
    stage,
    rest,
    vec_sc,
):
    core = lax.axis_index("section")
    first = core == 0
    choose(first, win_own, win_recv, win)
    choose(first, wout_own, wout_recv, wout)
    bias, gains, shifts = layer_vectors(small_own, small_recv, first, win.shape[0])
    pack = Pack(stage, rest, vec_sc)
    vec_sc[...] = jnp.zeros(vec_sc.shape, F32)
    dt = dt_ref[...]
    n2 = n2_ref[...]
    dv2 = normalise_back(dt, n2, inv2_ref[...], gains[1:2])
    pack.vector(2, row_sum(dt * n2))
    pack.vector(4, row_sum(dt))
    n1 = n1_ref[...]
    h1 = low(n1 * gains[0:1] + shifts[0:1])
    grad_low, inner, back = feed_back(dv2, slope_ref[...], win[...], wout[...])
    dh1 = dv2 + back
    pack.matrix(dot_rows(h1, inner))
    pack.matrix(dot_rows(grad_low, hid_ref[...]))
    pack.bias = row_sum(inner)
    pack.vector(5, row_sum(grad_low))
    pack.vector(1, row_sum(dh1 * n1))
    pack.vector(3, row_sum(dh1))
    dr1_out[...] = normalise_back(dh1, n1, inv1_ref[...], gains[0:1])
    pack.finish(core, keep_out, send_out)


def attention_back(
    heads,
    dr1_ref,
    qu_ref,
    qw_ref,
    k_ref,
    v_ref,
    p_ref,
    a_ref,
    wo_ref,
    *refs,
):
    dqr_out, dkv_out, dp_out, sums_out = refs[-4:]
    frames = dr1_ref.shape[0]
    head = dr1_ref.shape[1] // HEADS
    width = len(heads) * LANE
    scale = head**-0.5
    dr1_low = low(dr1_ref[...])
    flip = flip_rows(frames)
    for at, h in enumerate(heads):
        cols = slice(h * LANE, (h + 1) * LANE)
        here = slice(at * LANE, (at + 1) * LANE)
        weights = a_ref[h]
        grad = low(dot_cols(dr1_low, wo_ref[cols, :]))
        weights_f = weights.astype(F32)
        product = weights_f * dot_cols(grad, v_ref[:, cols])
        ds = low(product - weights_f * jnp.sum(product, axis=-1, keepdims=True))
        dkv_out[:, width + at * LANE : width + (at + 1) * LANE] = low(dot_rows(weights, grad))
        dkv_out[:, here] = low(scale * dot_rows(ds, qu_ref[:, cols]))
        dsr = low(dot(flip, ds))
        qwr = low(dot(flip, qw_ref[:, cols]))
        wide = jnp.concatenate([jnp.zeros((frames, frames), BF16), dsr], axis=1)
        band = pltpu.roll(wide.astype(F32), frames + 1, 1, stride=1, stride_axis=0).astype(BF16)
        dqu = scale * dot(dsr, k_ref[:, cols])
        dqw = scale * dot(band, p_ref[:, cols])
        dqr_out[:, here] = low(dqu + dqw)
        dp_out[:, here] = low(scale * dot_rows(band, qwr))
        sums_out[0:1, here] = row_sum(dqu + dqw)
        sums_out[1:2, here] = row_sum(dkv_out[:, width + at * LANE : width + (at + 1) * LANE])
        sums_out[2:3, here] = row_sum(dqu)
        sums_out[3:4, here] = row_sum(dqw)


def flip_rows(frames):
    hit = iota((frames, frames), 0) + iota((frames, frames), 1) == frames - 1
    return jnp.where(hit, 1.0, 0.0).astype(BF16)


def attention_weights_back(
    dr1_ref,
    xt_ref,
    o_ref,
    table_ref,
    mats_ref,
    vec_ref,
    kd_ref,
    *refs,
):
    parts, after_ref = (refs[0:4], refs[4:8]), refs[8]
    dq_out, dkv_out, keep_out, send_out, stage, rest, vec_sc = refs[9:]
    core = lax.axis_index("section")
    frames, features = dr1_ref.shape
    width = HEADS * LANE
    pack = Pack(stage, rest, vec_sc)
    vec_sc[...] = vec_ref[...]
    begin = 5 * features // LANE * LANE
    stage[:, begin : begin + mats_ref.shape[1]] = mats_ref[...]
    dr1_low = low(dr1_ref[...])
    unselect = head_unselect(features, features // HEADS)
    pack.vector(2, row_sum(dr1_low))
    pack.matrix(dot_rows(unselect, low(dot_rows(o_ref[...], dr1_low))))
    half = width // 2
    flip = flip_rows(frames)
    for at, (dqr, dkv, dp, sums) in enumerate(parts):
        here = slice(at * half, (at + 1) * half)
        dq_out[:, here] = low(dot(flip, dqr[...]))
        dkv_out[:, here] = dkv[:, 0:half]
        dkv_out[:, width + at * half : width + (at + 1) * half] = dkv[:, half:]
    sums = jnp.concatenate([sums[0:4, :] for _, _, _, sums in parts], axis=1)
    sums = dot(sums, unselect.astype(F32), precision=lax.Precision.HIGHEST)
    pack.vector(0, sums[0:2])
    pack.vector(3, sums[2:4])
    x_turned = xt_ref[...]
    pack.matrix(dot(low(dot(x_turned, dq_out[...])), unselect))
    pack.matrix(dot(low(dot(x_turned, dkv_out[:, 0:width])), unselect))
    pack.matrix(dot(low(dot(x_turned, dkv_out[:, width:])), unselect))
    dp = jnp.concatenate([dp[...] for _, _, dp, _ in parts], axis=1)
    pack.matrix(dot(low(dot_rows(table_ref[...], dp)), unselect))
    pack.used = 8 * features
    pack.finish(core, keep_out, send_out, [kd_ref[t] for t in range(kd_ref.shape[0])])


def input_back(dr1_ref, dq_ref, dkv_ref, w_ref, y_ref, after_ref, rows_out, cross_out):
    core = lax.axis_index("section")
    width = dq_ref.shape[1]
    dx = dr1_ref[...] + dot_cols(dq_ref[...], w_ref[:, 0:width])
    dx = (dx + dot_cols(dkv_ref[...], w_ref[:, width:])).T
    y = y_ref[...].T
    rows_out[...] = jnp.where(core == 0, dx, y)
    cross_out[...] = jnp.where(core == 0, y, dx)


def place_of(bit, core):
    return 1 - bit if bit < 2 and core == 1 else bit


def digits(bits, core):
    row = lax.axis_index("rows")
    digit = jnp.int32(0)
    for bit in bits:
        place = jnp.where(core == 0, place_of(bit, 0), place_of(bit, 1))
        digit = (digit << 1) | ((row >> place) & 1)
    return digit


def partner(values, bits, m):
    peers = lax.axis_size("rows")
    pairs = []
    for core in range(2):
        flips = [1 << place_of(b, core) for at, b in enumerate(reversed(bits)) if m >> at & 1]
        pairs += [(core * peers + r, core * peers + (r ^ sum(flips))) for r in range(peers)]
    return lax.ppermute(values, ("section", "rows"), pairs)


def step_kernel(bits, join, count, *refs):
    parts = refs[:count]
    if bits:
        outs = refs[-(1 << len(bits)) :]
        rows = outs[0].shape[0]
        mine = digits(bits, lax.axis_index("section"))
        for m, out in enumerate(outs):
            span = pl.ds(pl.multiple_of((mine ^ m) * rows, SUB), rows)
            out[...] = low(sum(part[span, :].astype(F32) for part in parts))
    elif join:
        rows = parts[0].shape[0]
        for at, part in enumerate(parts):
            refs[-1][at * rows : (at + 1) * rows, :] = part[...]
    else:
        refs[-1][...] = low(sum(part[...].astype(F32) for part in parts))


def step(parts, after, name, bits=(), join=False):
    rows = parts[0].shape[0]
    if bits:
        outs = [shape((rows >> len(bits), LANE), BF16)] * (1 << len(bits))
    else:
        outs = [shape((rows * (len(parts) if join else 1), LANE), BF16)]
    return call(
        functools.partial(step_kernel, bits, join, len(parts)),
        name,
        [VMEM] * len(parts) + [ANY] * len(after),
        outs,
        limit=STEP_LIMIT,
        cost=STEP_COST,
    )(*parts, *after)


class Chain:
    def __init__(self, name, keep, send, splits, whole, gathers):
        self.name = name
        self.parts = [keep, swap(send)]
        self.summing = True
        self.plan = [("split", bits) for bits in splits]
        self.plan += [("whole", bits) for bits in whole]
        self.plan += [("gather", bits) for bits in gathers] + [("last", ())]

    def advance(self, after=()):
        kind, bits = self.plan.pop(0)
        name = "_".join([self.name, kind, *map(str, bits)])
        if kind == "last":
            (send,) = step(self.parts[1:], after, name, join=True)
            self.pieces = [self.parts[0], send, self.early, swap(send)]
            return send
        if kind == "split":
            blocks = step(self.parts, after, name, bits=bits)
            self.parts = [blocks[0]] + [partner(b, bits, m + 1) for m, b in enumerate(blocks[1:])]
            return blocks[1]
        (block,) = step(self.parts, after, name, join=not self.summing)
        self.summing = kind == "whole"
        self.parts = [block] + [partner(block, bits, m) for m in range(1, 1 << len(bits))]
        if len(self.plan) == 1:
            self.early = swap(block)
        return block


def reorder(pieces, target, bits):
    core = lax.axis_index("section")
    half = target.shape[0] // 2
    block = half >> bits
    for side in range(2):
        owner = core if side == 0 else 1 - core
        mine = digits(range(bits), owner)
        at = 0
        for piece in pieces[2 * side : 2 * side + 2]:
            for first in range(0, piece.shape[0], block):
                begin = pl.multiple_of(owner * half + (mine ^ at) * block, SUB)
                target[pl.ds(begin, block), :] = piece[first : first + block, :]
                at += 1


def spread_tiles(pack, stage):
    rows, wide = stage.shape
    tall = rows // SUB * SUB
    tail = rows - tall
    tiles = wide // LANE
    at = tall * tiles
    rest = pack[at : at + up(tail * tiles, SUB), :].astype(F32)
    for t in range(tiles):
        cols = slice(t * LANE, (t + 1) * LANE)
        stage[0:tall, cols] = pack[t * tall : (t + 1) * tall, :].astype(F32)
        stage[tall:rows, cols] = rest[t * tail : (t + 1) * tail]
    return at + rest.shape[0]


def vectors_at(ref, row, features, rows=SUB):
    tiles = up(features, LANE) // LANE
    pieces = [ref[row + t * rows : row + (t + 1) * rows, :] for t in range(tiles)]
    return jnp.concatenate(pieces, axis=1).astype(F32)[:, 0:features], row + tiles * rows


def bias_at(ref, row, cols):
    lines = ref[row : row + SUB, :].astype(F32)
    pieces = [lines[t : t + 1] for t in range(up(cols, LANE) // LANE)]
    return jnp.concatenate(pieces, axis=1)[:, 0:cols]


def unpack_one(
    bits,
    piece0,
    piece1,
    piece2,
    piece3,
    after_ref,
    point_out,
    gain_out,
    win_out,
    wout_out,
    bias_out,
    vec_out,
    pack,
    stage,
):
    reorder((piece0, piece1, piece2, piece3), pack, bits)
    at = spread_tiles(pack, stage)
    features = point_out.shape[0]
    inner = win_out.shape[2]
    win_out[:, 0, :] = stage[:, 0:inner]
    wout_out[:, 0, :] = stage[:, inner : 2 * inner]
    point_out[...] = stage[:, 2 * inner : 2 * inner + features]
    rows, at = vectors_at(pack, at, features)
    vec_out[...] = rows
    gain_out[...] = rows[8:9]
    bias_out[...] = bias_at(pack, at, inner)


def unpack_two(
    bits,
    win_ref,
    wout_ref,
    bias_ref,
    vec_ref,
    piece0,
    piece1,
    piece2,
    piece3,
    after_ref,
    norm_out,
    win_out,
    bias_out,
    wout_out,
    block_out,
    pack,
    stage,
):
    core = lax.axis_index("section")
    reorder((piece0, piece1, piece2, piece3), pack, bits)
    at = spread_tiles(pack, stage)
    features = win_out.shape[0]
    inner = win_out.shape[2]

    @pl.when(core == 0)
    def _():
        win_out[:, 0, :] = stage[:, 0:inner]
        wout_out[:, 0, :] = stage[:, inner : 2 * inner]

    @pl.when(core != 0)
    def _():
        win_out[...] = win_ref[...]
        wout_out[...] = wout_ref[...]

    rows, at = vectors_at(pack, at, features)
    bias_out[...] = jnp.where(core == 0, bias_at(pack, at, inner), bias_ref[...])
    mine = jnp.where(core == 0, rows, vec_ref[...])
    norm_out[0] = mine[1:3]
    for row in range(3):
        block_out[row] = mine[3 + row : 4 + row]


def unpack_three(
    bits,
    vec_ref,
    piece0,
    piece1,
    piece2,
    piece3,
    after_ref,
    attn_in_out,
    pos_out,
    attn_out_out,
    glu_out,
    proj_out,
    conv_out,
    vec_out,
    taps_out,
    vec2_out,
    pack,
    stage,
):
    reorder((piece0, piece1, piece2, piece3), pack, bits)
    at = spread_tiles(pack, stage)
    features = pos_out.shape[0]
    attn_out_out[...] = stage[:, 0:features]
    attn_in_out[...] = stage[:, features : 4 * features]
    pos_out[...] = stage[:, 4 * features : 5 * features]
    glu_out[0:features, :] = stage[:, 5 * features : 6 * features]
    glu_out[features:, :] = stage[:, 6 * features : 7 * features]
    proj_out[...] = stage[:, 7 * features : 8 * features]
    taps = conv_out.shape[0]
    rows, at = vectors_at(pack, at, features, up(taps, SUB))
    conv_out[...] = rows[0:taps]
    rows, at = vectors_at(pack, at, features)
    vec_out[...] = rows[0:6]
    taps_out[...] = rows[6:9]
    vec2_out[0:2, :] = rows[9:11]
    vec2_out[2:4, :] = vec_ref[6:8, :]


def join_rows(rows_ref, cross_ref, after_ref, boundary_out, mark_out):
    mark_out[...] = jnp.zeros(mark_out.shape, F32)
    core = lax.axis_index("section")
    rows, cross = rows_ref[...], cross_ref[...]
    boundary_out[0, :, 0, :] = jnp.where(core == 0, rows, cross)
    boundary_out[0, :, 1, :] = jnp.where(core == 0, cross, rows)


def shape(dims, dtype=F32):
    return jax.ShapeDtypeStruct(dims, dtype)


SMEM = pl.BlockSpec(memory_space=pltpu.SMEM)
VMEM = pl.BlockSpec(memory_space=pltpu.VMEM)
ANY = pl.BlockSpec(memory_space=pl.ANY)
HBM = pl.BlockSpec(memory_space=pltpu.HBM)


def call(kernel, name, in_specs, out_shape, scratch=(), limit=None, cost=None):
    cost = KERNEL_COST if cost is None else cost
    return pl.pallas_call(
        kernel,
        name=name,
        in_specs=in_specs,
        out_specs=[VMEM] * len(out_shape),
        out_shape=out_shape,
        scratch_shapes=list(scratch),
        compiler_params=pltpu.CompilerParams(vmem_limit_bytes=limit or VMEM_LIMIT),
        cost_estimate=pl.CostEstimate(flops=400 * cost, bytes_accessed=cost, transcendentals=0),
    )


def position_table(frames, features):
    distance = (frames - np.arange(2 * frames)).astype(np.float32)
    frequency = np.exp(
        np.arange(0, features, 2).astype(np.float32) * np.float32(-math.log(10000.0) / features)
    ).astype(np.float32)
    angles = (distance[:, None] * frequency[None, :]).astype(np.float64)
    table = np.stack([np.sin(angles), np.cos(angles)], axis=-1).reshape(2 * frames, features)
    return jnp.asarray(table.astype(np.float32), BF16)


def in_hbm(values):
    return pltpu.with_memory_space_constraint(values, pltpu.HBM)


def swap(values):
    return lax.ppermute(values, "section", [(0, 1), (1, 0)])


def share(values):
    bits = lax.axis_size("rows").bit_length() - 1
    parts = [values]
    for begin in range(0, bits, 2):
        values = functools.reduce(jnp.add, parts)
        parts = [values]
        for step in range(1, 1 << min(2, bits - begin)):
            pairs = [(r, r ^ (step << begin)) for r in range(1 << bits)]
            parts.append(lax.ppermute(values, "rows", pairs))
    return parts, values


def shards(
    boundary,
    utt_lengths,
    attn_in,
    pos_proj,
    attn_out,
    first_vectors,
    reduce_taps,
    reduce_proj,
    glu_in,
    conv_taps,
    second_vectors,
    bn_gain,
    point_proj,
    ffn_in,
    ffn_bias,
    ffn_out,
    norm_gain,
    block_vectors,
):
    peers = lax.axis_size("rows")
    _, batches, frames, features = boundary.shape
    half = frames // 2
    inner = ffn_in.shape[2]
    width = HEADS * LANE
    tiles = up(features, LANE) // LANE
    tap_rows = up(conv_taps.shape[0], SUB)
    cols = (2 * inner + features, 2 * inner, 8 * features)
    wide = [up(count, LANE) for count in cols]
    others = (0, 0, tap_rows * tiles)
    heights = [
        pack_heights(features, count, bias, other)
        for count, bias, other in zip(cols, (inner, inner, 0), others)
    ]
    pack_rows = [up(height[2], peers * SUB) for height in heights]
    row_bits = peers.bit_length() - 1
    singles = [(bit,) for bit in range(row_bits - 1)]
    pairs = [tuple(range(at, min(at + 2, row_bits))) for at in range(0, row_bits, 2)]
    by_one = (singles, [(row_bits - 1,)], singles[::-1])
    by_two = (pairs, [], pairs[::-1])
    table = position_table(frames, features)
    turned = jnp.transpose(boundary, (0, 3, 1, 2))
    wout_own = jnp.transpose(ffn_out, (0, 2, 1))
    shift_own = jnp.transpose(block_vectors, (1, 0, 2))
    glu_turned = glu_in.T

    recv = swap(turned)
    weights = (ffn_in, swap(ffn_in), wout_own, swap(wout_own))

    def scratch(*dims, dtype=F32):
        return pltpu.VMEM(dims, dtype)

    p, w_pad, wo_pad, vectors, small = call(
        prepare,
        "prepare",
        [HBM] * 8,
        [
            shape((2 * frames, width), BF16),
            shape((features, 3 * width), BF16),
            shape((width, features), BF16),
            shape((first_vectors.shape[0], width)),
            shape((8, inner)),
        ],
        [
            scratch(*attn_in.shape, dtype=BF16),
            scratch(*pos_proj.shape, dtype=BF16),
            scratch(*attn_out.shape, dtype=BF16),
            scratch(*first_vectors.shape),
            scratch(*table.shape, dtype=BF16),
            scratch(*ffn_bias.shape),
            scratch(*norm_gain.shape),
            scratch(*shift_own.shape),
            pltpu.SemaphoreType.DMA((8,)),
        ],
        cost=10**7,
    )(
        *map(in_hbm, (attn_in, pos_proj, attn_out, first_vectors, table)),
        *map(in_hbm, (ffn_bias, norm_gain, shift_own)),
    )
    small = (small, swap(small))
    xt, qu, qw, k, v, a, o, n1, inv1 = call(
        attention_forward,
        "attention_forward",
        [SMEM] + [VMEM] * 7,
        [
            shape((features, frames), BF16),
            shape((frames, width), BF16),
            shape((frames, width), BF16),
            shape((frames, width), BF16),
            shape((frames, width), BF16),
            shape((HEADS, frames, frames), BF16),
            shape((frames, width), BF16),
            shape((frames, features)),
            shape((frames, 1)),
        ],
    )(
        in_hbm(utt_lengths),
        in_hbm(turned),
        recv,
        p,
        w_pad,
        wo_pad,
        vectors,
        in_hbm(first_vectors),
    )

    weights_scratch = [scratch(features, inner, dtype=BF16)] * 2
    rows_scratch = scratch(tiles, frames, LANE)
    edge_scratch = scratch(tiles, half + 2 * SUB, LANE)
    taps_scratch = scratch(tiles, tap_rows, LANE)
    vec_scratch = scratch(SUB, tiles * LANE)

    def pack_scratch(index):
        return scratch(pack_rows[index], LANE, dtype=BF16)

    def stage_scratch(index):
        return scratch(features, wide[index])

    def pack_stages(index):
        return [stage_scratch(index), scratch(heights[index][1], LANE), vec_scratch]

    def pack_halves(index):
        return [shape((pack_rows[index] // 2, LANE), BF16)] * 2

    hid, slope, n2, inv2, ml, red, lin, sg, u, c, stat = call(
        convolution_forward,
        "convolution_forward",
        [SMEM] + [VMEM] * 13,
        [
            shape((frames, inner), BF16),
            shape((frames, inner), BF16),
            shape((frames, features)),
            shape((frames, 1)),
            shape((half, features), BF16),
            shape((half, features), BF16),
            shape((half, features)),
            shape((half, features)),
            shape((half, features)),
            shape((half, features)),
            shape((8, LANE)),
        ],
        weights_scratch + [rows_scratch, edge_scratch, taps_scratch, scratch(tiles, half, LANE)],
    )(
        utt_lengths,
        n1,
        *small,
        *weights,
        first_vectors,
        reduce_taps,
        reduce_proj,
        glu_turned,
        conv_taps,
        second_vectors,
    )
    stat, _ = share(stat)
    g, dch, ch, dr3, sums, t2, h3, grad4, inner4, hid4, active, vec1 = call(
        functools.partial(second_layer, len(stat)),
        "second_layer",
        [SMEM] + [VMEM] * (13 + len(stat)),
        [
            shape((frames, features), BF16),
            shape((half, features)),
            shape((half, features)),
            shape((half, features)),
            shape((8, LANE)),
            shape((half, features)),
            shape((half, features), BF16),
            shape((half, features), BF16),
            shape((half, inner), BF16),
            shape((half, inner), BF16),
            shape((half, features), BF16),
            shape((8, features)),
        ],
        weights_scratch + [rows_scratch, scratch(half, inner, dtype=BF16)],
    )(
        utt_lengths,
        *stat,
        c,
        red,
        *small,
        *weights,
        point_proj,
        second_vectors,
        bn_gain[None],
        turned,
        recv,
    )
    sums, sent = share(sums)
    chains = {}
    made = {}

    def weights_two(mark):
        y, keep, send = call(
            second_weights,
            "second_weights",
            [SMEM] + [VMEM] * 11 + [ANY],
            [shape((frames, features))] + pack_halves(0),
            [rows_scratch] + pack_stages(0),
        )(utt_lengths, h3, grad4, inner4, hid4, active, dr3, vec1, t2, n2, *small, mark)
        made["y"] = y
        chains["1"] = Chain("one", keep, send, *by_one)
        return keep

    def conv_back(mark):
        made["conv"] = call(
            functools.partial(convolution_back, len(stat), 1),
            "convolution_back",
            [SMEM] + [VMEM] * (2 * len(stat)) + [ANY] + [VMEM] * 16,
            [
                shape((frames, features)),
                shape((features, up(5 * features % LANE + 3 * features, LANE))),
                shape((SUB, tiles * LANE)),
                shape((tiles, tap_rows, LANE)),
            ],
            [
                rows_scratch,
                scratch(tiles, half, LANE),
                edge_scratch,
                taps_scratch,
                scratch(tiles, half, LANE),
                scratch(half, 2 * features),
            ],
        )(
            utt_lengths,
            *stat,
            *sums,
            mark,
            dch,
            ch,
            dr3,
            u,
            lin,
            sg,
            red,
            ml,
            n2,
            *small,
            reduce_taps,
            reduce_proj,
            glu_turned,
            conv_taps,
            g,
        )
        return made["conv"][0]

    def first_back(mark):
        dr1, keep, send = call(
            first_layer_back,
            "first_layer_back",
            [VMEM] * 13 + [ANY],
            [shape((frames, features))] + pack_halves(1),
            weights_scratch + pack_stages(1),
        )(made["conv"][0], n2, inv2, n1, inv1, hid, slope, *small, *weights, mark)
        made["dr1"] = dr1
        chains["2"] = Chain("two", keep, send, *by_one)
        return dr1

    def heads_back(heads, mark):
        wide_heads = len(heads) * LANE
        made[heads[0]] = call(
            functools.partial(attention_back, heads),
            "attention_back",
            [VMEM] * 8 + [ANY],
            [
                shape((frames, wide_heads), BF16),
                shape((frames, 2 * wide_heads), BF16),
                shape((2 * frames, wide_heads), BF16),
                shape((8, wide_heads)),
            ],
        )(made["dr1"], qu, qw, k, v, p, a, wo_pad, mark)
        return made[heads[0]][0]

    def weights_one(mark):
        parts = made[0] + made[HEADS // 2]
        made["dq"], made["dkv"], keep, send = call(
            attention_weights_back,
            "attention_weights_back",
            [VMEM] * 15 + [ANY],
            [shape((frames, width), BF16), shape((frames, 2 * width), BF16)] + pack_halves(2),
            pack_stages(2),
        )(made["dr1"], xt, o, table, *made["conv"][1:], *parts, mark)
        chains["3"] = Chain("three", keep, send, *by_one)
        return keep

    def rows_back(mark):
        made["rows"], cross = call(
            input_back,
            "input_back",
            [VMEM] * 5 + [ANY],
            [shape((features, frames))] * 2,
        )(made["dr1"], made["dq"], made["dkv"], w_pad, made["y"], mark)
        made["cross"] = swap(cross)
        return made["rows"]

    def rows_join(mark):
        made["boundary"], mark = call(
            join_rows,
            "join_rows",
            [VMEM] * 2 + [ANY],
            [shape((1, features, batches, frames)), shape((8, LANE))],
        )(made["rows"], made["cross"], mark)
        return mark

    def open_one(mark):
        made["point"], made["gain"], *made["one"] = call(
            functools.partial(unpack_one, row_bits - 1),
            "unpack_one",
            [VMEM] * 4 + [ANY],
            [
                shape(point_proj.shape),
                shape((1, features)),
                shape((features, 1, inner)),
                shape((features, 1, inner)),
                shape(ffn_bias.shape),
                shape((SUB, features)),
            ],
            [pack_scratch(0), stage_scratch(0)],
        )(*chains["1"].pieces, mark)
        return made["one"][3]

    def open_two(mark):
        made["two"] = call(
            functools.partial(unpack_two, row_bits - 1),
            "unpack_two",
            [VMEM] * 8 + [ANY],
            [
                shape(norm_gain.shape),
                shape((features, 1, inner)),
                shape(ffn_bias.shape),
                shape((features, 1, inner)),
                shape(shift_own.shape),
            ],
            [pack_scratch(1), stage_scratch(1)],
        )(*made["one"], *chains["2"].pieces, mark)
        return made["two"][0]

    def open_three(mark):
        made["three"] = call(
            functools.partial(unpack_three, row_bits - 1),
            "unpack_three",
            [VMEM] * 5 + [ANY],
            [
                shape(attn_in.shape),
                shape(pos_proj.shape),
                shape(attn_out.shape),
                shape(glu_turned.shape),
                shape(reduce_proj.shape),
                shape(conv_taps.shape),
                shape(first_vectors.shape),
                shape(reduce_taps.shape),
                shape(second_vectors.shape),
            ],
            [pack_scratch(2), stage_scratch(2)],
        )(made["one"][3], *chains["3"].pieces, mark)
        return made["three"][6]

    runs = dict(K=weights_two, E=conv_back, F=first_back, C=weights_one, D=rows_back)
    runs.update(J=rows_join, U=open_one, V=open_two, W=open_three)
    runs["A"] = functools.partial(heads_back, range(HEADS // 2))
    runs["B"] = functools.partial(heads_back, range(HEADS // 2, HEADS))
    order = ORDER
    spare = len(singles) - 3
    for number in "123":
        at = order.index({"1": "K", "2": "F", "3": "D"}[number]) + 1
        at = order.index(number, at)
        order = order[:at] + number * (2 * spare) + order[at:]
    mark = sent
    for letter in order:
        mark = runs[letter](mark) if letter in runs else chains[letter].advance([mark])
    norm_out, win_out, bias_out, wout_out, block_out = made["two"]
    attn_in_out, pos_out, attn_out_out, glu_out, proj_out, conv_out = made["three"][0:6]
    vec_out, taps_out, vec2_out = made["three"][6:]
    return (
        jnp.transpose(made["boundary"], (0, 2, 3, 1)),
        attn_in_out,
        pos_out,
        attn_out_out,
        vec_out,
        taps_out,
        proj_out,
        glu_out.T,
        conv_out,
        vec2_out,
        made["gain"][0],
        made["point"],
        jnp.transpose(win_out, (1, 0, 2)),
        bias_out,
        jnp.transpose(wout_out, (1, 2, 0)),
        norm_out,
        jnp.transpose(block_out, (1, 0, 2)),
    )


def solution(mesh):
    split = (
        P("section", None, None),
        P("section", None),
        P("section", None, None),
        P("section", None, None),
        P("section", None, None),
    )
    return jax.shard_map(
        shards,
        mesh=mesh,
        in_specs=(P("section", None, "rows", None), P(None, "rows", None)) + (P(),) * 11 + split,
        out_specs=(P("section", None, "rows", None),) + (P(),) * 11 + split,
        check_vma=False,
    )
```

```python
import functools
import math

import jax
import jax.numpy as jnp
import numpy as np
from jax import lax
from jax.experimental import pallas as pl
from jax.experimental.pallas import tpu as pltpu
from jax.sharding import PartitionSpec as P

HEADS = 4
LANE = 128
SUB = 16
BLOCK = 64
EPSILON = 1e-05
MASKED = -1e30
F32 = jnp.float32
BF16 = jnp.bfloat16
VMEM_LIMIT = 28 << 20
STEP_LIMIT = 8 << 20
STEP_COST = 12 * 10**6
KERNEL_COST = 12 * 10**6
ORDER = "KE1FG2AB1C2D1321321J321321321323UV3W"


def up(value, step):
    return -(-value // step) * step


def low(values):
    return values.astype(BF16)


def dot(left, right, dims=((1,), (0,)), precision=None):
    return lax.dot_general(
        left, right, (dims, ((), ())), preferred_element_type=F32, precision=precision
    )


def dot_rows(left, right):
    return dot(left, right, ((0,), (0,)))


def dot_cols(left, right):
    return dot(left, right, ((1,), (1,)))


def row_sum(values):
    return jnp.sum(values.astype(F32), axis=0, keepdims=True)


def normalise(values):
    centre = values - jnp.mean(values, axis=-1, keepdims=True)
    inverse = lax.rsqrt(jnp.mean(centre * centre, axis=-1, keepdims=True) + EPSILON)
    return centre * inverse, inverse


def normalise_back(grad, normed, inverse, gain):
    scaled = grad * gain
    first = jnp.mean(scaled, axis=-1, keepdims=True)
    second = jnp.mean(scaled * normed, axis=-1, keepdims=True)
    return inverse * (scaled - first - normed * second)


def bounds_of(lens_ref, batch):
    ends = []
    total = jnp.int32(0)
    for slot in range(lens_ref.shape[-1]):
        total = total + lens_ref[batch, 0, slot]
        ends.append(total)
    return ends


def segment_of(position, ends):
    segment = jnp.zeros(position.shape, jnp.int32)
    for end in ends:
        segment = segment + (position >= end).astype(jnp.int32)
    return segment


def iota(shape, axis):
    return lax.broadcasted_iota(jnp.int32, shape, axis)


def padded_column(index, head):
    within = index & (LANE - 1)
    return jnp.where(within < head, (index >> (LANE.bit_length() - 1)) * head + within, -1 << 20)


def head_select(rows, base, head, dtype):
    wanted = padded_column(iota((1, HEADS * LANE), 1), head) - base
    hit = iota((rows, HEADS * LANE), 0) == wanted
    return jnp.where(hit, 1.0, 0.0).astype(dtype)


def head_unselect(cols, head):
    wanted = padded_column(iota((HEADS * LANE, 1), 0), head)
    hit = iota((HEADS * LANE, cols), 1) == wanted
    return jnp.where(hit, 1.0, 0.0).astype(BF16)


def choose(use_own, own_ref, other_ref, target):
    @pl.when(use_own)
    def _():
        target[...] = own_ref[0]

    @pl.when(jnp.logical_not(use_own))
    def _():
        target[...] = other_ref[0]


def pack_heights(features, cols, bias_cols, others):
    tall = features // SUB * SUB
    tiles = up(cols, LANE) // LANE
    rest = up((features - tall) * tiles, SUB)
    vectors = up(features, LANE) // LANE * SUB + (SUB if bias_cols else 0)
    return tall, rest, tall * tiles + rest + others + vectors


class Pack:
    def __init__(self, stage_ref, rest_ref, vec_ref):
        self.stage, self.rest, self.vec = stage_ref, rest_ref, vec_ref
        self.col = 0
        self.used = 0
        self.bias = None

    def matrix(self, values):
        rows, cols = values.shape
        self.stage[0:rows, self.col : self.col + cols] = values
        self.col += cols
        self.used = max(self.used, self.col)

    def vector(self, at, values):
        self.vec[at : at + values.shape[0], 0 : values.shape[1]] = values

    def finish(self, core, keep_out, send_out, others=()):
        rows, wide = self.stage.shape
        if self.used < wide:
            self.stage[:, self.used : wide] = jnp.zeros((rows, wide - self.used), F32)
        tall = rows // SUB * SUB
        tail = rows - tall
        self.rest[...] = jnp.zeros(self.rest.shape, F32)
        for t in range(wide // LANE):
            part = self.stage[tall:rows, t * LANE : (t + 1) * LANE]
            self.rest[t * tail : (t + 1) * tail, :] = part
        blocks = [lambda t=t: self.stage[0:tall, t * LANE : (t + 1) * LANE] for t in range(wide // LANE)]
        blocks += [lambda: self.rest[...]] + [lambda values=values: values for values in others]
        for t in range(self.vec.shape[1] // LANE):
            blocks.append(lambda t=t: self.vec[:, t * LANE : (t + 1) * LANE])
        if self.bias is not None:
            cols = self.bias.shape[1]
            lines = [self.bias[:, at : at + LANE] for at in range(0, cols, LANE)]
            lines[-1] = jnp.pad(lines[-1], ((0, 0), (0, LANE - lines[-1].shape[1])))
            lines.append(jnp.zeros((SUB - len(lines), LANE), F32))
            blocks.append(lambda: jnp.concatenate(lines, axis=0))

        @pl.when(core == 0)
        def _():
            self.place(keep_out, send_out, blocks)

        @pl.when(core != 0)
        def _():
            self.place(send_out, keep_out, blocks)

    def place(self, low_out, high_out, blocks):
        half = low_out.shape[0]
        row = 0

        def put(values):
            nonlocal row
            rows = values.shape[0]
            cut = min(max(half - row, 0), rows)
            if cut:
                low_out[row : row + cut, :] = low(values[0:cut])
            if cut < rows:
                high_out[row + cut - half : row + rows - half, :] = low(values[cut:])
            row += rows

        for block in blocks:
            put(block())
        if row < 2 * half:
            put(jnp.zeros((2 * half - row, LANE), F32))


def prepare(
    attn_in_hbm,
    pos_proj_hbm,
    attn_out_hbm,
    vec_hbm,
    table_hbm,
    bias_hbm,
    gain_hbm,
    shift_hbm,
    p_out,
    w_out,
    wo_out,
    vectors_out,
    small_out,
    attn_in_ref,
    pos_proj_ref,
    attn_out_ref,
    vec_ref,
    table_ref,
    bias_ref,
    gain_ref,
    shift_ref,
    sem,
):
    sources = (pos_proj_hbm, table_hbm, attn_in_hbm, attn_out_hbm, vec_hbm)
    sources += (bias_hbm, gain_hbm, shift_hbm)
    targets = (pos_proj_ref, table_ref, attn_in_ref, attn_out_ref, vec_ref)
    targets += (bias_ref, gain_ref, shift_ref)
    copies = [
        pltpu.make_async_copy(source, target, sem.at[at])
        for at, (source, target) in enumerate(zip(sources, targets))
    ]
    for copy in copies:
        copy.start()
    features = attn_out_ref.shape[0]
    head = features // HEADS
    width = HEADS * LANE
    select = head_select(features, 0, head, BF16)
    copies[0].wait()
    pos = low(dot(pos_proj_ref[...], select))
    copies[1].wait()
    p_out[...] = low(dot(table_ref[...], pos))
    copies[2].wait()
    for part in range(3):
        begin = part * features
        floor = begin // LANE * LANE
        stop = min(up(begin + features, LANE), 3 * features)
        piece = attn_in_ref[:, floor:stop]
        chosen = head_select(stop - floor, floor - begin, head, BF16)
        w_out[:, part * width : (part + 1) * width] = low(dot(piece, chosen))
    copies[3].wait()
    wo_out[...] = low(dot(head_unselect(features, head), attn_out_ref[...]))
    copies[4].wait()
    vectors_out[...] = dot(
        vec_ref[...], head_select(features, 0, head, F32), precision=lax.Precision.HIGHEST
    )
    for copy in copies[5:]:
        copy.wait()
    small_out[...] = jnp.zeros(small_out.shape, F32)
    small_out[0:1, :] = bias_ref[...]
    small_out[1:3, 0:features] = gain_ref[0]
    for at in range(3):
        small_out[3 + at : 4 + at, 0:features] = shift_ref[at]


def attention_forward(
    lens_ref,
    own_ref,
    recv_ref,
    p_ref,
    w_ref,
    wo_ref,
    vectors_ref,
    vec_ref,
    xt_out,
    qu_out,
    qw_out,
    k_out,
    v_out,
    a_out,
    o_out,
    n1_out,
    inv1_out,
):
    core = lax.axis_index("section")
    features, frames = xt_out.shape
    head = features // HEADS
    width = HEADS * LANE
    ends = bounds_of(lens_ref, core)
    x_turned = jnp.where(core == 0, own_ref[0, :, 0, :], recv_ref[0, :, 1, :])
    xt_out[...] = x_turned
    x_rows = x_turned.astype(F32).T
    x = low(x_rows)
    vectors = vectors_ref[...]
    q = dot(x, w_ref[:, 0:width]) + vectors[0:1]
    qu_out[...] = low(q + vectors[3:4])
    qw_out[...] = low(q + vectors[4:5])
    k_out[...] = low(dot(x, w_ref[:, width : 2 * width]))
    v_out[...] = low(dot(x, w_ref[:, 2 * width :]) + vectors[1:2])
    same = segment_of(iota((frames, 1), 0), ends) == segment_of(iota((1, frames), 1), ends)
    scale = head**-0.5
    for h in range(HEADS):
        cols = slice(h * LANE, (h + 1) * LANE)
        content = dot_cols(qu_out[:, cols], k_out[:, cols])
        relative = dot_cols(qw_out[:, cols], p_ref[:, cols])
        shifted = pltpu.roll(relative, 0, 1, stride=1, stride_axis=0)[:, frames:]
        scores = jnp.where(same, (content + shifted) * scale, MASKED)
        raised = jnp.exp(scores - jnp.max(scores, axis=-1, keepdims=True))
        weights = low(raised * (1.0 / jnp.sum(raised, axis=-1, keepdims=True)))
        a_out[h] = weights
        o_out[:, cols] = low(dot(weights, v_out[:, cols]))
    attended = dot(o_out[...], wo_ref[...]) + vec_ref[2:3, :]
    normed, inverse = normalise(x_rows + attended)
    n1_out[...] = normed
    inv1_out[...] = inverse


def half_masks(half, ends):
    position = 2 * iota((half, 1), 0)
    segment = segment_of(position, ends)
    before = segment_of(position - 1, ends)
    joined = jnp.where((segment == before) & (position > 0), 1.0, 0.0)
    valid = jnp.where(position < ends[-1], 1.0, 0.0)
    return joined, valid


def tap_ranges(half, ends, reach):
    position = iota((half, LANE), 0)
    first = jnp.zeros((half, LANE), jnp.int32)
    last = jnp.full((half, LANE), half, jnp.int32)
    for end in ends:
        edge = end // 2
        first = jnp.where(position >= edge, edge, first)
    for end in reversed(ends):
        edge = end // 2
        last = jnp.where(position < edge, edge, last)
    return first - position + reach, last - position + reach


def shift_tiles(ref, shifted):
    rows = shifted.shape[2]
    for by in range(shifted.shape[0]):
        for t in range(ref.shape[0]):
            shifted[by, t, :, :] = ref[t, by : by + rows, :]


def tap_rows_at(shifted, t, at):
    by = at % shifted.shape[0]
    return shifted[by, t, at - by : at - by + BLOCK, :]


def put_tiles(ref, at, values):
    rows, cols = values.shape
    for t in range(ref.shape[0]):
        stop = min(cols, (t + 1) * LANE)
        ref[t, at : at + rows, 0 : stop - t * LANE] = values[:, t * LANE : stop]


def get_tiles(ref, cols):
    return jnp.concatenate([ref[t] for t in range(ref.shape[0])], axis=1)[:, 0:cols]


def layer_vectors(own_ref, recv_ref, use_own, features):
    rows = jnp.where(use_own, own_ref[...], recv_ref[...])
    return rows[0:1], rows[1:3, 0:features], rows[3:6, 0:features]


def feed_forward(inputs, bias, w_in, w_out, shift, hid_ref, slope_ref):
    z = dot(low(inputs), w_in) + bias
    logistic = jax.nn.sigmoid(z)
    hid_ref[...] = low(z * logistic)
    slope_ref[...] = low(logistic * (1.0 + z * (1.0 - logistic)))
    return dot_cols(hid_ref[...], w_out) + shift


def convolution_forward(
    lens_ref,
    n1_ref,
    small_own,
    small_recv,
    win_own,
    win_recv,
    wout_own,
    wout_recv,
    vec_ref,
    taps_ref,
    proj_ref,
    glu_ref,
    conv_ref,
    vec2_ref,
    hid_out,
    slope_out,
    n2_out,
    inv2_out,
    ml_out,
    red_out,
    lin_out,
    sg_out,
    u_out,
    c_out,
    stat_out,
    win,
    wout,
    t_sc,
    u_sc,
    k_sc,
    c_sc,
    s_sc,
):
    core = lax.axis_index("section")
    first = core == 0
    frames, features = n1_ref.shape
    half = frames // 2
    choose(first, win_own, win_recv, win)
    choose(first, wout_own, wout_recv, wout)
    ends = bounds_of(lens_ref, core)
    bias, gains, shifts = layer_vectors(small_own, small_recv, first, features)
    h1 = n1_ref[...] * gains[0:1] + shifts[0:1]
    fed = feed_forward(h1, bias, win[...], wout[...], shifts[2:3], hid_out, slope_out)
    n2, inv2 = normalise(h1 + fed)
    n2_out[...] = n2
    inv2_out[...] = inv2
    inside = jnp.where(iota((frames, 1), 0) < ends[-1], 1.0, 0.0)
    put_tiles(t_sc, 0, (n2 * gains[1:2] + shifts[1:2]) * inside)
    joined, valid = half_masks(half, ends)
    even, odd = even_odd(t_sc, half, features)
    before = pltpu.roll(odd, 1, 0) * joined
    mixed = low(taps_ref[0:1] * before + taps_ref[1:2] * even + taps_ref[2:3] * odd)
    ml_out[...] = mixed
    reduced = low(dot(mixed, proj_ref[...]) + vec_ref[5:6])
    red_out[...] = reduced
    gates = dot_cols(reduced, glu_ref[...])
    linear = gates[:, 0:features] + vec2_ref[0:1]
    logistic = jax.nn.sigmoid(gates[:, features:] + vec2_ref[1:2])
    gated = linear * logistic
    lin_out[...] = linear
    sg_out[...] = logistic
    u_out[...] = gated
    tap_count = conv_ref.shape[0]
    reach = tap_count // 2
    lowest, highest = tap_ranges(half, ends, reach)
    u_sc[...] = jnp.zeros(u_sc.shape, F32)
    k_sc[...] = jnp.zeros(k_sc.shape, F32)
    put_tiles(u_sc, SUB, gated)
    shift_tiles(u_sc, s_sc)
    put_tiles(k_sc, 0, conv_ref[...])
    for begin in range(0, half, BLOCK):
        first, last = lowest[begin : begin + BLOCK], highest[begin : begin + BLOCK]
        totals = [jnp.zeros((BLOCK, LANE), F32)] * u_sc.shape[0]
        for o in range(tap_count):
            fits = (first <= o) & (o < last)
            at = SUB - reach + o + begin
            for t in range(u_sc.shape[0]):
                moved = jnp.where(fits, tap_rows_at(s_sc, t, at), 0.0)
                totals[t] = totals[t] + moved * k_sc[t, o : o + 1, :]
        for t, total in enumerate(totals):
            c_sc[t, begin : begin + BLOCK, :] = total
    convolved = get_tiles(c_sc, features)
    c_out[...] = convolved
    held = convolved * valid
    send_rows(
        stat_out, [row_sum(held), row_sum(held * convolved)], jnp.sum(valid, axis=0, keepdims=True)
    )


def even_odd(ref, half, features):
    even = [ref[t, pl.ds(0, half, stride=2), :] for t in range(ref.shape[0])]
    odd = [ref[t, pl.ds(1, half, stride=2), :] for t in range(ref.shape[0])]
    return (
        jnp.concatenate(even, axis=1)[:, 0:features],
        jnp.concatenate(odd, axis=1)[:, 0:features],
    )


def put_even_odd(ref, even, odd):
    half, features = even.shape
    for t in range(ref.shape[0]):
        stop = min(features, (t + 1) * LANE)
        span = slice(0, stop - t * LANE)
        ref[t, pl.ds(0, half, stride=2), span] = even[:, t * LANE : stop]
        ref[t, pl.ds(1, half, stride=2), span] = odd[:, t * LANE : stop]


def send_rows(out_ref, rows, count=None):
    out_ref[...] = jnp.zeros(out_ref.shape, F32)
    at = 0
    for row in rows:
        for begin in range(0, row.shape[1], LANE):
            stop = min(begin + LANE, row.shape[1])
            out_ref[at : at + 1, 0 : stop - begin] = row[:, begin:stop]
            at += 1
    if count is not None:
        out_ref[at : at + 1, :] = jnp.broadcast_to(count, (1, LANE))


def gather_rows(refs, features):
    total = functools.reduce(jnp.add, [ref[...] for ref in refs])
    tiles = up(features, LANE) // LANE
    rows = []
    for at in range(2):
        pieces = [total[at * tiles + t : at * tiles + t + 1, :] for t in range(tiles)]
        rows.append(jnp.concatenate(pieces, axis=1)[:, 0:features])
    return rows[0], rows[1], total[2 * tiles : 2 * tiles + 1, 0:1]


def batch_moments(stat_refs, features):
    first, second, count = gather_rows(stat_refs, features)
    centre = first / count
    return count, centre, lax.rsqrt(second / count - centre * centre + EPSILON)


def feed_back(grad, hid_slope, w_in, w_out):
    grad_low = low(grad)
    inner = low(dot(grad_low, w_out) * hid_slope.astype(F32))
    return grad_low, inner, dot_cols(inner, w_in)


def second_layer(
    parts,
    lens_ref,
    *refs,
):
    second_layer_body(lens_ref, refs[0:parts], *refs[parts:])


def second_layer_body(
    lens_ref,
    stat_refs,
    c_ref,
    red_ref,
    small_own,
    small_recv,
    win_own,
    win_recv,
    wout_own,
    wout_recv,
    point_ref,
    vec2_ref,
    gain_ref,
    own_ref,
    recv_ref,
    g_out,
    dch_out,
    ch_out,
    dr3_out,
    sums_out,
    t2_out,
    h3_out,
    grad_out,
    inner_out,
    hid_out,
    active_out,
    vec_out,
    win,
    wout,
    t_sc,
    slope_sc,
):
    core = lax.axis_index("section")
    first = core == 0
    frames, features = g_out.shape
    half = frames // 2
    choose(first, win_recv, win_own, win)
    choose(first, wout_recv, wout_own, wout)
    ends = bounds_of(lens_ref, core)
    inside = jnp.where(iota((frames, 1), 0) < ends[-1], 1.0, 0.0)
    bias, gains, shifts = layer_vectors(small_own, small_recv, jnp.logical_not(first), features)
    count, centre, rho = batch_moments(stat_refs, features)
    ch = (c_ref[...] - centre) * rho
    bnv = ch * gain_ref[...] + vec2_ref[3:4]
    logistic = jax.nn.sigmoid(bnv)
    active = low(bnv * logistic)
    active_slope = logistic * (1.0 + bnv * (1.0 - logistic))
    branch = dot(active, point_ref[...]) + vec2_ref[2:3]
    n3, inv3 = normalise(red_ref[...].astype(F32) + branch)
    h3 = n3 * gains[0:1] + shifts[0:1]
    fed = feed_forward(h3, bias, win[...], wout[...], shifts[2:3], hid_out, slope_sc)
    n4, inv4 = normalise(h3 + fed)
    t2 = n4 * gains[1:2] + shifts[1:2]
    t2_out[...] = n4 * gains[1:2] + shifts[1:2]
    grad = jnp.where(first, recv_ref[0, :, 0, :], own_ref[0, :, 1, :]).astype(F32).T * inside
    g_out[...] = low(grad)
    put_tiles(t_sc, 0, grad)
    even, odd = even_odd(t_sc, half, features)
    dt2 = even + odd
    dv4 = normalise_back(dt2, n4, inv4, gains[1:2])
    grad_low, inner, back = feed_back(dv4, slope_sc[...], win[...], wout[...])
    dh3 = dv4 + back
    dr3 = normalise_back(dh3, n3, inv3, gains[0:1])
    dr3_out[...] = dr3
    dpw = low(dr3)
    dbn = dot_cols(dpw, point_ref[...]) * active_slope
    dch = dbn * gain_ref[...]
    dch_out[...] = dch
    ch_out[...] = ch
    send_rows(sums_out, [row_sum(dch), row_sum(dch * ch)])
    h3_out[...] = low(h3)
    grad_out[...] = grad_low
    inner_out[...] = inner
    active_out[...] = active
    sums = (dh3 * n3, dt2 * n4, dh3, dt2, grad_low, dpw, dbn, dbn * ch)
    vec_out[...] = jnp.zeros(vec_out.shape, F32)
    for at, values in enumerate(sums):
        vec_out[at : at + 1, :] = row_sum(values)


def second_weights(
    h3_ref,
    grad_ref,
    inner_ref,
    hid_ref,
    active_ref,
    dr3_ref,
    vec_ref,
    after_ref,
    keep_out,
    send_out,
    stage,
    rest,
    vec_sc,
):
    core = lax.axis_index("section")
    inner = inner_ref[...]
    pack = Pack(stage, rest, vec_sc)
    vec_sc[...] = jnp.zeros(vec_sc.shape, F32)
    pack.matrix(dot_rows(h3_ref[...], inner))
    pack.matrix(dot_rows(grad_ref[...], hid_ref[...]))
    pack.matrix(dot_rows(active_ref[...], low(dr3_ref[...])))
    pack.bias = row_sum(inner)
    pack.vector(1, vec_ref[...])
    pack.finish(core, keep_out, send_out)


def output_rows(
    lens_ref,
    t2_ref,
    n2_ref,
    small_own,
    small_recv,
    dlin_ref,
    dgat_ref,
    dred_ref,
    red_ref,
    ml_ref,
    after_ref,
    y_out,
    mats_out,
    y_sc,
):
    core = lax.axis_index("section")
    frames, features = n2_ref.shape
    at = 5 * features % LANE
    reduced = red_ref[...]
    for left, right in (
        (dlin_ref[...], reduced),
        (dgat_ref[...], reduced),
        (ml_ref[...], dred_ref[...]),
    ):
        mats_out[:, at : at + features] = dot_rows(left, right)
        at += features
    ends = bounds_of(lens_ref, core)
    inside = jnp.where(iota((frames, 1), 0) < ends[-1], 1.0, 0.0)
    _, gains, shifts = layer_vectors(small_own, small_recv, core == 0, features)
    skip = low((n2_ref[...] * gains[1:2] + shifts[1:2]) * inside).astype(F32)
    put_even_odd(y_sc, t2_ref[...], t2_ref[...])
    y_out[...] = (get_tiles(y_sc, features) + skip) * inside


def convolution_back(
    parts,
    after,
    lens_ref,
    *refs,
):
    convolution_back_body(
        lens_ref, refs[0:parts], refs[parts : 2 * parts], *refs[2 * parts + after :]
    )


def convolution_back_body(
    lens_ref,
    stat_refs,
    sums_refs,
    dch_ref,
    ch_ref,
    dr3_ref,
    u_ref,
    lin_ref,
    sg_ref,
    n2_ref,
    small_own,
    small_recv,
    taps_ref,
    proj_ref,
    glu_ref,
    conv_ref,
    g_ref,
    dt_out,
    dlin_out,
    dgat_out,
    dred_out,
    vec_out,
    kd_out,
    t_sc,
    u_sc,
    d_sc,
    k_sc,
    c_sc,
    gate_sc,
    s_sc,
    m_sc,
):
    first = lax.axis_index("section") == 0
    frames, features = n2_ref.shape
    half = frames // 2
    ends = bounds_of(lens_ref, lax.axis_index("section"))
    inside = jnp.where(iota((frames, 1), 0) < ends[-1], 1.0, 0.0)
    joined, valid = half_masks(half, ends)
    bias, gains, shifts = layer_vectors(small_own, small_recv, first, features)
    count, centre, rho = batch_moments(stat_refs, features)
    sum1, sum2, _ = gather_rows(sums_refs, features)
    dc = (rho * valid) * (dch_ref[...] - sum1 / count - ch_ref[...] * (sum2 / count))
    tap_count = conv_ref.shape[0]
    reach = tap_count // 2
    lowest, highest = tap_ranges(half, ends, reach)
    u_sc[...] = jnp.zeros(u_sc.shape, F32)
    d_sc[...] = jnp.zeros(d_sc.shape, F32)
    k_sc[...] = jnp.zeros(k_sc.shape, F32)
    kd_out[...] = jnp.zeros(kd_out.shape, F32)
    vec_out[...] = jnp.zeros(vec_out.shape, F32)
    put_tiles(u_sc, 0, u_ref[...])
    put_tiles(d_sc, SUB, dc)
    shift_tiles(d_sc, s_sc)
    put_tiles(k_sc, 0, conv_ref[...])
    for begin in range(0, half, BLOCK):
        lead, stop = lowest[begin : begin + BLOCK], highest[begin : begin + BLOCK]
        totals = [jnp.zeros((BLOCK, LANE), F32)] * u_sc.shape[0]
        for o in range(tap_count):
            fits = (lead <= o) & (o < stop)
            at = SUB - reach + o + begin
            tap = slice(tap_count - 1 - o, tap_count - o)
            for t in range(u_sc.shape[0]):
                moved = jnp.where(fits, tap_rows_at(s_sc, t, at), 0.0)
                totals[t] = totals[t] + moved * k_sc[t, tap, :]
                met = moved * u_sc[t, begin : begin + BLOCK, :]
                met = functools.reduce(jnp.add, [met[r : r + 8] for r in range(0, BLOCK, 8)])
                if begin:
                    met = met + m_sc[t, tap.start]
                m_sc[t, tap.start] = met
        for t, total in enumerate(totals):
            c_sc[t, begin : begin + BLOCK, :] = total
    for t in range(kd_out.shape[0]):
        for o in range(tap_count):
            kd_out[t, o : o + 1, :] = row_sum(m_sc[t, o])
    du = get_tiles(c_sc, features)
    logistic = sg_ref[...]
    dlin = low(du * logistic)
    dgat = low(du * lin_ref[...] * logistic * (1.0 - logistic))
    gate_sc[:, 0:features] = dlin.astype(F32)
    gate_sc[:, features:] = dgat.astype(F32)
    dred = low(dot(low(gate_sc[...]), glu_ref[...]) + dr3_ref[...])
    dlin_out[...] = dlin
    dgat_out[...] = dgat
    dred_out[...] = dred
    for row, values in ((9, dlin), (10, dgat), (5, dred)):
        vec_out[row : row + 1, 0:features] = row_sum(values)
    dm = dot_cols(dred, proj_ref[...])
    n2 = n2_ref[...]
    put_tiles(t_sc, 0, (n2 * gains[1:2] + shifts[1:2]) * inside)
    even, odd = even_odd(t_sc, half, features)
    vec_out[6:7, 0:features] = row_sum(pltpu.roll(odd, 1, 0) * joined * dm)
    vec_out[7:8, 0:features] = row_sum(even * dm)
    vec_out[8:9, 0:features] = row_sum(odd * dm)
    carried = pltpu.roll(taps_ref[0:1] * joined * dm, half - 1, 0)
    put_even_odd(t_sc, taps_ref[1:2] * dm, taps_ref[2:3] * dm + carried)
    dt_out[...] = (g_ref[...].astype(F32) + get_tiles(t_sc, features)) * inside

def first_layer_back(
    dt_ref,
    n2_ref,
    inv2_ref,
    n1_ref,
    inv1_ref,
    hid_ref,
    slope_ref,
    small_own,
    small_recv,
    win_own,
    win_recv,
    wout_own,
    wout_recv,
    after_ref,
    dr1_out,
    keep_out,
    send_out,
    win,
    wout,
    stage,
    rest,
    vec_sc,
):
    core = lax.axis_index("section")
    first = core == 0
    choose(first, win_own, win_recv, win)
    choose(first, wout_own, wout_recv, wout)
    bias, gains, shifts = layer_vectors(small_own, small_recv, first, win.shape[0])
    pack = Pack(stage, rest, vec_sc)
    vec_sc[...] = jnp.zeros(vec_sc.shape, F32)
    dt = dt_ref[...]
    n2 = n2_ref[...]
    dv2 = normalise_back(dt, n2, inv2_ref[...], gains[1:2])
    pack.vector(2, row_sum(dt * n2))
    pack.vector(4, row_sum(dt))
    n1 = n1_ref[...]
    h1 = low(n1 * gains[0:1] + shifts[0:1])
    grad_low, inner, back = feed_back(dv2, slope_ref[...], win[...], wout[...])
    dh1 = dv2 + back
    pack.matrix(dot_rows(h1, inner))
    pack.matrix(dot_rows(grad_low, hid_ref[...]))
    pack.bias = row_sum(inner)
    pack.vector(5, row_sum(grad_low))
    pack.vector(1, row_sum(dh1 * n1))
    pack.vector(3, row_sum(dh1))
    dr1_out[...] = normalise_back(dh1, n1, inv1_ref[...], gains[0:1])
    pack.finish(core, keep_out, send_out)


def attention_back(
    heads,
    dr1_ref,
    qu_ref,
    qw_ref,
    k_ref,
    v_ref,
    p_ref,
    a_ref,
    wo_ref,
    *refs,
):
    dqr_out, dkv_out, dp_out, sums_out = refs[-4:]
    frames = dr1_ref.shape[0]
    head = dr1_ref.shape[1] // HEADS
    width = len(heads) * LANE
    scale = head**-0.5
    dr1_low = low(dr1_ref[...])
    flip = flip_rows(frames)
    for at, h in enumerate(heads):
        cols = slice(h * LANE, (h + 1) * LANE)
        here = slice(at * LANE, (at + 1) * LANE)
        weights = a_ref[h]
        grad = low(dot_cols(dr1_low, wo_ref[cols, :]))
        weights_f = weights.astype(F32)
        product = weights_f * dot_cols(grad, v_ref[:, cols])
        ds = low(product - weights_f * jnp.sum(product, axis=-1, keepdims=True))
        dkv_out[:, width + at * LANE : width + (at + 1) * LANE] = low(dot_rows(weights, grad))
        dkv_out[:, here] = low(scale * dot_rows(ds, qu_ref[:, cols]))
        dsr = low(dot(flip, ds))
        qwr = low(dot(flip, qw_ref[:, cols]))
        wide = jnp.concatenate([jnp.zeros((frames, frames), BF16), dsr], axis=1)
        band = pltpu.roll(wide, frames + 1, 1, stride=1, stride_axis=0)
        dqu = scale * dot(dsr, k_ref[:, cols])
        dqw = scale * dot(band, p_ref[:, cols])
        dqr_out[:, here] = low(dqu + dqw)
        dp_out[:, here] = low(scale * dot_rows(band, qwr))
        sums_out[0:1, here] = row_sum(dqu + dqw)
        sums_out[1:2, here] = row_sum(dkv_out[:, width + at * LANE : width + (at + 1) * LANE])
        sums_out[2:3, here] = row_sum(dqu)
        sums_out[3:4, here] = row_sum(dqw)


def flip_rows(frames):
    hit = iota((frames, frames), 0) + iota((frames, frames), 1) == frames - 1
    return jnp.where(hit, 1.0, 0.0).astype(BF16)


def attention_weights_back(
    dr1_ref,
    xt_ref,
    o_ref,
    table_ref,
    mats_ref,
    vec_ref,
    kd_ref,
    *refs,
):
    parts, after_ref = (refs[0:4], refs[4:8]), refs[8]
    dq_out, dkv_out, keep_out, send_out, stage, rest, vec_sc = refs[9:]
    core = lax.axis_index("section")
    frames, features = dr1_ref.shape
    width = HEADS * LANE
    pack = Pack(stage, rest, vec_sc)
    vec_sc[...] = vec_ref[...]
    begin = 5 * features // LANE * LANE
    stage[:, begin : begin + mats_ref.shape[1]] = mats_ref[...]
    dr1_low = low(dr1_ref[...])
    unselect = head_unselect(features, features // HEADS)
    pack.vector(2, row_sum(dr1_low))
    pack.matrix(dot_rows(unselect, low(dot_rows(o_ref[...], dr1_low))))
    half = width // 2
    flip = flip_rows(frames)
    for at, (dqr, dkv, dp, sums) in enumerate(parts):
        here = slice(at * half, (at + 1) * half)
        dq_out[:, here] = low(dot(flip, dqr[...]))
        dkv_out[:, here] = dkv[:, 0:half]
        dkv_out[:, width + at * half : width + (at + 1) * half] = dkv[:, half:]
    sums = jnp.concatenate([sums[0:4, :] for _, _, _, sums in parts], axis=1)
    sums = dot(sums, unselect.astype(F32), precision=lax.Precision.HIGHEST)
    pack.vector(0, sums[0:2])
    pack.vector(3, sums[2:4])
    x_turned = xt_ref[...]
    pack.matrix(dot(low(dot(x_turned, dq_out[...])), unselect))
    pack.matrix(dot(low(dot(x_turned, dkv_out[:, 0:width])), unselect))
    pack.matrix(dot(low(dot(x_turned, dkv_out[:, width:])), unselect))
    dp = jnp.concatenate([dp[...] for _, _, dp, _ in parts], axis=1)
    pack.matrix(dot(low(dot_rows(table_ref[...], dp)), unselect))
    pack.used = 8 * features
    pack.finish(core, keep_out, send_out, [kd_ref[t] for t in range(kd_ref.shape[0])])


def input_back(dr1_ref, dq_ref, dkv_ref, w_ref, y_ref, after_ref, rows_out, cross_out):
    core = lax.axis_index("section")
    width = dq_ref.shape[1]
    dx = dr1_ref[...] + dot_cols(dq_ref[...], w_ref[:, 0:width])
    dx = (dx + dot_cols(dkv_ref[...], w_ref[:, width:])).T
    y = y_ref[...].T
    rows_out[...] = jnp.where(core == 0, dx, y)
    cross_out[...] = jnp.where(core == 0, y, dx)


def place_of(bit, core):
    return 1 - bit if bit < 2 and core == 1 else bit


def digits(bits, core):
    row = lax.axis_index("rows")
    digit = jnp.int32(0)
    for bit in bits:
        place = jnp.where(core == 0, place_of(bit, 0), place_of(bit, 1))
        digit = (digit << 1) | ((row >> place) & 1)
    return digit


def partner(values, bits, m):
    peers = lax.axis_size("rows")
    pairs = []
    for core in range(2):
        flips = [1 << place_of(b, core) for at, b in enumerate(reversed(bits)) if m >> at & 1]
        pairs += [(core * peers + r, core * peers + (r ^ sum(flips))) for r in range(peers)]
    return lax.ppermute(values, ("section", "rows"), pairs)


def step_kernel(bits, join, count, *refs):
    parts = refs[:count]
    if bits:
        outs = refs[-(1 << len(bits)) :]
        rows = outs[0].shape[0]
        mine = digits(bits, lax.axis_index("section"))
        for m, out in enumerate(outs):
            span = pl.ds(pl.multiple_of((mine ^ m) * rows, SUB), rows)
            out[...] = low(sum(part[span, :].astype(F32) for part in parts))
    elif join:
        rows = parts[0].shape[0]
        for at, part in enumerate(parts):
            refs[-1][at * rows : (at + 1) * rows, :] = part[...]
    else:
        refs[-1][...] = low(sum(part[...].astype(F32) for part in parts))


def step(parts, after, name, bits=(), join=False):
    rows = parts[0].shape[0]
    if bits:
        outs = [shape((rows >> len(bits), LANE), BF16)] * (1 << len(bits))
    else:
        outs = [shape((rows * (len(parts) if join else 1), LANE), BF16)]
    return call(
        functools.partial(step_kernel, bits, join, len(parts)),
        name,
        [VMEM] * len(parts) + [ANY] * len(after),
        outs,
        limit=STEP_LIMIT,
        cost=STEP_COST,
    )(*parts, *after)


class Chain:
    def __init__(self, name, keep, send, splits, whole, gathers):
        self.name = name
        self.parts = [keep, swap(send)]
        self.summing = True
        self.plan = [("split", bits) for bits in splits]
        self.plan += [("whole", bits) for bits in whole]
        self.plan += [("gather", bits) for bits in gathers] + [("last", ())]

    def advance(self, after=()):
        kind, bits = self.plan.pop(0)
        name = "_".join([self.name, kind, *map(str, bits)])
        if kind == "last":
            (send,) = step(self.parts[1:], after, name, join=True)
            self.pieces = [self.parts[0], send, self.early, swap(send)]
            return send
        if kind == "split":
            blocks = step(self.parts, after, name, bits=bits)
            self.parts = [blocks[0]] + [partner(b, bits, m + 1) for m, b in enumerate(blocks[1:])]
            return blocks[1]
        (block,) = step(self.parts, after, name, join=not self.summing)
        self.summing = kind == "whole"
        self.parts = [block] + [partner(block, bits, m) for m in range(1, 1 << len(bits))]
        if len(self.plan) == 1:
            self.early = swap(block)
        return block


def reorder(pieces, target, bits):
    core = lax.axis_index("section")
    half = target.shape[0] // 2
    block = half >> bits
    for side in range(2):
        owner = core if side == 0 else 1 - core
        mine = digits(range(bits), owner)
        at = 0
        for piece in pieces[2 * side : 2 * side + 2]:
            for first in range(0, piece.shape[0], block):
                begin = pl.multiple_of(owner * half + (mine ^ at) * block, SUB)
                target[pl.ds(begin, block), :] = piece[first : first + block, :]
                at += 1


def spread_tiles(pack, stage):
    rows, wide = stage.shape
    tall = rows // SUB * SUB
    tail = rows - tall
    tiles = wide // LANE
    at = tall * tiles
    rest = pack[at : at + up(tail * tiles, SUB), :].astype(F32)
    for t in range(tiles):
        cols = slice(t * LANE, (t + 1) * LANE)
        stage[0:tall, cols] = pack[t * tall : (t + 1) * tall, :].astype(F32)
        stage[tall:rows, cols] = rest[t * tail : (t + 1) * tail]
    return at + rest.shape[0]


def vectors_at(ref, row, features, rows=SUB):
    tiles = up(features, LANE) // LANE
    pieces = [ref[row + t * rows : row + (t + 1) * rows, :] for t in range(tiles)]
    return jnp.concatenate(pieces, axis=1).astype(F32)[:, 0:features], row + tiles * rows


def bias_at(ref, row, cols):
    lines = ref[row : row + SUB, :].astype(F32)
    pieces = [lines[t : t + 1] for t in range(up(cols, LANE) // LANE)]
    return jnp.concatenate(pieces, axis=1)[:, 0:cols]


def unpack_one(
    bits,
    piece0,
    piece1,
    piece2,
    piece3,
    after_ref,
    point_out,
    gain_out,
    win_out,
    wout_out,
    bias_out,
    vec_out,
    pack,
    stage,
):
    reorder((piece0, piece1, piece2, piece3), pack, bits)
    at = spread_tiles(pack, stage)
    features = point_out.shape[0]
    inner = win_out.shape[2]
    win_out[:, 0, :] = stage[:, 0:inner]
    wout_out[:, 0, :] = stage[:, inner : 2 * inner]
    point_out[...] = stage[:, 2 * inner : 2 * inner + features]
    rows, at = vectors_at(pack, at, features)
    vec_out[...] = rows
    gain_out[...] = rows[8:9]
    bias_out[...] = bias_at(pack, at, inner)


def unpack_two(
    bits,
    win_ref,
    wout_ref,
    bias_ref,
    vec_ref,
    piece0,
    piece1,
    piece2,
    piece3,
    after_ref,
    norm_out,
    win_out,
    bias_out,
    wout_out,
    block_out,
    pack,
    stage,
):
    core = lax.axis_index("section")
    reorder((piece0, piece1, piece2, piece3), pack, bits)
    at = spread_tiles(pack, stage)
    features = win_out.shape[0]
    inner = win_out.shape[2]

    @pl.when(core == 0)
    def _():
        win_out[:, 0, :] = stage[:, 0:inner]
        wout_out[:, 0, :] = stage[:, inner : 2 * inner]

    @pl.when(core != 0)
    def _():
        win_out[...] = win_ref[...]
        wout_out[...] = wout_ref[...]

    rows, at = vectors_at(pack, at, features)
    bias_out[...] = jnp.where(core == 0, bias_at(pack, at, inner), bias_ref[...])
    mine = jnp.where(core == 0, rows, vec_ref[...])
    norm_out[0] = mine[1:3]
    for row in range(3):
        block_out[row] = mine[3 + row : 4 + row]


def unpack_three(
    bits,
    vec_ref,
    piece0,
    piece1,
    piece2,
    piece3,
    after_ref,
    attn_in_out,
    pos_out,
    attn_out_out,
    glu_out,
    proj_out,
    conv_out,
    vec_out,
    taps_out,
    vec2_out,
    pack,
    stage,
):
    reorder((piece0, piece1, piece2, piece3), pack, bits)
    at = spread_tiles(pack, stage)
    features = pos_out.shape[0]
    attn_out_out[...] = stage[:, 0:features]
    attn_in_out[...] = stage[:, features : 4 * features]
    pos_out[...] = stage[:, 4 * features : 5 * features]
    glu_out[0:features, :] = stage[:, 5 * features : 6 * features]
    glu_out[features:, :] = stage[:, 6 * features : 7 * features]
    proj_out[...] = stage[:, 7 * features : 8 * features]
    taps = conv_out.shape[0]
    rows, at = vectors_at(pack, at, features, up(taps, SUB))
    conv_out[...] = rows[0:taps]
    rows, at = vectors_at(pack, at, features)
    vec_out[...] = rows[0:6]
    taps_out[...] = rows[6:9]
    vec2_out[0:2, :] = rows[9:11]
    vec2_out[2:4, :] = vec_ref[6:8, :]


def join_rows(rows_ref, cross_ref, after_ref, boundary_out, mark_out):
    mark_out[...] = jnp.zeros(mark_out.shape, F32)
    core = lax.axis_index("section")
    rows, cross = rows_ref[...], cross_ref[...]
    boundary_out[0, :, 0, :] = jnp.where(core == 0, rows, cross)
    boundary_out[0, :, 1, :] = jnp.where(core == 0, cross, rows)


def shape(dims, dtype=F32):
    return jax.ShapeDtypeStruct(dims, dtype)


SMEM = pl.BlockSpec(memory_space=pltpu.SMEM)
VMEM = pl.BlockSpec(memory_space=pltpu.VMEM)
ANY = pl.BlockSpec(memory_space=pl.ANY)
HBM = pl.BlockSpec(memory_space=pltpu.HBM)


def call(kernel, name, in_specs, out_shape, scratch=(), limit=None, cost=None):
    cost = KERNEL_COST if cost is None else cost
    return pl.pallas_call(
        kernel,
        name=name,
        in_specs=in_specs,
        out_specs=[VMEM] * len(out_shape),
        out_shape=out_shape,
        scratch_shapes=list(scratch),
        compiler_params=pltpu.CompilerParams(vmem_limit_bytes=limit or VMEM_LIMIT),
        cost_estimate=pl.CostEstimate(flops=400 * cost, bytes_accessed=cost, transcendentals=0),
    )


def position_table(frames, features):
    distance = (frames - np.arange(2 * frames)).astype(np.float32)
    frequency = np.exp(
        np.arange(0, features, 2).astype(np.float32) * np.float32(-math.log(10000.0) / features)
    ).astype(np.float32)
    angles = (distance[:, None] * frequency[None, :]).astype(np.float64)
    table = np.stack([np.sin(angles), np.cos(angles)], axis=-1).reshape(2 * frames, features)
    return jnp.asarray(table.astype(np.float32), BF16)


def in_hbm(values):
    return pltpu.with_memory_space_constraint(values, pltpu.HBM)


def swap(values):
    return lax.ppermute(values, "section", [(0, 1), (1, 0)])


def share(values):
    bits = lax.axis_size("rows").bit_length() - 1
    parts = [values]
    for begin in range(0, bits, 2):
        values = functools.reduce(jnp.add, parts)
        parts = [values]
        for step in reversed(range(1, 1 << min(2, bits - begin))):
            pairs = [(r, r ^ (step << begin)) for r in range(1 << bits)]
            parts.append(lax.ppermute(values, "rows", pairs))
    return parts, values


def shards(
    boundary,
    utt_lengths,
    attn_in,
    pos_proj,
    attn_out,
    first_vectors,
    reduce_taps,
    reduce_proj,
    glu_in,
    conv_taps,
    second_vectors,
    bn_gain,
    point_proj,
    ffn_in,
    ffn_bias,
    ffn_out,
    norm_gain,
    block_vectors,
):
    peers = lax.axis_size("rows")
    _, batches, frames, features = boundary.shape
    half = frames // 2
    inner = ffn_in.shape[2]
    width = HEADS * LANE
    tiles = up(features, LANE) // LANE
    tap_rows = up(conv_taps.shape[0], SUB)
    cols = (2 * inner + features, 2 * inner, 8 * features)
    wide = [up(count, LANE) for count in cols]
    others = (0, 0, tap_rows * tiles)
    heights = [
        pack_heights(features, count, bias, other)
        for count, bias, other in zip(cols, (inner, inner, 0), others)
    ]
    pack_rows = [up(height[2], peers * SUB) for height in heights]
    row_bits = peers.bit_length() - 1
    singles = [(bit,) for bit in range(row_bits - 1)]
    pairs = [tuple(range(at, min(at + 2, row_bits))) for at in range(0, row_bits, 2)]
    by_one = (singles, [(row_bits - 1,)], singles[::-1])
    by_two = (pairs, [], pairs[::-1])
    table = position_table(frames, features)
    turned = jnp.transpose(boundary, (0, 3, 1, 2))
    wout_own = jnp.transpose(ffn_out, (0, 2, 1))
    shift_own = jnp.transpose(block_vectors, (1, 0, 2))
    glu_turned = glu_in.T

    recv = swap(turned)
    weights = (ffn_in, swap(ffn_in), wout_own, swap(wout_own))

    def scratch(*dims, dtype=F32):
        return pltpu.VMEM(dims, dtype)

    p, w_pad, wo_pad, vectors, small = call(
        prepare,
        "prepare",
        [HBM] * 8,
        [
            shape((2 * frames, width), BF16),
            shape((features, 3 * width), BF16),
            shape((width, features), BF16),
            shape((first_vectors.shape[0], width)),
            shape((8, inner)),
        ],
        [
            scratch(*attn_in.shape, dtype=BF16),
            scratch(*pos_proj.shape, dtype=BF16),
            scratch(*attn_out.shape, dtype=BF16),
            scratch(*first_vectors.shape),
            scratch(*table.shape, dtype=BF16),
            scratch(*ffn_bias.shape),
            scratch(*norm_gain.shape),
            scratch(*shift_own.shape),
            pltpu.SemaphoreType.DMA((8,)),
        ],
        cost=10**7,
    )(
        *map(in_hbm, (attn_in, pos_proj, attn_out, first_vectors, table)),
        *map(in_hbm, (ffn_bias, norm_gain, shift_own)),
    )
    small = (small, swap(small))
    xt, qu, qw, k, v, a, o, n1, inv1 = call(
        attention_forward,
        "attention_forward",
        [SMEM] + [VMEM] * 7,
        [
            shape((features, frames), BF16),
            shape((frames, width), BF16),
            shape((frames, width), BF16),
            shape((frames, width), BF16),
            shape((frames, width), BF16),
            shape((HEADS, frames, frames), BF16),
            shape((frames, width), BF16),
            shape((frames, features)),
            shape((frames, 1)),
        ],
    )(
        utt_lengths,
        turned,
        recv,
        p,
        w_pad,
        wo_pad,
        vectors,
        first_vectors,
    )

    weights_scratch = [scratch(features, inner, dtype=BF16)] * 2
    rows_scratch = scratch(tiles, frames, LANE)
    edge_scratch = scratch(tiles, half + 2 * SUB, LANE)
    taps_scratch = scratch(tiles, tap_rows, LANE)
    shift_scratch = scratch(8, tiles, half + 2 * SUB - 8, LANE)
    vec_scratch = scratch(SUB, tiles * LANE)

    def pack_scratch(index):
        return scratch(pack_rows[index], LANE, dtype=BF16)

    def stage_scratch(index):
        return scratch(features, wide[index])

    def pack_stages(index):
        return [stage_scratch(index), scratch(heights[index][1], LANE), vec_scratch]

    def pack_halves(index):
        return [shape((pack_rows[index] // 2, LANE), BF16)] * 2

    hid, slope, n2, inv2, ml, red, lin, sg, u, c, stat = call(
        convolution_forward,
        "convolution_forward",
        [SMEM] + [VMEM] * 13,
        [
            shape((frames, inner), BF16),
            shape((frames, inner), BF16),
            shape((frames, features)),
            shape((frames, 1)),
            shape((half, features), BF16),
            shape((half, features), BF16),
            shape((half, features)),
            shape((half, features)),
            shape((half, features)),
            shape((half, features)),
            shape((8, LANE)),
        ],
        weights_scratch + [rows_scratch, edge_scratch, taps_scratch, scratch(tiles, half, LANE), shift_scratch],
    )(
        utt_lengths,
        n1,
        *small,
        *weights,
        first_vectors,
        reduce_taps,
        reduce_proj,
        glu_turned,
        conv_taps,
        second_vectors,
    )
    stat, _ = share(stat)
    g, dch, ch, dr3, sums, t2, h3, grad4, inner4, hid4, active, vec1 = call(
        functools.partial(second_layer, len(stat)),
        "second_layer",
        [SMEM] + [VMEM] * (13 + len(stat)),
        [
            shape((frames, features), BF16),
            shape((half, features)),
            shape((half, features)),
            shape((half, features)),
            shape((8, LANE)),
            shape((half, features)),
            shape((half, features), BF16),
            shape((half, features), BF16),
            shape((half, inner), BF16),
            shape((half, inner), BF16),
            shape((half, features), BF16),
            shape((8, features)),
        ],
        weights_scratch + [rows_scratch, scratch(half, inner, dtype=BF16)],
    )(
        utt_lengths,
        *stat,
        c,
        red,
        *small,
        *weights,
        point_proj,
        second_vectors,
        bn_gain[None],
        turned,
        recv,
    )
    sums, sent = share(sums)
    chains = {}
    made = {}

    def weights_two(mark):
        keep, send = call(
            second_weights,
            "second_weights",
            [VMEM] * 7 + [ANY],
            pack_halves(0),
            pack_stages(0),
        )(h3, grad4, inner4, hid4, active, dr3, vec1, mark)
        chains["1"] = Chain("one", keep, send, *by_one)
        return keep

    def conv_back(mark):
        made["conv"] = call(
            functools.partial(convolution_back, len(stat), 1),
            "convolution_back",
            [SMEM] + [VMEM] * (2 * len(stat)) + [ANY] + [VMEM] * 14,
            [
                shape((frames, features)),
                shape((half, features), BF16),
                shape((half, features), BF16),
                shape((half, features), BF16),
                shape((SUB, tiles * LANE)),
                shape((tiles, tap_rows, LANE)),
            ],
            [
                rows_scratch,
                scratch(tiles, half, LANE),
                edge_scratch,
                taps_scratch,
                scratch(tiles, half, LANE),
                scratch(half, 2 * features),
                shift_scratch,
                scratch(tiles, tap_rows, 8, LANE),
            ],
        )(
            utt_lengths,
            *stat,
            *sums,
            mark,
            dch,
            ch,
            dr3,
            u,
            lin,
            sg,
            n2,
            *small,
            reduce_taps,
            reduce_proj,
            glu_turned,
            conv_taps,
            g,
        )
        return made["conv"][0]

    def rows_out(mark):
        made["y"], made["mats"] = call(
            output_rows,
            "output_rows",
            [SMEM] + [VMEM] * 9 + [ANY],
            [
                shape((frames, features)),
                shape((features, up(5 * features % LANE + 3 * features, LANE))),
            ],
            [rows_scratch],
        )(utt_lengths, t2, n2, *small, *made["conv"][1:4], red, ml, mark)
        return made["y"]

    def first_back(mark):
        dr1, keep, send = call(
            first_layer_back,
            "first_layer_back",
            [VMEM] * 13 + [ANY],
            [shape((frames, features))] + pack_halves(1),
            weights_scratch + pack_stages(1),
        )(made["conv"][0], n2, inv2, n1, inv1, hid, slope, *small, *weights, mark)
        made["dr1"] = dr1
        chains["2"] = Chain("two", keep, send, *by_one)
        return dr1

    def heads_back(heads, mark):
        wide_heads = len(heads) * LANE
        made[heads[0]] = call(
            functools.partial(attention_back, heads),
            "attention_back",
            [VMEM] * 8 + [ANY],
            [
                shape((frames, wide_heads), BF16),
                shape((frames, 2 * wide_heads), BF16),
                shape((2 * frames, wide_heads), BF16),
                shape((8, wide_heads)),
            ],
        )(made["dr1"], qu, qw, k, v, p, a, wo_pad, mark)
        return made[heads[0]][0]

    def weights_one(mark):
        parts = made[0] + made[HEADS // 2]
        made["dq"], made["dkv"], keep, send = call(
            attention_weights_back,
            "attention_weights_back",
            [VMEM] * 15 + [ANY],
            [shape((frames, width), BF16), shape((frames, 2 * width), BF16)] + pack_halves(2),
            pack_stages(2),
        )(made["dr1"], xt, o, table, made["mats"], *made["conv"][4:], *parts, mark)
        chains["3"] = Chain("three", keep, send, *by_one)
        return keep

    def rows_back(mark):
        made["rows"], cross = call(
            input_back,
            "input_back",
            [VMEM] * 5 + [ANY],
            [shape((features, frames))] * 2,
        )(made["dr1"], made["dq"], made["dkv"], w_pad, made["y"], mark)
        made["cross"] = swap(cross)
        return made["rows"]

    def rows_join(mark):
        made["boundary"], mark = call(
            join_rows,
            "join_rows",
            [VMEM] * 2 + [ANY],
            [shape((1, features, batches, frames)), shape((8, LANE))],
        )(made["rows"], made["cross"], mark)
        return mark

    def open_one(mark):
        made["point"], made["gain"], *made["one"] = call(
            functools.partial(unpack_one, row_bits - 1),
            "unpack_one",
            [VMEM] * 4 + [ANY],
            [
                shape(point_proj.shape),
                shape((1, features)),
                shape((features, 1, inner)),
                shape((features, 1, inner)),
                shape(ffn_bias.shape),
                shape((SUB, features)),
            ],
            [pack_scratch(0), stage_scratch(0)],
        )(*chains["1"].pieces, mark)
        return made["one"][3]

    def open_two(mark):
        made["two"] = call(
            functools.partial(unpack_two, row_bits - 1),
            "unpack_two",
            [VMEM] * 8 + [ANY],
            [
                shape(norm_gain.shape),
                shape((features, 1, inner)),
                shape(ffn_bias.shape),
                shape((features, 1, inner)),
                shape(shift_own.shape),
            ],
            [pack_scratch(1), stage_scratch(1)],
        )(*made["one"], *chains["2"].pieces, mark)
        return made["two"][0]

    def open_three(mark):
        made["three"] = call(
            functools.partial(unpack_three, row_bits - 1),
            "unpack_three",
            [VMEM] * 5 + [ANY],
            [
                shape(attn_in.shape),
                shape(pos_proj.shape),
                shape(attn_out.shape),
                shape(glu_turned.shape),
                shape(reduce_proj.shape),
                shape(conv_taps.shape),
                shape(first_vectors.shape),
                shape(reduce_taps.shape),
                shape(second_vectors.shape),
            ],
            [pack_scratch(2), stage_scratch(2)],
        )(made["one"][3], *chains["3"].pieces, mark)
        return made["three"][6]

    runs = dict(K=weights_two, E=conv_back, F=first_back, G=rows_out, C=weights_one, D=rows_back)
    runs.update(J=rows_join, U=open_one, V=open_two, W=open_three)
    runs["A"] = functools.partial(heads_back, range(HEADS // 2))
    runs["B"] = functools.partial(heads_back, range(HEADS // 2, HEADS))
    order = ORDER
    spare = len(singles) - 3
    for number in "123":
        at = order.index({"1": "K", "2": "F", "3": "D"}[number]) + 1
        at = order.index(number, at)
        order = order[:at] + number * (2 * spare) + order[at:]
    mark = sent
    for letter in order:
        mark = runs[letter](mark) if letter in runs else chains[letter].advance([mark])
    norm_out, win_out, bias_out, wout_out, block_out = made["two"]
    attn_in_out, pos_out, attn_out_out, glu_out, proj_out, conv_out = made["three"][0:6]
    vec_out, taps_out, vec2_out = made["three"][6:]
    return (
        jnp.transpose(made["boundary"], (0, 2, 3, 1)),
        attn_in_out,
        pos_out,
        attn_out_out,
        vec_out,
        taps_out,
        proj_out,
        glu_out.T,
        conv_out,
        vec2_out,
        made["gain"][0],
        made["point"],
        jnp.transpose(win_out, (1, 0, 2)),
        bias_out,
        jnp.transpose(wout_out, (1, 2, 0)),
        norm_out,
        jnp.transpose(block_out, (1, 0, 2)),
    )


def solution(mesh):
    split = (
        P("section", None, None),
        P("section", None),
        P("section", None, None),
        P("section", None, None),
        P("section", None, None),
    )
    return jax.shard_map(
        shards,
        mesh=mesh,
        in_specs=(P("section", None, "rows", None), P(None, "rows", None)) + (P(),) * 11 + split,
        out_specs=(P("section", None, "rows", None),) + (P(),) * 11 + split,
        check_vma=False,
    )
```

```python
import functools
import math

import jax
import jax.numpy as jnp
import numpy as np
from jax import lax
from jax.experimental import pallas as pl
from jax.experimental.pallas import tpu as pltpu
from jax.sharding import PartitionSpec as P

HEADS = 4
LANE = 128
SUB = 16
BLOCK = 64
EPSILON = 1e-05
MASKED = -1e30
F32 = jnp.float32
BF16 = jnp.bfloat16
VMEM_LIMIT = 28 << 20
STEP_LIMIT = 8 << 20
STEP_COST = 12 * 10**6
KERNEL_COST = 12 * 10**6
ORDER = "KE1FG2AB1C2D1321321J321321321323UV3W"


def up(value, step):
    return -(-value // step) * step


def low(values):
    return values.astype(BF16)


def dot(left, right, dims=((1,), (0,)), precision=None):
    return lax.dot_general(
        left, right, (dims, ((), ())), preferred_element_type=F32, precision=precision
    )


def dot_rows(left, right):
    return dot(left, right, ((0,), (0,)))


def dot_cols(left, right):
    return dot(left, right, ((1,), (1,)))


def row_sum(values):
    return jnp.sum(values.astype(F32), axis=0, keepdims=True)


def normalise(values):
    centre = values - jnp.mean(values, axis=-1, keepdims=True)
    inverse = lax.rsqrt(jnp.mean(centre * centre, axis=-1, keepdims=True) + EPSILON)
    return centre * inverse, inverse


def normalise_back(grad, normed, inverse, gain):
    scaled = grad * gain
    first = jnp.mean(scaled, axis=-1, keepdims=True)
    second = jnp.mean(scaled * normed, axis=-1, keepdims=True)
    return inverse * (scaled - first - normed * second)


def bounds_of(lens_ref, batch):
    ends = []
    total = jnp.int32(0)
    for slot in range(lens_ref.shape[-1]):
        total = total + lens_ref[batch, 0, slot]
        ends.append(total)
    return ends


def segment_of(position, ends):
    segment = jnp.zeros(position.shape, jnp.int32)
    for end in ends:
        segment = segment + (position >= end).astype(jnp.int32)
    return segment


def iota(shape, axis):
    return lax.broadcasted_iota(jnp.int32, shape, axis)


def padded_column(index, head):
    within = index & (LANE - 1)
    return jnp.where(within < head, (index >> (LANE.bit_length() - 1)) * head + within, -1 << 20)


def head_select(rows, base, head, dtype):
    wanted = padded_column(iota((1, HEADS * LANE), 1), head) - base
    hit = iota((rows, HEADS * LANE), 0) == wanted
    return jnp.where(hit, 1.0, 0.0).astype(dtype)


def head_unselect(cols, head):
    wanted = padded_column(iota((HEADS * LANE, 1), 0), head)
    hit = iota((HEADS * LANE, cols), 1) == wanted
    return jnp.where(hit, 1.0, 0.0).astype(BF16)


def choose(use_own, own_ref, other_ref, target):
    @pl.when(use_own)
    def _():
        target[...] = own_ref[0]

    @pl.when(jnp.logical_not(use_own))
    def _():
        target[...] = other_ref[0]


def pack_heights(features, cols, bias_cols, others):
    tall = features // SUB * SUB
    tiles = up(cols, LANE) // LANE
    rest = up((features - tall) * tiles, SUB)
    vectors = up(features, LANE) // LANE * SUB + (SUB if bias_cols else 0)
    return tall, rest, tall * tiles + rest + others + vectors


class Pack:
    def __init__(self, stage_ref, rest_ref, vec_ref):
        self.stage, self.rest, self.vec = stage_ref, rest_ref, vec_ref
        self.col = 0
        self.used = 0
        self.bias = None

    def matrix(self, values):
        rows, cols = values.shape
        self.stage[0:rows, self.col : self.col + cols] = values
        self.col += cols
        self.used = max(self.used, self.col)

    def vector(self, at, values):
        self.vec[at : at + values.shape[0], 0 : values.shape[1]] = values

    def finish(self, core, keep_out, send_out, others=()):
        rows, wide = self.stage.shape
        if self.used < wide:
            self.stage[:, self.used : wide] = jnp.zeros((rows, wide - self.used), F32)
        tall = rows // SUB * SUB
        tail = rows - tall
        self.rest[...] = jnp.zeros(self.rest.shape, F32)
        for t in range(wide // LANE):
            part = self.stage[tall:rows, t * LANE : (t + 1) * LANE]
            self.rest[t * tail : (t + 1) * tail, :] = part
        blocks = [lambda t=t: self.stage[0:tall, t * LANE : (t + 1) * LANE] for t in range(wide // LANE)]
        blocks += [lambda: self.rest[...]] + [lambda values=values: values for values in others]
        for t in range(self.vec.shape[1] // LANE):
            blocks.append(lambda t=t: self.vec[:, t * LANE : (t + 1) * LANE])
        if self.bias is not None:
            cols = self.bias.shape[1]
            lines = [self.bias[:, at : at + LANE] for at in range(0, cols, LANE)]
            lines[-1] = jnp.pad(lines[-1], ((0, 0), (0, LANE - lines[-1].shape[1])))
            lines.append(jnp.zeros((SUB - len(lines), LANE), F32))
            blocks.append(lambda: jnp.concatenate(lines, axis=0))

        @pl.when(core == 0)
        def _():
            self.place(keep_out, send_out, blocks)

        @pl.when(core != 0)
        def _():
            self.place(send_out, keep_out, blocks)

    def place(self, low_out, high_out, blocks):
        half = low_out.shape[0]
        row = 0

        def put(values):
            nonlocal row
            rows = values.shape[0]
            cut = min(max(half - row, 0), rows)
            if cut:
                low_out[row : row + cut, :] = low(values[0:cut])
            if cut < rows:
                high_out[row + cut - half : row + rows - half, :] = low(values[cut:])
            row += rows

        for block in blocks:
            put(block())
        if row < 2 * half:
            put(jnp.zeros((2 * half - row, LANE), F32))


def prepare(
    attn_in_hbm,
    pos_proj_hbm,
    attn_out_hbm,
    vec_hbm,
    table_hbm,
    bias_hbm,
    gain_hbm,
    shift_hbm,
    p_out,
    w_out,
    wo_out,
    vectors_out,
    small_out,
    attn_in_ref,
    pos_proj_ref,
    attn_out_ref,
    vec_ref,
    table_ref,
    bias_ref,
    gain_ref,
    shift_ref,
    sem,
):
    sources = (pos_proj_hbm, table_hbm, attn_in_hbm, attn_out_hbm, vec_hbm)
    sources += (bias_hbm, gain_hbm, shift_hbm)
    targets = (pos_proj_ref, table_ref, attn_in_ref, attn_out_ref, vec_ref)
    targets += (bias_ref, gain_ref, shift_ref)
    copies = [
        pltpu.make_async_copy(source, target, sem.at[at])
        for at, (source, target) in enumerate(zip(sources, targets))
    ]
    for copy in copies:
        copy.start()
    features = attn_out_ref.shape[0]
    head = features // HEADS
    width = HEADS * LANE
    select = head_select(features, 0, head, BF16)
    copies[0].wait()
    pos = low(dot(pos_proj_ref[...], select))
    copies[1].wait()
    p_out[...] = low(dot(table_ref[...], pos))
    copies[2].wait()
    for part in range(3):
        begin = part * features
        floor = begin // LANE * LANE
        stop = min(up(begin + features, LANE), 3 * features)
        piece = attn_in_ref[:, floor:stop]
        chosen = head_select(stop - floor, floor - begin, head, BF16)
        w_out[:, part * width : (part + 1) * width] = low(dot(piece, chosen))
    copies[3].wait()
    wo_out[...] = low(dot(head_unselect(features, head), attn_out_ref[...]))
    copies[4].wait()
    vectors_out[...] = dot(
        vec_ref[...], head_select(features, 0, head, F32), precision=lax.Precision.HIGHEST
    )
    for copy in copies[5:]:
        copy.wait()
    small_out[...] = jnp.zeros(small_out.shape, F32)
    small_out[0:1, :] = bias_ref[...]
    small_out[1:3, 0:features] = gain_ref[0]
    for at in range(3):
        small_out[3 + at : 4 + at, 0:features] = shift_ref[at]


def attention_forward(
    lens_ref,
    own_ref,
    recv_ref,
    p_ref,
    w_ref,
    wo_ref,
    vectors_ref,
    vec_ref,
    xt_out,
    qu_out,
    qw_out,
    k_out,
    v_out,
    a_out,
    o_out,
    n1_out,
    inv1_out,
):
    core = lax.axis_index("section")
    features, frames = xt_out.shape
    head = features // HEADS
    width = HEADS * LANE
    ends = bounds_of(lens_ref, core)
    x_turned = jnp.where(core == 0, own_ref[0, :, 0, :], recv_ref[0, :, 1, :])
    xt_out[...] = x_turned
    x_rows = x_turned.astype(F32).T
    x = low(x_rows)
    vectors = vectors_ref[...]
    q = dot(x, w_ref[:, 0:width]) + vectors[0:1]
    qu_out[...] = low(q + vectors[3:4])
    qw_out[...] = low(q + vectors[4:5])
    k_out[...] = low(dot(x, w_ref[:, width : 2 * width]))
    v_out[...] = low(dot(x, w_ref[:, 2 * width :]) + vectors[1:2])
    same = segment_of(iota((frames, 1), 0), ends) == segment_of(iota((1, frames), 1), ends)
    scale = head**-0.5
    for h in range(HEADS):
        cols = slice(h * LANE, (h + 1) * LANE)
        content = dot_cols(qu_out[:, cols], k_out[:, cols])
        relative = dot_cols(qw_out[:, cols], p_ref[:, cols])
        shifted = pltpu.roll(relative, 0, 1, stride=1, stride_axis=0)[:, frames:]
        scores = jnp.where(same, (content + shifted) * scale, MASKED)
        raised = jnp.exp(scores - jnp.max(scores, axis=-1, keepdims=True))
        weights = low(raised * (1.0 / jnp.sum(raised, axis=-1, keepdims=True)))
        a_out[h] = weights
        o_out[:, cols] = low(dot(weights, v_out[:, cols]))
    attended = dot(o_out[...], wo_ref[...]) + vec_ref[2:3, :]
    normed, inverse = normalise(x_rows + attended)
    n1_out[...] = normed
    inv1_out[...] = inverse


def half_masks(half, ends):
    position = 2 * iota((half, 1), 0)
    segment = segment_of(position, ends)
    before = segment_of(position - 1, ends)
    joined = jnp.where((segment == before) & (position > 0), 1.0, 0.0)
    valid = jnp.where(position < ends[-1], 1.0, 0.0)
    return joined, valid


def tap_ranges(half, ends, reach):
    position = iota((half, LANE), 0)
    first = jnp.zeros((half, LANE), jnp.int32)
    last = jnp.full((half, LANE), half, jnp.int32)
    for end in ends:
        edge = end // 2
        first = jnp.where(position >= edge, edge, first)
    for end in reversed(ends):
        edge = end // 2
        last = jnp.where(position < edge, edge, last)
    return first - position + reach, last - position + reach


def shift_tiles(ref, shifted):
    rows = shifted.shape[2]
    for by in range(shifted.shape[0]):
        for t in range(ref.shape[0]):
            shifted[by, t, :, :] = ref[t, by : by + rows, :]


def tap_rows_at(shifted, t, at):
    by = at % shifted.shape[0]
    return shifted[by, t, at - by : at - by + BLOCK, :]


def put_tiles(ref, at, values):
    rows, cols = values.shape
    for t in range(ref.shape[0]):
        stop = min(cols, (t + 1) * LANE)
        ref[t, at : at + rows, 0 : stop - t * LANE] = values[:, t * LANE : stop]


def get_tiles(ref, cols):
    return jnp.concatenate([ref[t] for t in range(ref.shape[0])], axis=1)[:, 0:cols]


def layer_vectors(own_ref, recv_ref, use_own, features):
    rows = jnp.where(use_own, own_ref[...], recv_ref[...])
    return rows[0:1], rows[1:3, 0:features], rows[3:6, 0:features]


def feed_forward(inputs, bias, w_in, w_out, shift, hid_ref, slope_ref):
    z = dot(low(inputs), w_in) + bias
    logistic = jax.nn.sigmoid(z)
    hid_ref[...] = low(z * logistic)
    slope_ref[...] = low(logistic * (1.0 + z * (1.0 - logistic)))
    return dot_cols(hid_ref[...], w_out) + shift


def convolution_forward(
    lens_ref,
    n1_ref,
    small_own,
    small_recv,
    win_own,
    win_recv,
    wout_own,
    wout_recv,
    vec_ref,
    taps_ref,
    proj_ref,
    glu_ref,
    conv_ref,
    vec2_ref,
    hid_out,
    slope_out,
    n2_out,
    inv2_out,
    ml_out,
    red_out,
    lin_out,
    sg_out,
    u_out,
    c_out,
    stat_out,
    win,
    wout,
    t_sc,
    u_sc,
    k_sc,
    c_sc,
    s_sc,
):
    core = lax.axis_index("section")
    first = core == 0
    frames, features = n1_ref.shape
    half = frames // 2
    choose(first, win_own, win_recv, win)
    choose(first, wout_own, wout_recv, wout)
    ends = bounds_of(lens_ref, core)
    bias, gains, shifts = layer_vectors(small_own, small_recv, first, features)
    h1 = n1_ref[...] * gains[0:1] + shifts[0:1]
    fed = feed_forward(h1, bias, win[...], wout[...], shifts[2:3], hid_out, slope_out)
    n2, inv2 = normalise(h1 + fed)
    n2_out[...] = n2
    inv2_out[...] = inv2
    inside = jnp.where(iota((frames, 1), 0) < ends[-1], 1.0, 0.0)
    put_tiles(t_sc, 0, (n2 * gains[1:2] + shifts[1:2]) * inside)
    joined, valid = half_masks(half, ends)
    even, odd = even_odd(t_sc, half, features)
    before = pltpu.roll(odd, 1, 0) * joined
    mixed = low(taps_ref[0:1] * before + taps_ref[1:2] * even + taps_ref[2:3] * odd)
    ml_out[...] = mixed
    reduced = low(dot(mixed, proj_ref[...]) + vec_ref[5:6])
    red_out[...] = reduced
    gates = dot_cols(reduced, glu_ref[...])
    linear = gates[:, 0:features] + vec2_ref[0:1]
    logistic = jax.nn.sigmoid(gates[:, features:] + vec2_ref[1:2])
    gated = linear * logistic
    lin_out[...] = linear
    sg_out[...] = logistic
    u_out[...] = gated
    tap_count = conv_ref.shape[0]
    reach = tap_count // 2
    lowest, highest = tap_ranges(half, ends, reach)
    u_sc[...] = jnp.zeros(u_sc.shape, F32)
    k_sc[...] = jnp.zeros(k_sc.shape, F32)
    put_tiles(u_sc, SUB, gated)
    shift_tiles(u_sc, s_sc)
    put_tiles(k_sc, 0, conv_ref[...])
    for begin in range(0, half, BLOCK):
        first, last = lowest[begin : begin + BLOCK], highest[begin : begin + BLOCK]
        totals = [jnp.zeros((BLOCK, LANE), F32)] * u_sc.shape[0]
        for o in range(tap_count):
            fits = (first <= o) & (o < last)
            at = SUB - reach + o + begin
            for t in range(u_sc.shape[0]):
                moved = jnp.where(fits, tap_rows_at(s_sc, t, at), 0.0)
                totals[t] = totals[t] + moved * k_sc[t, o : o + 1, :]
        for t, total in enumerate(totals):
            c_sc[t, begin : begin + BLOCK, :] = total
    convolved = get_tiles(c_sc, features)
    c_out[...] = convolved
    held = convolved * valid
    send_rows(
        stat_out, [row_sum(held), row_sum(held * convolved)], jnp.sum(valid, axis=0, keepdims=True)
    )


def even_odd(ref, half, features):
    even = [ref[t, pl.ds(0, half, stride=2), :] for t in range(ref.shape[0])]
    odd = [ref[t, pl.ds(1, half, stride=2), :] for t in range(ref.shape[0])]
    return (
        jnp.concatenate(even, axis=1)[:, 0:features],
        jnp.concatenate(odd, axis=1)[:, 0:features],
    )


def put_even_odd(ref, even, odd):
    half, features = even.shape
    for t in range(ref.shape[0]):
        stop = min(features, (t + 1) * LANE)
        span = slice(0, stop - t * LANE)
        ref[t, pl.ds(0, half, stride=2), span] = even[:, t * LANE : stop]
        ref[t, pl.ds(1, half, stride=2), span] = odd[:, t * LANE : stop]


def send_rows(out_ref, rows, count=None):
    out_ref[...] = jnp.zeros(out_ref.shape, F32)
    at = 0
    for row in rows:
        for begin in range(0, row.shape[1], LANE):
            stop = min(begin + LANE, row.shape[1])
            out_ref[at : at + 1, 0 : stop - begin] = row[:, begin:stop]
            at += 1
    if count is not None:
        out_ref[at : at + 1, :] = jnp.broadcast_to(count, (1, LANE))


def gather_rows(refs, features):
    total = functools.reduce(jnp.add, [ref[...] for ref in refs])
    tiles = up(features, LANE) // LANE
    rows = []
    for at in range(2):
        pieces = [total[at * tiles + t : at * tiles + t + 1, :] for t in range(tiles)]
        rows.append(jnp.concatenate(pieces, axis=1)[:, 0:features])
    return rows[0], rows[1], total[2 * tiles : 2 * tiles + 1, 0:1]


def batch_moments(stat_refs, features):
    first, second, count = gather_rows(stat_refs, features)
    centre = first / count
    return count, centre, lax.rsqrt(second / count - centre * centre + EPSILON)


def feed_back(grad, hid_slope, w_in, w_out):
    grad_low = low(grad)
    inner = low(dot(grad_low, w_out) * hid_slope.astype(F32))
    return grad_low, inner, dot_cols(inner, w_in)


def second_layer(
    parts,
    lens_ref,
    *refs,
):
    second_layer_body(lens_ref, refs[0:parts], *refs[parts:])


def second_layer_body(
    lens_ref,
    stat_refs,
    c_ref,
    red_ref,
    small_own,
    small_recv,
    win_own,
    win_recv,
    wout_own,
    wout_recv,
    point_ref,
    vec2_ref,
    gain_ref,
    own_ref,
    recv_ref,
    g_out,
    dch_out,
    ch_out,
    dr3_out,
    sums_out,
    t2_out,
    h3_out,
    grad_out,
    inner_out,
    hid_out,
    active_out,
    vec_out,
    win,
    wout,
    t_sc,
    slope_sc,
):
    core = lax.axis_index("section")
    first = core == 0
    frames, features = g_out.shape
    half = frames // 2
    choose(first, win_recv, win_own, win)
    choose(first, wout_recv, wout_own, wout)
    ends = bounds_of(lens_ref, core)
    inside = jnp.where(iota((frames, 1), 0) < ends[-1], 1.0, 0.0)
    bias, gains, shifts = layer_vectors(small_own, small_recv, jnp.logical_not(first), features)
    count, centre, rho = batch_moments(stat_refs, features)
    ch = (c_ref[...] - centre) * rho
    bnv = ch * gain_ref[...] + vec2_ref[3:4]
    logistic = jax.nn.sigmoid(bnv)
    active = low(bnv * logistic)
    active_slope = logistic * (1.0 + bnv * (1.0 - logistic))
    branch = dot(active, point_ref[...]) + vec2_ref[2:3]
    n3, inv3 = normalise(red_ref[...].astype(F32) + branch)
    h3 = n3 * gains[0:1] + shifts[0:1]
    fed = feed_forward(h3, bias, win[...], wout[...], shifts[2:3], hid_out, slope_sc)
    n4, inv4 = normalise(h3 + fed)
    t2 = n4 * gains[1:2] + shifts[1:2]
    t2_out[...] = n4 * gains[1:2] + shifts[1:2]
    grad = jnp.where(first, recv_ref[0, :, 0, :], own_ref[0, :, 1, :]).astype(F32).T * inside
    g_out[...] = low(grad)
    put_tiles(t_sc, 0, grad)
    even, odd = even_odd(t_sc, half, features)
    dt2 = even + odd
    dv4 = normalise_back(dt2, n4, inv4, gains[1:2])
    grad_low, inner, back = feed_back(dv4, slope_sc[...], win[...], wout[...])
    dh3 = dv4 + back
    dr3 = normalise_back(dh3, n3, inv3, gains[0:1])
    dr3_out[...] = dr3
    dpw = low(dr3)
    dbn = dot_cols(dpw, point_ref[...]) * active_slope
    dch = dbn * gain_ref[...]
    dch_out[...] = dch
    ch_out[...] = ch
    send_rows(sums_out, [row_sum(dch), row_sum(dch * ch)])
    h3_out[...] = low(h3)
    grad_out[...] = grad_low
    inner_out[...] = inner
    active_out[...] = active
    sums = (dh3 * n3, dt2 * n4, dh3, dt2, grad_low, dpw, dbn, dbn * ch)
    vec_out[...] = jnp.zeros(vec_out.shape, F32)
    for at, values in enumerate(sums):
        vec_out[at : at + 1, :] = row_sum(values)


def second_weights(
    h3_ref,
    grad_ref,
    inner_ref,
    hid_ref,
    active_ref,
    dr3_ref,
    vec_ref,
    after_ref,
    keep_out,
    send_out,
    stage,
    rest,
    vec_sc,
):
    core = lax.axis_index("section")
    inner = inner_ref[...]
    pack = Pack(stage, rest, vec_sc)
    vec_sc[...] = jnp.zeros(vec_sc.shape, F32)
    pack.matrix(dot_rows(h3_ref[...], inner))
    pack.matrix(dot_rows(grad_ref[...], hid_ref[...]))
    pack.matrix(dot_rows(active_ref[...], low(dr3_ref[...])))
    pack.bias = row_sum(inner)
    pack.vector(1, vec_ref[...])
    pack.finish(core, keep_out, send_out)


def output_rows(
    lens_ref,
    t2_ref,
    n2_ref,
    small_own,
    small_recv,
    dlin_ref,
    dgat_ref,
    dred_ref,
    red_ref,
    ml_ref,
    after_ref,
    y_out,
    mats_out,
    y_sc,
):
    core = lax.axis_index("section")
    frames, features = n2_ref.shape
    at = 5 * features % LANE
    reduced = red_ref[...]
    for left, right in (
        (dlin_ref[...], reduced),
        (dgat_ref[...], reduced),
        (ml_ref[...], dred_ref[...]),
    ):
        mats_out[:, at : at + features] = dot_rows(left, right)
        at += features
    ends = bounds_of(lens_ref, core)
    inside = jnp.where(iota((frames, 1), 0) < ends[-1], 1.0, 0.0)
    _, gains, shifts = layer_vectors(small_own, small_recv, core == 0, features)
    skip = low((n2_ref[...] * gains[1:2] + shifts[1:2]) * inside).astype(F32)
    put_even_odd(y_sc, t2_ref[...], t2_ref[...])
    y_out[...] = (get_tiles(y_sc, features) + skip) * inside


def convolution_back(
    parts,
    after,
    lens_ref,
    *refs,
):
    convolution_back_body(
        lens_ref, refs[0:parts], refs[parts : 2 * parts], *refs[2 * parts + after :]
    )


def convolution_back_body(
    lens_ref,
    stat_refs,
    sums_refs,
    dch_ref,
    ch_ref,
    dr3_ref,
    u_ref,
    lin_ref,
    sg_ref,
    n2_ref,
    small_own,
    small_recv,
    taps_ref,
    proj_ref,
    glu_ref,
    conv_ref,
    g_ref,
    dt_out,
    dlin_out,
    dgat_out,
    dred_out,
    vec_out,
    kd_out,
    t_sc,
    u_sc,
    d_sc,
    k_sc,
    c_sc,
    gate_sc,
    s_sc,
    m_sc,
):
    first = lax.axis_index("section") == 0
    frames, features = n2_ref.shape
    half = frames // 2
    ends = bounds_of(lens_ref, lax.axis_index("section"))
    inside = jnp.where(iota((frames, 1), 0) < ends[-1], 1.0, 0.0)
    joined, valid = half_masks(half, ends)
    bias, gains, shifts = layer_vectors(small_own, small_recv, first, features)
    count, centre, rho = batch_moments(stat_refs, features)
    sum1, sum2, _ = gather_rows(sums_refs, features)
    dc = (rho * valid) * (dch_ref[...] - sum1 / count - ch_ref[...] * (sum2 / count))
    tap_count = conv_ref.shape[0]
    reach = tap_count // 2
    lowest, highest = tap_ranges(half, ends, reach)
    u_sc[...] = jnp.zeros(u_sc.shape, F32)
    d_sc[...] = jnp.zeros(d_sc.shape, F32)
    k_sc[...] = jnp.zeros(k_sc.shape, F32)
    kd_out[...] = jnp.zeros(kd_out.shape, F32)
    vec_out[...] = jnp.zeros(vec_out.shape, F32)
    put_tiles(u_sc, 0, u_ref[...])
    put_tiles(d_sc, SUB, dc)
    shift_tiles(d_sc, s_sc)
    put_tiles(k_sc, 0, conv_ref[...])
    for begin in range(0, half, BLOCK):
        lead, stop = lowest[begin : begin + BLOCK], highest[begin : begin + BLOCK]
        totals = [jnp.zeros((BLOCK, LANE), F32)] * u_sc.shape[0]
        for o in range(tap_count):
            fits = (lead <= o) & (o < stop)
            at = SUB - reach + o + begin
            tap = slice(tap_count - 1 - o, tap_count - o)
            for t in range(u_sc.shape[0]):
                moved = jnp.where(fits, tap_rows_at(s_sc, t, at), 0.0)
                totals[t] = totals[t] + moved * k_sc[t, tap, :]
                met = moved * u_sc[t, begin : begin + BLOCK, :]
                met = functools.reduce(jnp.add, [met[r : r + 8] for r in range(0, BLOCK, 8)])
                if begin:
                    met = met + m_sc[t, tap.start]
                m_sc[t, tap.start] = met
        for t, total in enumerate(totals):
            c_sc[t, begin : begin + BLOCK, :] = total
    for t in range(kd_out.shape[0]):
        for o in range(tap_count):
            kd_out[t, o : o + 1, :] = row_sum(m_sc[t, o])
    du = get_tiles(c_sc, features)
    logistic = sg_ref[...]
    dlin = low(du * logistic)
    dgat = low(du * lin_ref[...] * logistic * (1.0 - logistic))
    gate_sc[:, 0:features] = dlin.astype(F32)
    gate_sc[:, features:] = dgat.astype(F32)
    dred = low(dot(low(gate_sc[...]), glu_ref[...]) + dr3_ref[...])
    dlin_out[...] = dlin
    dgat_out[...] = dgat
    dred_out[...] = dred
    for row, values in ((9, dlin), (10, dgat), (5, dred)):
        vec_out[row : row + 1, 0:features] = row_sum(values)
    dm = dot_cols(dred, proj_ref[...])
    n2 = n2_ref[...]
    put_tiles(t_sc, 0, (n2 * gains[1:2] + shifts[1:2]) * inside)
    even, odd = even_odd(t_sc, half, features)
    vec_out[6:7, 0:features] = row_sum(pltpu.roll(odd, 1, 0) * joined * dm)
    vec_out[7:8, 0:features] = row_sum(even * dm)
    vec_out[8:9, 0:features] = row_sum(odd * dm)
    carried = pltpu.roll(taps_ref[0:1] * joined * dm, half - 1, 0)
    put_even_odd(t_sc, taps_ref[1:2] * dm, taps_ref[2:3] * dm + carried)
    dt_out[...] = (g_ref[...].astype(F32) + get_tiles(t_sc, features)) * inside

def first_layer_back(
    dt_ref,
    n2_ref,
    inv2_ref,
    n1_ref,
    inv1_ref,
    hid_ref,
    slope_ref,
    small_own,
    small_recv,
    win_own,
    win_recv,
    wout_own,
    wout_recv,
    after_ref,
    dr1_out,
    keep_out,
    send_out,
    win,
    wout,
    stage,
    rest,
    vec_sc,
):
    core = lax.axis_index("section")
    first = core == 0
    choose(first, win_own, win_recv, win)
    choose(first, wout_own, wout_recv, wout)
    bias, gains, shifts = layer_vectors(small_own, small_recv, first, win.shape[0])
    pack = Pack(stage, rest, vec_sc)
    vec_sc[...] = jnp.zeros(vec_sc.shape, F32)
    dt = dt_ref[...]
    n2 = n2_ref[...]
    dv2 = normalise_back(dt, n2, inv2_ref[...], gains[1:2])
    pack.vector(2, row_sum(dt * n2))
    pack.vector(4, row_sum(dt))
    n1 = n1_ref[...]
    h1 = low(n1 * gains[0:1] + shifts[0:1])
    grad_low, inner, back = feed_back(dv2, slope_ref[...], win[...], wout[...])
    dh1 = dv2 + back
    pack.matrix(dot_rows(h1, inner))
    pack.matrix(dot_rows(grad_low, hid_ref[...]))
    pack.bias = row_sum(inner)
    pack.vector(5, row_sum(grad_low))
    pack.vector(1, row_sum(dh1 * n1))
    pack.vector(3, row_sum(dh1))
    dr1_out[...] = normalise_back(dh1, n1, inv1_ref[...], gains[0:1])
    pack.finish(core, keep_out, send_out)


def attention_back(
    heads,
    dr1_ref,
    qu_ref,
    qw_ref,
    k_ref,
    v_ref,
    p_ref,
    a_ref,
    wo_ref,
    *refs,
):
    dqr_out, dkv_out, dp_out, sums_out = refs[-4:]
    frames = dr1_ref.shape[0]
    head = dr1_ref.shape[1] // HEADS
    width = len(heads) * LANE
    scale = head**-0.5
    dr1_low = low(dr1_ref[...])
    flip = flip_rows(frames)
    for at, h in enumerate(heads):
        cols = slice(h * LANE, (h + 1) * LANE)
        here = slice(at * LANE, (at + 1) * LANE)
        weights = a_ref[h]
        grad = low(dot_cols(dr1_low, wo_ref[cols, :]))
        weights_f = weights.astype(F32)
        product = weights_f * dot_cols(grad, v_ref[:, cols])
        ds = low(product - weights_f * jnp.sum(product, axis=-1, keepdims=True))
        dkv_out[:, width + at * LANE : width + (at + 1) * LANE] = low(dot_rows(weights, grad))
        dkv_out[:, here] = low(scale * dot_rows(ds, qu_ref[:, cols]))
        dsr = low(dot(flip, ds))
        qwr = low(dot(flip, qw_ref[:, cols]))
        wide = jnp.concatenate([jnp.zeros((frames, frames), BF16), dsr], axis=1)
        band = pltpu.roll(wide, frames + 1, 1, stride=1, stride_axis=0)
        dqu = scale * dot(dsr, k_ref[:, cols])
        dqw = scale * dot(band, p_ref[:, cols])
        dqr_out[:, here] = low(dqu + dqw)
        dp_out[:, here] = low(scale * dot_rows(band, qwr))
        sums_out[0:1, here] = row_sum(dqu + dqw)
        sums_out[1:2, here] = row_sum(dkv_out[:, width + at * LANE : width + (at + 1) * LANE])
        sums_out[2:3, here] = row_sum(dqu)
        sums_out[3:4, here] = row_sum(dqw)


def flip_rows(frames):
    hit = iota((frames, frames), 0) + iota((frames, frames), 1) == frames - 1
    return jnp.where(hit, 1.0, 0.0).astype(BF16)


def attention_weights_back(
    dr1_ref,
    xt_ref,
    o_ref,
    table_ref,
    mats_ref,
    vec_ref,
    kd_ref,
    *refs,
):
    parts, after_ref = (refs[0:4], refs[4:8]), refs[8]
    dq_out, dkv_out, keep_out, send_out, stage, rest, vec_sc = refs[9:]
    core = lax.axis_index("section")
    frames, features = dr1_ref.shape
    width = HEADS * LANE
    pack = Pack(stage, rest, vec_sc)
    vec_sc[...] = vec_ref[...]
    begin = 5 * features // LANE * LANE
    stage[:, begin : begin + mats_ref.shape[1]] = mats_ref[...]
    dr1_low = low(dr1_ref[...])
    unselect = head_unselect(features, features // HEADS)
    pack.vector(2, row_sum(dr1_low))
    pack.matrix(dot_rows(unselect, low(dot_rows(o_ref[...], dr1_low))))
    half = width // 2
    flip = flip_rows(frames)
    for at, (dqr, dkv, dp, sums) in enumerate(parts):
        here = slice(at * half, (at + 1) * half)
        dq_out[:, here] = low(dot(flip, dqr[...]))
        dkv_out[:, here] = dkv[:, 0:half]
        dkv_out[:, width + at * half : width + (at + 1) * half] = dkv[:, half:]
    sums = jnp.concatenate([sums[0:4, :] for _, _, _, sums in parts], axis=1)
    sums = dot(sums, unselect.astype(F32), precision=lax.Precision.HIGHEST)
    pack.vector(0, sums[0:2])
    pack.vector(3, sums[2:4])
    x_turned = xt_ref[...]
    pack.matrix(dot(low(dot(x_turned, dq_out[...])), unselect))
    pack.matrix(dot(low(dot(x_turned, dkv_out[:, 0:width])), unselect))
    pack.matrix(dot(low(dot(x_turned, dkv_out[:, width:])), unselect))
    dp = jnp.concatenate([dp[...] for _, _, dp, _ in parts], axis=1)
    pack.matrix(dot(low(dot_rows(table_ref[...], dp)), unselect))
    pack.used = 8 * features
    pack.finish(core, keep_out, send_out, [kd_ref[t] for t in range(kd_ref.shape[0])])


def input_back(dr1_ref, dq_ref, dkv_ref, w_ref, y_ref, after_ref, rows_out, cross_out):
    core = lax.axis_index("section")
    width = dq_ref.shape[1]
    dx = dr1_ref[...] + dot_cols(dq_ref[...], w_ref[:, 0:width])
    dx = (dx + dot_cols(dkv_ref[...], w_ref[:, width:])).T
    y = y_ref[...].T
    rows_out[...] = jnp.where(core == 0, dx, y)
    cross_out[...] = jnp.where(core == 0, y, dx)


def place_of(bit, core):
    return 1 - bit if bit < 2 and core == 1 else bit


def digits(bits, core):
    row = lax.axis_index("rows")
    digit = jnp.int32(0)
    for bit in bits:
        place = jnp.where(core == 0, place_of(bit, 0), place_of(bit, 1))
        digit = (digit << 1) | ((row >> place) & 1)
    return digit


def partner(values, bits, m):
    peers = lax.axis_size("rows")
    pairs = []
    for core in range(2):
        flips = [1 << place_of(b, core) for at, b in enumerate(reversed(bits)) if m >> at & 1]
        pairs += [(core * peers + r, core * peers + (r ^ sum(flips))) for r in range(peers)]
    return lax.ppermute(values, ("section", "rows"), pairs)


def step_kernel(bits, join, count, *refs):
    parts = refs[:count]
    if bits:
        outs = refs[-(1 << len(bits)) :]
        rows = outs[0].shape[0]
        mine = digits(bits, lax.axis_index("section"))
        for m, out in enumerate(outs):
            span = pl.ds(pl.multiple_of((mine ^ m) * rows, SUB), rows)
            out[...] = low(sum(part[span, :].astype(F32) for part in parts))
    elif join:
        rows = parts[0].shape[0]
        for at, part in enumerate(parts):
            refs[-1][at * rows : (at + 1) * rows, :] = part[...]
    else:
        refs[-1][...] = low(sum(part[...].astype(F32) for part in parts))


def step(parts, after, name, bits=(), join=False):
    rows = parts[0].shape[0]
    if bits:
        outs = [shape((rows >> len(bits), LANE), BF16)] * (1 << len(bits))
    else:
        outs = [shape((rows * (len(parts) if join else 1), LANE), BF16)]
    return call(
        functools.partial(step_kernel, bits, join, len(parts)),
        name,
        [VMEM] * len(parts) + [ANY] * len(after),
        outs,
        limit=STEP_LIMIT,
        cost=STEP_COST,
    )(*parts, *after)


class Chain:
    def __init__(self, name, keep, send, splits, whole, gathers):
        self.name = name
        self.parts = [keep, swap(send)]
        self.summing = True
        self.plan = [("split", bits) for bits in splits]
        self.plan += [("whole", bits) for bits in whole]
        self.plan += [("gather", bits) for bits in gathers] + [("last", ())]

    def advance(self, after=()):
        kind, bits = self.plan.pop(0)
        name = "_".join([self.name, kind, *map(str, bits)])
        if kind == "last":
            (send,) = step(self.parts[1:], after, name, join=True)
            self.pieces = [self.parts[0], send, self.early, swap(send)]
            return send
        if kind == "split":
            blocks = step(self.parts, after, name, bits=bits)
            self.parts = [blocks[0]] + [partner(b, bits, m + 1) for m, b in enumerate(blocks[1:])]
            return blocks[1]
        (block,) = step(self.parts, after, name, join=not self.summing)
        self.summing = kind == "whole"
        self.parts = [block] + [partner(block, bits, m) for m in range(1, 1 << len(bits))]
        if len(self.plan) == 1:
            self.early = swap(block)
        return block


def reorder(pieces, target, bits):
    core = lax.axis_index("section")
    half = target.shape[0] // 2
    block = half >> bits
    for side in range(2):
        owner = core if side == 0 else 1 - core
        mine = digits(range(bits), owner)
        at = 0
        for piece in pieces[2 * side : 2 * side + 2]:
            for first in range(0, piece.shape[0], block):
                begin = pl.multiple_of(owner * half + (mine ^ at) * block, SUB)
                target[pl.ds(begin, block), :] = piece[first : first + block, :]
                at += 1


def spread_tiles(pack, stage):
    rows, wide = stage.shape
    tall = rows // SUB * SUB
    tail = rows - tall
    tiles = wide // LANE
    at = tall * tiles
    rest = pack[at : at + up(tail * tiles, SUB), :].astype(F32)
    for t in range(tiles):
        cols = slice(t * LANE, (t + 1) * LANE)
        stage[0:tall, cols] = pack[t * tall : (t + 1) * tall, :].astype(F32)
        stage[tall:rows, cols] = rest[t * tail : (t + 1) * tail]
    return at + rest.shape[0]


def vectors_at(ref, row, features, rows=SUB):
    tiles = up(features, LANE) // LANE
    pieces = [ref[row + t * rows : row + (t + 1) * rows, :] for t in range(tiles)]
    return jnp.concatenate(pieces, axis=1).astype(F32)[:, 0:features], row + tiles * rows


def bias_at(ref, row, cols):
    lines = ref[row : row + SUB, :].astype(F32)
    pieces = [lines[t : t + 1] for t in range(up(cols, LANE) // LANE)]
    return jnp.concatenate(pieces, axis=1)[:, 0:cols]


def unpack_one(
    bits,
    piece0,
    piece1,
    piece2,
    piece3,
    after_ref,
    point_out,
    gain_out,
    win_out,
    wout_out,
    bias_out,
    vec_out,
    pack,
    stage,
):
    reorder((piece0, piece1, piece2, piece3), pack, bits)
    at = spread_tiles(pack, stage)
    features = point_out.shape[0]
    inner = win_out.shape[2]
    win_out[:, 0, :] = stage[:, 0:inner]
    wout_out[:, 0, :] = stage[:, inner : 2 * inner]
    point_out[...] = stage[:, 2 * inner : 2 * inner + features]
    rows, at = vectors_at(pack, at, features)
    vec_out[...] = rows
    gain_out[...] = rows[8:9]
    bias_out[...] = bias_at(pack, at, inner)


def unpack_two(
    bits,
    win_ref,
    wout_ref,
    bias_ref,
    vec_ref,
    piece0,
    piece1,
    piece2,
    piece3,
    after_ref,
    norm_out,
    win_out,
    bias_out,
    wout_out,
    block_out,
    pack,
    stage,
):
    core = lax.axis_index("section")
    reorder((piece0, piece1, piece2, piece3), pack, bits)
    at = spread_tiles(pack, stage)
    features = win_out.shape[0]
    inner = win_out.shape[2]

    @pl.when(core == 0)
    def _():
        win_out[:, 0, :] = stage[:, 0:inner]
        wout_out[:, 0, :] = stage[:, inner : 2 * inner]

    @pl.when(core != 0)
    def _():
        win_out[...] = win_ref[...]
        wout_out[...] = wout_ref[...]

    rows, at = vectors_at(pack, at, features)
    bias_out[...] = jnp.where(core == 0, bias_at(pack, at, inner), bias_ref[...])
    mine = jnp.where(core == 0, rows, vec_ref[...])
    norm_out[0] = mine[1:3]
    for row in range(3):
        block_out[row] = mine[3 + row : 4 + row]


def unpack_three(
    bits,
    vec_ref,
    piece0,
    piece1,
    piece2,
    piece3,
    after_ref,
    attn_in_out,
    pos_out,
    attn_out_out,
    glu_out,
    proj_out,
    conv_out,
    vec_out,
    taps_out,
    vec2_out,
    pack,
    stage,
):
    reorder((piece0, piece1, piece2, piece3), pack, bits)
    at = spread_tiles(pack, stage)
    features = pos_out.shape[0]
    attn_out_out[...] = stage[:, 0:features]
    attn_in_out[...] = stage[:, features : 4 * features]
    pos_out[...] = stage[:, 4 * features : 5 * features]
    glu_out[0:features, :] = stage[:, 5 * features : 6 * features]
    glu_out[features:, :] = stage[:, 6 * features : 7 * features]
    proj_out[...] = stage[:, 7 * features : 8 * features]
    taps = conv_out.shape[0]
    rows, at = vectors_at(pack, at, features, up(taps, SUB))
    conv_out[...] = rows[0:taps]
    rows, at = vectors_at(pack, at, features)
    vec_out[...] = rows[0:6]
    taps_out[...] = rows[6:9]
    vec2_out[0:2, :] = rows[9:11]
    vec2_out[2:4, :] = vec_ref[6:8, :]


def join_rows(rows_ref, cross_ref, after_ref, boundary_out, mark_out):
    mark_out[...] = jnp.zeros(mark_out.shape, F32)
    core = lax.axis_index("section")
    rows, cross = rows_ref[...], cross_ref[...]
    boundary_out[0, :, 0, :] = jnp.where(core == 0, rows, cross)
    boundary_out[0, :, 1, :] = jnp.where(core == 0, cross, rows)


def shape(dims, dtype=F32):
    return jax.ShapeDtypeStruct(dims, dtype)


SMEM = pl.BlockSpec(memory_space=pltpu.SMEM)
VMEM = pl.BlockSpec(memory_space=pltpu.VMEM)
ANY = pl.BlockSpec(memory_space=pl.ANY)
HBM = pl.BlockSpec(memory_space=pltpu.HBM)


def call(kernel, name, in_specs, out_shape, scratch=(), limit=None, cost=None):
    cost = KERNEL_COST if cost is None else cost
    return pl.pallas_call(
        kernel,
        name=name,
        in_specs=in_specs,
        out_specs=[VMEM] * len(out_shape),
        out_shape=out_shape,
        scratch_shapes=list(scratch),
        compiler_params=pltpu.CompilerParams(vmem_limit_bytes=limit or VMEM_LIMIT),
        cost_estimate=pl.CostEstimate(flops=400 * cost, bytes_accessed=cost, transcendentals=0),
    )


def position_table(frames, features):
    distance = (frames - np.arange(2 * frames)).astype(np.float32)
    frequency = np.exp(
        np.arange(0, features, 2).astype(np.float32) * np.float32(-math.log(10000.0) / features)
    ).astype(np.float32)
    angles = (distance[:, None] * frequency[None, :]).astype(np.float64)
    table = np.stack([np.sin(angles), np.cos(angles)], axis=-1).reshape(2 * frames, features)
    return jnp.asarray(table.astype(np.float32), BF16)


def in_hbm(values):
    return pltpu.with_memory_space_constraint(values, pltpu.HBM)


def swap(values):
    return lax.ppermute(values, "section", [(0, 1), (1, 0)])


def share(values):
    bits = lax.axis_size("rows").bit_length() - 1
    parts = [values]
    for begin in range(0, bits, 2):
        values = functools.reduce(jnp.add, parts)
        parts = [values]
        count = min(2, bits - begin)
        for step in [m for m in ((2, 3, 1) if begin else (3, 2, 1)) if m < 1 << count]:
            pairs = [(r, r ^ (step << begin)) for r in range(1 << bits)]
            parts.append(lax.ppermute(values, "rows", pairs))
    return parts, values


def shards(
    boundary,
    utt_lengths,
    attn_in,
    pos_proj,
    attn_out,
    first_vectors,
    reduce_taps,
    reduce_proj,
    glu_in,
    conv_taps,
    second_vectors,
    bn_gain,
    point_proj,
    ffn_in,
    ffn_bias,
    ffn_out,
    norm_gain,
    block_vectors,
):
    peers = lax.axis_size("rows")
    _, batches, frames, features = boundary.shape
    half = frames // 2
    inner = ffn_in.shape[2]
    width = HEADS * LANE
    tiles = up(features, LANE) // LANE
    tap_rows = up(conv_taps.shape[0], SUB)
    cols = (2 * inner + features, 2 * inner, 8 * features)
    wide = [up(count, LANE) for count in cols]
    others = (0, 0, tap_rows * tiles)
    heights = [
        pack_heights(features, count, bias, other)
        for count, bias, other in zip(cols, (inner, inner, 0), others)
    ]
    pack_rows = [up(height[2], peers * SUB) for height in heights]
    row_bits = peers.bit_length() - 1
    singles = [(bit,) for bit in range(row_bits - 1)]
    pairs = [tuple(range(at, min(at + 2, row_bits))) for at in range(0, row_bits, 2)]
    by_one = (singles, [(row_bits - 1,)], singles[::-1])
    by_two = (pairs, [], pairs[::-1])
    table = position_table(frames, features)
    turned = jnp.transpose(boundary, (0, 3, 1, 2))
    wout_own = jnp.transpose(ffn_out, (0, 2, 1))
    shift_own = jnp.transpose(block_vectors, (1, 0, 2))
    glu_turned = glu_in.T

    recv = swap(turned)
    weights = (ffn_in, swap(ffn_in), wout_own, swap(wout_own))

    def scratch(*dims, dtype=F32):
        return pltpu.VMEM(dims, dtype)

    p, w_pad, wo_pad, vectors, small = call(
        prepare,
        "prepare",
        [HBM] * 8,
        [
            shape((2 * frames, width), BF16),
            shape((features, 3 * width), BF16),
            shape((width, features), BF16),
            shape((first_vectors.shape[0], width)),
            shape((8, inner)),
        ],
        [
            scratch(*attn_in.shape, dtype=BF16),
            scratch(*pos_proj.shape, dtype=BF16),
            scratch(*attn_out.shape, dtype=BF16),
            scratch(*first_vectors.shape),
            scratch(*table.shape, dtype=BF16),
            scratch(*ffn_bias.shape),
            scratch(*norm_gain.shape),
            scratch(*shift_own.shape),
            pltpu.SemaphoreType.DMA((8,)),
        ],
        cost=10**7,
    )(
        *map(in_hbm, (attn_in, pos_proj, attn_out, first_vectors, table)),
        *map(in_hbm, (ffn_bias, norm_gain, shift_own)),
    )
    small = (small, swap(small))
    xt, qu, qw, k, v, a, o, n1, inv1 = call(
        attention_forward,
        "attention_forward",
        [SMEM] + [VMEM] * 7,
        [
            shape((features, frames), BF16),
            shape((frames, width), BF16),
            shape((frames, width), BF16),
            shape((frames, width), BF16),
            shape((frames, width), BF16),
            shape((HEADS, frames, frames), BF16),
            shape((frames, width), BF16),
            shape((frames, features)),
            shape((frames, 1)),
        ],
    )(
        utt_lengths,
        turned,
        recv,
        p,
        w_pad,
        wo_pad,
        vectors,
        first_vectors,
    )

    weights_scratch = [scratch(features, inner, dtype=BF16)] * 2
    rows_scratch = scratch(tiles, frames, LANE)
    edge_scratch = scratch(tiles, half + 2 * SUB, LANE)
    taps_scratch = scratch(tiles, tap_rows, LANE)
    shift_scratch = scratch(8, tiles, half + 2 * SUB - 8, LANE)
    vec_scratch = scratch(SUB, tiles * LANE)

    def pack_scratch(index):
        return scratch(pack_rows[index], LANE, dtype=BF16)

    def stage_scratch(index):
        return scratch(features, wide[index])

    def pack_stages(index):
        return [stage_scratch(index), scratch(heights[index][1], LANE), vec_scratch]

    def pack_halves(index):
        return [shape((pack_rows[index] // 2, LANE), BF16)] * 2

    hid, slope, n2, inv2, ml, red, lin, sg, u, c, stat = call(
        convolution_forward,
        "convolution_forward",
        [SMEM] + [VMEM] * 13,
        [
            shape((frames, inner), BF16),
            shape((frames, inner), BF16),
            shape((frames, features)),
            shape((frames, 1)),
            shape((half, features), BF16),
            shape((half, features), BF16),
            shape((half, features)),
            shape((half, features)),
            shape((half, features)),
            shape((half, features)),
            shape((8, LANE)),
        ],
        weights_scratch + [rows_scratch, edge_scratch, taps_scratch, scratch(tiles, half, LANE), shift_scratch],
    )(
        utt_lengths,
        n1,
        *small,
        *weights,
        first_vectors,
        reduce_taps,
        reduce_proj,
        glu_turned,
        conv_taps,
        second_vectors,
    )
    stat, _ = share(stat)
    g, dch, ch, dr3, sums, t2, h3, grad4, inner4, hid4, active, vec1 = call(
        functools.partial(second_layer, len(stat)),
        "second_layer",
        [SMEM] + [VMEM] * (13 + len(stat)),
        [
            shape((frames, features), BF16),
            shape((half, features)),
            shape((half, features)),
            shape((half, features)),
            shape((8, LANE)),
            shape((half, features)),
            shape((half, features), BF16),
            shape((half, features), BF16),
            shape((half, inner), BF16),
            shape((half, inner), BF16),
            shape((half, features), BF16),
            shape((8, features)),
        ],
        weights_scratch + [rows_scratch, scratch(half, inner, dtype=BF16)],
    )(
        utt_lengths,
        *stat,
        c,
        red,
        *small,
        *weights,
        point_proj,
        second_vectors,
        bn_gain[None],
        turned,
        recv,
    )
    sums, sent = share(sums)
    chains = {}
    made = {}

    def weights_two(mark):
        keep, send = call(
            second_weights,
            "second_weights",
            [VMEM] * 7 + [ANY],
            pack_halves(0),
            pack_stages(0),
        )(h3, grad4, inner4, hid4, active, dr3, vec1, mark)
        chains["1"] = Chain("one", keep, send, *by_one)
        return keep

    def conv_back(mark):
        made["conv"] = call(
            functools.partial(convolution_back, len(stat), 1),
            "convolution_back",
            [SMEM] + [VMEM] * (2 * len(stat)) + [ANY] + [VMEM] * 14,
            [
                shape((frames, features)),
                shape((half, features), BF16),
                shape((half, features), BF16),
                shape((half, features), BF16),
                shape((SUB, tiles * LANE)),
                shape((tiles, tap_rows, LANE)),
            ],
            [
                rows_scratch,
                scratch(tiles, half, LANE),
                edge_scratch,
                taps_scratch,
                scratch(tiles, half, LANE),
                scratch(half, 2 * features),
                shift_scratch,
                scratch(tiles, tap_rows, 8, LANE),
            ],
        )(
            utt_lengths,
            *stat,
            *sums,
            mark,
            dch,
            ch,
            dr3,
            u,
            lin,
            sg,
            n2,
            *small,
            reduce_taps,
            reduce_proj,
            glu_turned,
            conv_taps,
            g,
        )
        return made["conv"][0]

    def rows_out(mark):
        made["y"], made["mats"] = call(
            output_rows,
            "output_rows",
            [SMEM] + [VMEM] * 9 + [ANY],
            [
                shape((frames, features)),
                shape((features, up(5 * features % LANE + 3 * features, LANE))),
            ],
            [rows_scratch],
        )(utt_lengths, t2, n2, *small, *made["conv"][1:4], red, ml, mark)
        return made["y"]

    def first_back(mark):
        dr1, keep, send = call(
            first_layer_back,
            "first_layer_back",
            [VMEM] * 13 + [ANY],
            [shape((frames, features))] + pack_halves(1),
            weights_scratch + pack_stages(1),
        )(made["conv"][0], n2, inv2, n1, inv1, hid, slope, *small, *weights, mark)
        made["dr1"] = dr1
        chains["2"] = Chain("two", keep, send, *by_one)
        return dr1

    def heads_back(heads, mark):
        wide_heads = len(heads) * LANE
        made[heads[0]] = call(
            functools.partial(attention_back, heads),
            "attention_back",
            [VMEM] * 8 + [ANY],
            [
                shape((frames, wide_heads), BF16),
                shape((frames, 2 * wide_heads), BF16),
                shape((2 * frames, wide_heads), BF16),
                shape((8, wide_heads)),
            ],
        )(made["dr1"], qu, qw, k, v, p, a, wo_pad, mark)
        return made[heads[0]][0]

    def weights_one(mark):
        parts = made[0] + made[HEADS // 2]
        made["dq"], made["dkv"], keep, send = call(
            attention_weights_back,
            "attention_weights_back",
            [VMEM] * 15 + [ANY],
            [shape((frames, width), BF16), shape((frames, 2 * width), BF16)] + pack_halves(2),
            pack_stages(2),
        )(made["dr1"], xt, o, table, made["mats"], *made["conv"][4:], *parts, mark)
        chains["3"] = Chain("three", keep, send, *by_one)
        return keep

    def rows_back(mark):
        made["rows"], cross = call(
            input_back,
            "input_back",
            [VMEM] * 5 + [ANY],
            [shape((features, frames))] * 2,
        )(made["dr1"], made["dq"], made["dkv"], w_pad, made["y"], mark)
        made["cross"] = swap(cross)
        return made["rows"]

    def rows_join(mark):
        made["boundary"], mark = call(
            join_rows,
            "join_rows",
            [VMEM] * 2 + [ANY],
            [shape((1, features, batches, frames)), shape((8, LANE))],
        )(made["rows"], made["cross"], mark)
        return mark

    def open_one(mark):
        made["point"], made["gain"], *made["one"] = call(
            functools.partial(unpack_one, row_bits - 1),
            "unpack_one",
            [VMEM] * 4 + [ANY],
            [
                shape(point_proj.shape),
                shape((1, features)),
                shape((features, 1, inner)),
                shape((features, 1, inner)),
                shape(ffn_bias.shape),
                shape((SUB, features)),
            ],
            [pack_scratch(0), stage_scratch(0)],
        )(*chains["1"].pieces, mark)
        return made["one"][3]

    def open_two(mark):
        made["two"] = call(
            functools.partial(unpack_two, row_bits - 1),
            "unpack_two",
            [VMEM] * 8 + [ANY],
            [
                shape(norm_gain.shape),
                shape((features, 1, inner)),
                shape(ffn_bias.shape),
                shape((features, 1, inner)),
                shape(shift_own.shape),
            ],
            [pack_scratch(1), stage_scratch(1)],
        )(*made["one"], *chains["2"].pieces, mark)
        return made["two"][0]

    def open_three(mark):
        made["three"] = call(
            functools.partial(unpack_three, row_bits - 1),
            "unpack_three",
            [VMEM] * 5 + [ANY],
            [
                shape(attn_in.shape),
                shape(pos_proj.shape),
                shape(attn_out.shape),
                shape(glu_turned.shape),
                shape(reduce_proj.shape),
                shape(conv_taps.shape),
                shape(first_vectors.shape),
                shape(reduce_taps.shape),
                shape(second_vectors.shape),
            ],
            [pack_scratch(2), stage_scratch(2)],
        )(made["one"][3], *chains["3"].pieces, mark)
        return made["three"][6]

    runs = dict(K=weights_two, E=conv_back, F=first_back, G=rows_out, C=weights_one, D=rows_back)
    runs.update(J=rows_join, U=open_one, V=open_two, W=open_three)
    runs["A"] = functools.partial(heads_back, range(HEADS // 2))
    runs["B"] = functools.partial(heads_back, range(HEADS // 2, HEADS))
    order = ORDER
    spare = len(singles) - 3
    for number in "123":
        at = order.index({"1": "K", "2": "F", "3": "D"}[number]) + 1
        at = order.index(number, at)
        order = order[:at] + number * (2 * spare) + order[at:]
    mark = sent
    for letter in order:
        mark = runs[letter](mark) if letter in runs else chains[letter].advance([mark])
    norm_out, win_out, bias_out, wout_out, block_out = made["two"]
    attn_in_out, pos_out, attn_out_out, glu_out, proj_out, conv_out = made["three"][0:6]
    vec_out, taps_out, vec2_out = made["three"][6:]
    return (
        jnp.transpose(made["boundary"], (0, 2, 3, 1)),
        attn_in_out,
        pos_out,
        attn_out_out,
        vec_out,
        taps_out,
        proj_out,
        glu_out.T,
        conv_out,
        vec2_out,
        made["gain"][0],
        made["point"],
        jnp.transpose(win_out, (1, 0, 2)),
        bias_out,
        jnp.transpose(wout_out, (1, 2, 0)),
        norm_out,
        jnp.transpose(block_out, (1, 0, 2)),
    )


def solution(mesh):
    split = (
        P("section", None, None),
        P("section", None),
        P("section", None, None),
        P("section", None, None),
        P("section", None, None),
    )
    return jax.shard_map(
        shards,
        mesh=mesh,
        in_specs=(P("section", None, "rows", None), P(None, "rows", None)) + (P(),) * 11 + split,
        out_specs=(P("section", None, "rows", None),) + (P(),) * 11 + split,
        check_vma=False,
    )
```
